32 devices in a mesh: pages: 16 (over z, y, x), slab: 2 (over core).
Axes of the slice: x: 2, y: 2, z: 4, core: 2. Of those that a mesh axis runs over, the one named last changes fastest.
Arguments:
- tokens: bfloat16 [32, 512, 768], P('pages', 'slab'), may hold values from -6 to 6
- boxes: int32 [32, 4, 512], P('pages'), may hold values from 0 to 1000, as said below
- lengths: int32 [32], P('pages'), may hold values from 40 to 512, as said below
- w_qkv: bfloat16 [768, 2304], replicated, may hold values from -0.21875 to 0.21875
- b_qkv: bfloat16 [2304], replicated, may hold values from -3 to 3
- w_posk: bfloat16 [256, 768], replicated, may hold values from -0.375 to 0.375
- w_posq: bfloat16 [256, 768], replicated, may hold values from -0.375 to 0.375
- w_out: bfloat16 [768, 768], replicated, may hold values from -0.75 to 0.75
- b_out: bfloat16 [768], replicated, may hold values from -2 to 2
- gain_one: bfloat16 [768], replicated, may hold values from 0.25 to 1.75
- shift_one: bfloat16 [768], replicated, may hold values from -2 to 2
- w_in: bfloat16 [768, 3072], replicated, may hold values from -0.21875 to 0.21875
- b_in: bfloat16 [3072], replicated, may hold values from -3 to 3
- w_down: bfloat16 [3072, 768], replicated, may hold values from -0.109375 to 0.109375
- b_down: bfloat16 [768], replicated, may hold values from -2 to 2
- gain_two: bfloat16 [768], replicated, may hold values from 0.25 to 1.75
- shift_two: bfloat16 [768], replicated, may hold values from -2 to 2
- cotangent: bfloat16 [32, 512, 768], P('pages', 'slab'), may hold values from -9 to 9
Outputs:
- output: bfloat16 [32, 512, 768], P('pages', 'slab')
- grad_tokens: bfloat16 [32, 512, 768], P('pages', 'slab')
- grad_w_qkv: float32 [768, 2304], P('pages')
- grad_b_qkv: float32 [2304], P('pages')
- grad_w_posk: float32 [256, 768], P('pages')
- grad_w_posq: float32 [256, 768], P('pages')
- grad_w_out: float32 [768, 768], P('pages')
- grad_b_out: float32 [768], P('pages')
- grad_gain_one: float32 [768], P('pages')
- grad_shift_one: float32 [768], P('pages')
- grad_w_in: float32 [768, 3072], P('pages')
- grad_b_in: float32 [3072], P('pages')
- grad_w_down: float32 [3072, 768], P('pages')
- grad_b_down: float32 [768], P('pages')
- grad_gain_two: float32 [768], P('pages')
- grad_shift_two: float32 [768], P('pages')
The draws below stay inside these ranges and needn't reach their ends.
Inputs may be any that keep to these rules, and one draw needn't show every extreme that they name: `boxes`: every box has left <= right and top <= bottom. `lengths`: of the 2 pages of each index of pages, one has 512 real tokens.
All inputs are finite; a program needn't handle non-finite values.
Results may differ from the reference program's by a relative error of at most 0.02.
Values may be sent and summed in bfloat16 or wider, within the bound.
No kernel may reach another device: no remote copies, remote signals or barrier semaphores. Data moves between devices by JAX's collectives and lax.ppermute only.
A program may use at most 192 MiB of HBM per device.

```python
import math
import jax
import jax.numpy as jnp
from jax import lax

D = 768
HEADS = 12
FF = 3072
HEAD = 64
POS = 256
PAGE = 512
LEN_MIN = 40
PAGES_DEV = 2
PAGES = 32


def draw_boxes(key, part):
    key = jax.random.fold_in(key, 11)
    keys = jax.random.split(key, 4)
    left = jax.random.randint(keys[0], (PAGES, PAGE), 0, 901)
    top = jax.random.randint(keys[1], (PAGES, PAGE), 0, 901)
    width_box = jax.random.randint(keys[2], (PAGES, PAGE), 1, 101)
    height_box = jax.random.randint(keys[3], (PAGES, PAGE), 1, 101)
    return jnp.stack([left, top, left + width_box, top + height_box], 1).astype(jnp.int32)


def draw_lengths(key, part):
    key = jax.random.fold_in(key, 12)
    first, second = jax.random.split(key)
    raw = jax.random.randint(first, (PAGES,), LEN_MIN, PAGE + 1)
    chosen = jax.random.randint(second, (PAGES // PAGES_DEV, 1), 0, PAGES_DEV)
    slots = jnp.arange(PAGES_DEV, dtype=jnp.int32)[None, :]
    full = (slots == chosen).reshape(PAGES)
    return jnp.where(full, PAGE, raw).astype(jnp.int32)


def draw_cotangent(key, part):
    key = jax.random.fold_in(key, 13)
    first = jax.random.fold_in(key, 0)
    ramp = jnp.arange(PAGES, dtype=jnp.float32) / max(PAGES - 1, 1)
    noise = jnp.clip(jax.random.normal(first, (PAGES, PAGE, D), jnp.float32), -6.0, 6.0)
    values = noise * (0.5 + ramp)[:, None, None]
    return values.astype(jnp.bfloat16)


def block_scale(rng, shape, cuts, least, high):
    level = 1.0
    for dim, blocks in cuts:
        draws = jax.random.uniform(jax.random.fold_in(jax.random.fold_in(rng, 6), dim), (blocks,), jnp.float32, least / len(cuts), high / len(cuts))
        level = level * jnp.repeat(jnp.exp(draws), shape[dim] // blocks).reshape((-1,) + (1,) * (len(shape) - 1 - dim))
    return level


def scatter_about(rng, shape, deviation, bound, cuts=(), held_as=jnp.bfloat16):
    level = block_scale(rng, shape, cuts, -0.22, 0.18) if cuts else 1.0
    result = jax.random.normal(rng, shape, jnp.float32) * deviation * level
    return jnp.minimum(jnp.maximum(result, -bound), bound).astype(held_as)


def setup_inputs(seed: int = 0) -> dict:
    splits = jax.random.split(jax.random.key(seed), 19)
    tokens = scatter_about(splits[0], (PAGES, PAGE, D), 1.0, 6.0, ((0, 16), (1, 2)))
    boxes = draw_boxes(jax.random.fold_in(splits[18], 71), 0)
    lengths = draw_lengths(jax.random.fold_in(splits[18], 71), 0)
    w_qkv = scatter_about(splits[3], (D, 3 * D), D ** -0.5, 0.21875)
    b_qkv = scatter_about(splits[4], (3 * D,), 0.5, 3.0)
    w_posk = scatter_about(splits[5], (POS, D), POS ** -0.5, 0.375)
    w_posq = scatter_about(splits[6], (POS, D), POS ** -0.5, 0.375)
    w_out = scatter_about(splits[7], (D, D), HEAD ** -0.5, 0.75)
    b_out = scatter_about(splits[8], (D,), 0.3, 2.0)
    gain_one = jnp.clip(1.0 + 0.15 * jax.random.normal(splits[9], (D,), jnp.float32), 0.25, 1.75).astype(jnp.bfloat16)
    shift_one = scatter_about(splits[10], (D,), 0.3, 2.0)
    w_in = scatter_about(splits[11], (D, FF), D ** -0.5, 0.21875)
    b_in = scatter_about(splits[12], (FF,), 0.5, 3.0)
    w_down = scatter_about(splits[13], (FF, D), FF ** -0.5, 0.109375)
    b_down = scatter_about(splits[14], (D,), 0.3, 2.0)
    gain_two = jnp.clip(1.0 + 0.15 * jax.random.normal(splits[15], (D,), jnp.float32), 0.25, 1.75).astype(jnp.bfloat16)
    shift_two = scatter_about(splits[16], (D,), 0.3, 2.0)
    cotangent = draw_cotangent(jax.random.fold_in(splits[18], 71), 0)
    return dict(tokens=tokens, boxes=boxes, lengths=lengths, w_qkv=w_qkv, b_qkv=b_qkv, w_posk=w_posk, w_posq=w_posq, w_out=w_out, b_out=b_out, gain_one=gain_one, shift_one=shift_one, w_in=w_in, b_in=b_in, w_down=w_down, b_down=b_down, gain_two=gain_two, shift_two=shift_two, cotangent=cotangent)


@jax.custom_vjp
def low(v):
    return lax.optimization_barrier(v.astype(jnp.bfloat16)).astype(jnp.float32)

@jax.custom_vjp
def low_back(v):
    return v

def low_keep(v):
    return (low(v), None)

def low_pass(kept, grad):
    return (grad,)

def back_keep(v):
    return (v, None)

def back_low(kept, grad):
    return (low(grad),)
low.defvjp(low_keep, low_pass)
low_back.defvjp(back_keep, back_low)
highest = lax.Precision.HIGHEST
epsilon = 1e-06
masked_score = -1000000000.0

def box_tables(boxes):
    quarter = POS // 4
    rates = jnp.exp(jnp.arange(quarter, dtype=jnp.float32) * (-math.log(10000.0) / quarter))
    centre_x = (boxes[:, 0, :] + boxes[:, 2, :]).astype(jnp.float32) * 0.5
    centre_y = (boxes[:, 1, :] + boxes[:, 3, :]).astype(jnp.float32) * 0.5
    angle_x = centre_x[:, :, None] * rates
    angle_y = centre_y[:, :, None] * rates
    return (jnp.sin(angle_x), jnp.cos(angle_x), jnp.sin(angle_y), jnp.cos(angle_y))

def layer_norm(values, gain, shift):
    mean = lax.optimization_barrier(jnp.mean(values, -1, keepdims=True))
    centred = values - mean
    variance = lax.optimization_barrier(jnp.mean(centred * centred, -1, keepdims=True))
    return centred * lax.rsqrt(variance + epsilon) * gain + shift

def quarters(values):
    quarter = values.shape[-1] // 4
    return (values[..., :quarter], values[..., quarter:2 * quarter], values[..., 2 * quarter:3 * quarter], values[..., 3 * quarter:])

def layer_forward(params, inputs, boxes, lengths):
    w_qkv, b_qkv, w_posk, w_posq, w_out, b_out, gain_one, shift_one, w_in, b_in, w_down, b_down, gain_two, shift_two = params
    group = inputs.shape[0]
    sine_x, cosine_x, sine_y, cosine_y = box_tables(boxes)
    key_factor = low(jnp.concatenate([cosine_x, sine_x, cosine_y, sine_y], -1))
    query_factor = low(jnp.concatenate([sine_x, cosine_x, sine_y, cosine_y], -1))
    proj = jnp.einsum('gtd,dc->gtc', inputs, w_qkv, precision=highest) + b_qkv
    proj = low_back(low(proj))
    query = proj[..., :D].reshape(group, PAGE, HEADS, HEAD)
    key = proj[..., D:2 * D].reshape(group, PAGE, HEADS, HEAD)
    value = proj[..., 2 * D:].reshape(group, PAGE, HEADS, HEAD)
    pos_k = w_posk.reshape(POS, HEADS, HEAD)
    pos_q = w_posq.reshape(POS, HEADS, HEAD)
    sx = sine_x[:, :, None, :]
    cx = cosine_x[:, :, None, :]
    sy = sine_y[:, :, None, :]
    cy = cosine_y[:, :, None, :]
    a_mix = low_back(jnp.einsum('gthe,khe->gthk', query, pos_k, precision=highest))
    axs, axc, ays, ayc = quarters(a_mix)
    u_feat = jnp.concatenate([axs * sx + axc * cx, axc * sx - axs * cx, ays * sy + ayc * cy, ayc * sy - ays * cy], -1)
    u_feat = low_back(low(u_feat))
    b_mix = jnp.einsum('gthe,khe->gthk', key, pos_q, precision=highest)
    bxs, bxc, bys, byc = quarters(b_mix)
    z_feat = jnp.concatenate([bxs * cx + bxc * sx, bxc * cx - bxs * sx, bys * cy + byc * sy, byc * cy - bys * sy], -1)
    z_feat = low(z_feat)
    text = jnp.einsum('gihe,gjhe->ghij', query, key, precision=highest)
    text_pos = jnp.einsum('gihk,gjk->ghij', u_feat, key_factor, precision=highest)
    pos_text = jnp.einsum('gik,gjhk->ghij', query_factor, z_feat, precision=highest)
    score = low_back((text + text_pos + pos_text) * HEAD ** (-0.5))
    valid = jnp.arange(PAGE, dtype=jnp.int32)[None, :] < lengths[:, None]
    score = jnp.where(valid[:, None, None, :], score, masked_score)
    probs = low(jax.nn.softmax(score, -1))
    attended = jnp.einsum('ghij,gjhe->gihe', probs, value, precision=highest).reshape(group, PAGE, D)
    attended = low_back(low(attended))
    branch = low_back(jnp.einsum('gtd,dc->gtc', attended, w_out, precision=highest) + b_out)
    first = layer_norm(inputs + branch, gain_one, shift_one)
    first_low = low_back(low(first))
    hidden = low_back(jnp.einsum('gtd,df->gtf', first_low, w_in, precision=highest) + b_in)
    active = low_back(low(jax.nn.gelu(hidden, approximate=False)))
    second = low_back(jnp.einsum('gtf,fd->gtd', active, w_down, precision=highest) + b_down)
    return layer_norm(first + second, gain_two, shift_two)

def reference(tokens, boxes, lengths, w_qkv, b_qkv, w_posk, w_posq, w_out, b_out, gain_one, shift_one, w_in, b_in, w_down, b_down, gain_two, shift_two, cotangent):
    params = (w_qkv.astype(jnp.float32), b_qkv.astype(jnp.float32), w_posk.astype(jnp.float32), w_posq.astype(jnp.float32), w_out.astype(jnp.float32), b_out.astype(jnp.float32), gain_one.astype(jnp.float32), shift_one.astype(jnp.float32), w_in.astype(jnp.float32), b_in.astype(jnp.float32), w_down.astype(jnp.float32), b_down.astype(jnp.float32), gain_two.astype(jnp.float32), shift_two.astype(jnp.float32))
    inputs = tokens.astype(jnp.float32)
    group = math.gcd(PAGES, 8)
    rounds = PAGES // group

    def whole(params, inputs):
        stacked = inputs.reshape(rounds, group, PAGE, D)
        box_groups = boxes.reshape(rounds, group, 4, PAGE)
        length_groups = lengths.reshape(rounds, group)

        def one_group(carry, item):
            piece, box_piece, length_piece = item
            return (carry, layer_forward(params, piece, box_piece, length_piece))
        _, results = lax.scan(jax.checkpoint(one_group), jnp.zeros((), jnp.float32), (stacked, box_groups, length_groups))
        return results.reshape(PAGES, PAGE, D)
    output, pullback = jax.vjp(whole, params, inputs)
    grad_params, grad_inputs = pullback(cotangent.astype(jnp.float32))
    return (output.astype(jnp.bfloat16), grad_inputs.astype(jnp.bfloat16), grad_params[0], grad_params[1], grad_params[2], grad_params[3], grad_params[4], grad_params[5], grad_params[6], grad_params[7], grad_params[8], grad_params[9], grad_params[10], grad_params[11], grad_params[12], grad_params[13])
```

```python
import math

import jax
import jax.numpy as jnp
from jax import lax
from jax.sharding import PartitionSpec as P

HEADS = 12

epsilon = 1e-06
masked_score = -1000000000.0


def box_tables(boxes, quarter):
    rates = jnp.exp(jnp.arange(quarter, dtype=jnp.float32) * (-math.log(10000.0) / quarter))
    centre_x = (boxes[0] + boxes[2]).astype(jnp.float32) * 0.5
    centre_y = (boxes[1] + boxes[3]).astype(jnp.float32) * 0.5
    angle_x = centre_x[:, None] * rates
    angle_y = centre_y[:, None] * rates
    return (jnp.sin(angle_x), jnp.cos(angle_x), jnp.sin(angle_y), jnp.cos(angle_y))


def layer_norm(values, gain, shift):
    mean = jnp.mean(values, -1, keepdims=True)
    centred = values - mean
    variance = jnp.mean(centred * centred, -1, keepdims=True)
    return centred * lax.rsqrt(variance + epsilon) * gain + shift


def gelu_exact(values):
    return jax.nn.gelu(values, approximate=False)


def quarters(values):
    quarter = values.shape[-1] // 4
    return (
        values[..., :quarter],
        values[..., quarter : 2 * quarter],
        values[..., 2 * quarter : 3 * quarter],
        values[..., 3 * quarter :],
    )


def dot(spec, a, b):
    return jnp.einsum(spec, a, b, preferred_element_type=jnp.float32)


def swap(x):
    return lax.ppermute(x, "slab", [(0, 1), (1, 0)])


def own_page(x, core):
    mine = lax.dynamic_index_in_dim(x, core, 0, keepdims=False)
    other = swap(lax.dynamic_index_in_dim(x, 1 - core, 0, keepdims=False))
    return jnp.where(
        core == 0, jnp.concatenate([mine, other], 0), jnp.concatenate([other, mine], 0)
    )


def own_rows(x, core):
    x = x.reshape(2, x.shape[0] // 2, x.shape[1])
    mine = lax.dynamic_index_in_dim(x, core, 0, keepdims=False)
    other = swap(lax.dynamic_index_in_dim(x, 1 - core, 0, keepdims=False))
    return jnp.where(core == 0, jnp.stack([mine, other], 0), jnp.stack([other, mine], 0))


def scatter_sum(g, place, order):
    n, r, c = g.shape
    left = list(range(n.bit_length() - 2, -1, -1))
    acc = g.reshape((2,) * len(left) + (r, c))
    for bit in order:
        axis = left.index(bit)
        mine = (place >> bit) & 1
        send = lax.dynamic_index_in_dim(acc, 1 - mine, axis, keepdims=False)
        keep = lax.dynamic_index_in_dim(acc, mine, axis, keepdims=False)
        got = lax.ppermute(send, "pages", [(i, i ^ (1 << bit)) for i in range(n)])
        acc = (keep.astype(jnp.float32) + got.astype(jnp.float32)).astype(jnp.bfloat16)
        left.remove(bit)
    return acc


def orders(bits):
    low = list(range(bits - 1))
    return [low[i:] + low[:i] + [bits - 1] for i in range(3)]


def reduce_grad(g, place, core, n):
    rows, cols = g.shape
    halves = g.astype(jnp.bfloat16).reshape(n, rows // n, 2, cols // 2)
    keep = lax.dynamic_index_in_dim(halves, core, 2, keepdims=False)
    got = swap(lax.dynamic_index_in_dim(halves, 1 - core, 2, keepdims=False))
    acc = (keep.astype(jnp.float32) + got.astype(jnp.float32)).astype(jnp.bfloat16)
    width = cols // 6
    parts = [
        scatter_sum(acc[:, :, i * width : (i + 1) * width], place, order)
        for i, order in enumerate(orders(n.bit_length() - 1))
    ]
    mine = jnp.concatenate(parts, -1)
    other = swap(mine)
    return jnp.where(
        core == 0, jnp.concatenate([mine, other], -1), jnp.concatenate([other, mine], -1)
    ).astype(jnp.float32)


def body(
    n,
    tokens,
    boxes,
    lengths,
    w_qkv,
    b_qkv,
    w_posk,
    w_posq,
    w_out,
    b_out,
    gain_one,
    shift_one,
    w_in,
    b_in,
    w_down,
    b_down,
    gain_two,
    shift_two,
    cotangent,
):
    f32, bf16 = jnp.float32, jnp.bfloat16
    place, core = lax.axis_index("pages"), lax.axis_index("slab")
    tokens = own_page(tokens, core)
    cotangent = own_page(cotangent, core)
    boxes = lax.dynamic_index_in_dim(boxes, core, 0, keepdims=False)
    length = lax.dynamic_index_in_dim(lengths, core, 0, keepdims=False)
    rows, width = tokens.shape
    heads = HEADS
    head_dim = width // heads
    pos_dim = w_posk.shape[0]
    scale = head_dim ** (-0.5)
    sx, cx, sy, cy = box_tables(boxes, pos_dim // 4)
    key_factor = jnp.concatenate([cx, sx, cy, sy], -1).astype(bf16)
    query_factor = jnp.concatenate([sx, cx, sy, cy], -1).astype(bf16)
    sx, cx, sy, cy = (t[:, None, :] for t in (sx, cx, sy, cy))
    valid = jnp.arange(rows, dtype=jnp.int32) < length
    pos_k = w_posk.reshape(pos_dim, heads, head_dim)
    pos_q = w_posq.reshape(pos_dim, heads, head_dim)
    proj = (dot("rd,dc->rc", tokens, w_qkv) + b_qkv.astype(f32)).astype(bf16)
    query = proj[:, :width].reshape(rows, heads, head_dim)
    key = proj[:, width : 2 * width].reshape(rows, heads, head_dim)
    value = proj[:, 2 * width :].reshape(rows, heads, head_dim)
    bxs, bxc, bys, byc = quarters(dot("jhe,khe->jhk", key, pos_q))
    z = jnp.concatenate(
        [bxs * cx + bxc * sx, bxc * cx - bxs * sx, bys * cy + byc * sy, byc * cy - bys * sy], -1
    ).astype(bf16)
    axs, axc, ays, ayc = quarters(dot("ihe,khe->ihk", query, pos_k))
    u = jnp.concatenate(
        [axs * sx + axc * cx, axc * sx - axs * cx, ays * sy + ayc * cy, ayc * sy - ays * cy], -1
    ).astype(bf16)
    shape = (rows, heads, pos_dim)
    left = jnp.concatenate(
        [query, u, jnp.broadcast_to(query_factor[:, None, :], shape)], -1
    )
    right = jnp.concatenate([key, jnp.broadcast_to(key_factor[:, None, :], shape), z], -1)
    score = jnp.where(valid[None, None, :], dot("ihk,jhk->hij", left, right) * scale, masked_score)
    probs = jax.nn.softmax(score, -1).astype(bf16)
    attended = dot("hij,jhe->ihe", probs, value).reshape(rows, width).astype(bf16)
    branch = dot("rd,dc->rc", attended, w_out) + b_out.astype(f32)
    gain_one, shift_one = gain_one.astype(f32), shift_one.astype(f32)
    residual_one = tokens.astype(f32) + branch
    first = layer_norm(residual_one, gain_one, shift_one)
    first_low = first.astype(bf16)
    hidden = dot("rd,df->rf", first_low, w_in) + b_in.astype(f32)
    active = gelu_exact(hidden).astype(bf16)
    second = dot("rf,fd->rd", active, w_down) + b_down.astype(f32)
    output, norm_two_back = jax.vjp(
        layer_norm, first + second, gain_two.astype(f32), shift_two.astype(f32)
    )
    d_res_two, g_gain_two, g_shift_two = norm_two_back(cotangent.astype(f32))
    d_second = d_res_two.astype(bf16)
    g_w_down = dot("rf,rd->fd", active, d_second)
    g_b_down = jnp.sum(d_second.astype(f32), 0)
    d_active = dot("rd,fd->rf", d_second, w_down).astype(bf16)
    _, gelu_back = jax.vjp(gelu_exact, hidden)
    d_hidden = gelu_back(d_active.astype(f32))[0].astype(bf16)
    g_w_in = dot("rd,rf->df", first_low, d_hidden)
    g_b_in = jnp.sum(d_hidden.astype(f32), 0)
    d_first = d_res_two + dot("rf,df->rd", d_hidden, w_in).astype(bf16).astype(f32)
    _, norm_one_back = jax.vjp(layer_norm, residual_one, gain_one, shift_one)
    d_res_one, g_gain_one, g_shift_one = norm_one_back(d_first)
    d_branch = d_res_one.astype(bf16)
    g_w_out = dot("rd,rc->dc", attended, d_branch)
    g_b_out = jnp.sum(d_branch.astype(f32), 0)
    d_attended = dot("rc,dc->rd", d_branch, w_out).astype(bf16).reshape(rows, heads, head_dim)
    d_probs = dot("ihe,jhe->hij", d_attended, value)
    probs_wide = probs.astype(f32)
    d_score = (probs_wide * (d_probs - jnp.sum(d_probs * probs_wide, -1, keepdims=True))).astype(
        bf16
    )
    d_value = dot("hij,ihe->jhe", probs, d_attended).astype(bf16)
    d_query_text = dot("hij,jhe->ihe", d_score, key) * scale
    d_u = (dot("hij,jk->ihk", d_score, key_factor) * scale).astype(bf16)
    d_key_text = dot("hij,ihe->jhe", d_score, query) * scale
    d_z = dot("hij,ik->jhk", d_score, query_factor) * scale
    zx1, zx2, zy1, zy2 = quarters(d_z)
    d_b = jnp.concatenate(
        [zx1 * cx - zx2 * sx, zx1 * sx + zx2 * cx, zy1 * cy - zy2 * sy, zy1 * sy + zy2 * cy], -1
    ).astype(bf16)
    ux1, ux2, uy1, uy2 = quarters(d_u.astype(f32))
    d_a = jnp.concatenate(
        [ux1 * sx - ux2 * cx, ux1 * cx + ux2 * sx, uy1 * sy - uy2 * cy, uy1 * cy + uy2 * sy], -1
    ).astype(bf16)
    d_key = (d_key_text + dot("jhk,khe->jhe", d_b, pos_q)).astype(bf16)
    d_query = (d_query_text + dot("ihk,khe->ihe", d_a, pos_k)).astype(bf16)
    g_w_posq = dot("jhk,jhe->khe", d_b, key).reshape(pos_dim, width)
    g_w_posk = dot("ihk,ihe->khe", d_a, query).reshape(pos_dim, width)
    d_proj = jnp.concatenate(
        [x.reshape(rows, width) for x in (d_query, d_key, d_value)], -1
    )
    g_w_qkv = dot("rd,rc->dc", tokens, d_proj)
    g_b_qkv = jnp.sum(d_proj.astype(f32), 0)
    d_tokens = d_res_one + dot("rc,dc->rd", d_proj, w_qkv)
    big = [
        reduce_grad(g, place, core, n)
        for g in (g_w_down, g_w_in, g_w_out, g_w_posk, g_w_posq, g_w_qkv)
    ]
    small = (
        g_b_qkv, g_b_out, g_gain_one, g_shift_one, g_b_in, g_b_down, g_gain_two, g_shift_two
    )
    packed = jnp.concatenate([g.reshape(n, -1) for g in small], -1)
    packed = lax.psum(packed, ("pages", "slab"))
    packed = lax.dynamic_index_in_dim(packed, place, 0, keepdims=False)
    totals, at = [], 0
    for g in small:
        totals.append(packed[at : at + g.size // n])
        at += g.size // n
    return (
        own_rows(output.astype(bf16), core),
        own_rows(d_tokens.astype(bf16), core),
        big[5],
        totals[0],
        big[3],
        big[4],
        big[2],
        totals[1],
        totals[2],
        totals[3],
        big[1],
        totals[4],
        big[0],
        totals[5],
        totals[6],
        totals[7],
    )


def solution(mesh):
    import functools

    n = mesh.shape["pages"]
    rows = P("pages", "slab", None)
    mat, vec = P("pages", None), P("pages")
    return jax.shard_map(
        functools.partial(body, n),
        mesh=mesh,
        in_specs=(rows, P("pages", None, None), P("pages")) + (P(),) * 14 + (rows,),
        out_specs=(rows, rows, mat, vec, mat, mat, mat, vec, vec, vec, mat, vec, mat, vec, vec, vec),
        check_vma=False,
    )
```

```python
import functools
import math

import jax
import jax.numpy as jnp
import numpy as np
from jax import lax
from jax.experimental import pallas as pl
from jax.experimental.pallas import tpu as pltpu
from jax.sharding import PartitionSpec as P

F32, BF16 = jnp.float32, jnp.bfloat16
HEADS = 12
PAIRS = HEADS // 2
BIG = 1e9
SDS = jax.ShapeDtypeStruct


def mm(a, b):
    return lax.dot_general(a, b, (((1,), (0,)), ((), ())), preferred_element_type=F32)


def mm_nt(a, b):
    return lax.dot_general(a, b, (((1,), (1,)), ((), ())), preferred_element_type=F32)


def whole(shape):
    return pl.BlockSpec(shape, lambda *_: (0,) * len(shape))


def call(kernel, name, grid, ids, args, in_specs, out_specs, out_shape, scratch=(), vmem=40, flops=0, moved=0):
    return pl.pallas_call(
        kernel,
        grid_spec=pltpu.PrefetchScalarGridSpec(
            num_scalar_prefetch=1, grid=grid, in_specs=in_specs, out_specs=out_specs, scratch_shapes=list(scratch)
        ),
        out_shape=out_shape,
        compiler_params=pltpu.CompilerParams(vmem_limit_bytes=vmem << 20),
        cost_estimate=pl.CostEstimate(flops=flops, bytes_accessed=moved, transcendentals=0),
        name=name,
    )(ids, *args)


def sin_cos(angle):
    turns = jnp.round(angle * (2.0 / math.pi))
    r = angle - turns * 1.5703125
    r = r - turns * 4.837512969970703125e-4
    r = r - turns * 7.54978995489188216e-8
    z = r * r
    s = ((-1.9515295891e-4 * z + 8.3321608736e-3) * z - 1.6666654611e-1) * z * r + r
    c = (
        (2.443315711809948e-5 * z - 1.388731625493765e-3) * z + 4.166664568298827e-2
    ) * z * z + (1.0 - 0.5 * z)
    q = turns.astype(jnp.int32)
    odd = (q & 1) == 1
    one, two = jnp.where(odd, c, s), jnp.where(odd, s, c)
    sine = jnp.where((q & 2) == 2, -one, one)
    cosine = jnp.where(((q + 1) & 2) == 2, -two, two)
    return sine, cosine


def project_kernel(ids, own_ref, other_ref, w_ref, b_ref, box_ref, rrow_ref, rcol_ref, wk_ref, wq_ref,
                   pt_ref, p_ref, xt_ref, kf_ref, tab_ref, tabt_ref, fkt_ref, fqt_ref, wkt_ref, wqt_ref, x):
    step = pl.program_id(0)

    @pl.when(step == 0)
    def _():
        half = own_ref.shape[1]
        x[:half, :] = own_ref[0]
        x[half:, :] = other_ref[0]
        xt_ref[...] = x[...].T
        wkt_ref[...] = wk_ref[...].T
        wqt_ref[...] = wq_ref[...].T
        box = box_ref[0].astype(F32)
        centre = (box[0:2, :] + box[2:4, :]) * 0.5
        turned = jnp.concatenate([centre[:, half:], centre[:, :half]], 1)
        centre = jnp.where(ids[1] == 0, centre, turned)
        column = jnp.concatenate([centre, jnp.zeros((6, 2 * half), F32)], 0).T
        front = lax.broadcasted_iota(jnp.int32, (2 * half, 128), 1) < 64
        for axis in range(2):
            s, c = sin_cos(column[:, axis : axis + 1] * rrow_ref[...])
            kf_ref[:, axis * 128 : axis * 128 + 128] = jnp.where(front, c, s).astype(BF16)
            tab_ref[axis] = c
            tab_ref[2 + axis] = jnp.where(front, s, -s)
            st, ct = sin_cos(rcol_ref[...] * centre[axis : axis + 1, :])
            tabt_ref[2 * axis] = st
            tabt_ref[2 * axis + 1] = ct
            sl, cl = st.astype(BF16), ct.astype(BF16)
            at = 128 * axis
            fkt_ref[at : at + 64, :] = cl
            fkt_ref[at + 64 : at + 128, :] = sl
            fqt_ref[at : at + 64, :] = sl * 0.125
            fqt_ref[at + 64 : at + 128, :] = cl * 0.125

    p = (mm(x[...], w_ref[...]) + b_ref[...]).astype(BF16)
    p_ref[...] = p
    pt_ref[...] = p.T


def page_specs(half, width):
    spec = pl.BlockSpec((1, half, width), lambda i, ids: (ids[1], 0, 0))
    return spec, spec


def project(ids, tokens, other, w, vectors, boxes, wk, wq):
    _, half, width = tokens.shape
    rows = 2 * half
    cols = w.shape[1]
    block = 768
    rates = np.exp(np.arange(64) * (-math.log(10000.0) / 64)).astype(np.float32)
    return call(
        project_kernel, "project", (cols // block,), ids,
        (tokens, other, w, vectors, boxes, np.tile(rates, 2)[None, :], rates[:, None], wk, wq),
        [
            *page_specs(half, width),
            pl.BlockSpec((width, block), lambda i, ids: (0, i)),
            pl.BlockSpec((1, block), lambda i, ids: (0, 4 + i)),
            pl.BlockSpec((1, 4, rows), lambda i, ids: (ids[1], 0, 0)),
            whole((1, 128)), whole((64, 1)), whole((256, width)), whole((256, width)),
        ],
        [
            pl.BlockSpec((block, rows), lambda i, ids: (i, 0)),
            pl.BlockSpec((rows, block), lambda i, ids: (0, i)),
            whole((width, rows)), whole((rows, 256)), whole((4, rows, 128)), whole((4, 64, rows)),
            whole((256, rows)), whole((256, rows)), whole((width, 256)), whole((width, 256)),
        ],
        [
            SDS((cols, rows), BF16), SDS((rows, cols), BF16), SDS((width, rows), BF16), SDS((rows, 256), BF16),
            SDS((4, rows, 128), F32), SDS((4, 64, rows), F32), SDS((256, rows), BF16), SDS((256, rows), BF16),
            SDS((width, 256), BF16), SDS((width, 256), BF16),
        ],
        [pltpu.VMEM((rows, width), BF16)],
        flops=2 * rows * width * cols, moved=2 * (width * cols + 2 * rows * cols),
    )


def attend_kernel(ids, qt_ref, vt_ref, k_ref, wk_ref, wq_ref, kf_ref, tab_ref, tabt_ref, fqt_ref,
                  e_ref, at_ref, r_ref, fk, fq):
    rows = k_ref.shape[0]

    @pl.when(pl.program_id(0) == 0)
    def _():
        lane = lax.broadcasted_iota(jnp.int32, (rows, 128), 1)
        at = lax.broadcasted_iota(jnp.int32, (rows, 128), 0)
        turned = jnp.where(at < rows // 2, at + rows // 2, at - rows // 2)
        at = jnp.where(ids[1] == 0, at, turned)
        fk[:, 0:256] = kf_ref[...]
        fk[:, 640:768] = jnp.where((lane == 0) & (at >= ids[2]), -BIG, 0.0).astype(BF16)
        fq[256:512, :] = fqt_ref[...]
        sub = lax.broadcasted_iota(jnp.int32, (128, rows), 0)
        fq[640:768, :] = jnp.where(sub == 0, 1.0, 0.0).astype(BF16)

    fk[:, 512:640] = k_ref[...]
    lane = lax.broadcasted_iota(jnp.int32, (256, 128), 1)
    for h in range(2):
        mine = (lane < 64) if h == 0 else (lane >= 64)
        qt = qt_ref[h * 64 : h * 64 + 64, :]
        zero = jnp.zeros_like(qt)
        pad = jnp.concatenate([qt, zero] if h == 0 else [zero, qt], 0)
        fq[512:640, :] = pad * 0.125
        a = mm(wk_ref[...], pad)
        sx, cx, sy, cy = (tabt_ref[i] * 0.125 for i in range(4))
        axs, axc, ays, ayc = (a[i * 64 : i * 64 + 64, :] for i in range(4))
        fq[0:64, :] = (axs * sx + axc * cx).astype(BF16)
        fq[64:128, :] = (axc * sx - axs * cx).astype(BF16)
        fq[128:192, :] = (ays * sy + ayc * cy).astype(BF16)
        fq[192:256, :] = (ayc * sy - ays * cy).astype(BF16)
        w = jnp.where(mine, wq_ref[...], 0).astype(BF16)
        b = mm_nt(k_ref[...], w)
        for axis in range(2):
            part = b[:, axis * 128 : axis * 128 + 128]
            turned = pltpu.roll(part, 64, 1)
            fk[:, 256 + axis * 128 : 384 + axis * 128] = (
                part * tab_ref[axis] + turned * tab_ref[2 + axis]
            ).astype(BF16)
        s = mm(fk[...], fq[...])
        e = jnp.exp(s - jnp.max(s, 0, keepdims=True))
        r = 1.0 / jnp.sum(e, 0, keepdims=True)
        low = e.astype(BF16)
        e_ref[h] = low
        at_ref[h * 64 : h * 64 + 64, :] = (mm(vt_ref[h * 64 : h * 64 + 64, :], low) * r).astype(BF16)
        r_ref[0, h : h + 1, :] = r


def attend(ids, pt, p, w_posk, w_posq, kf, tab, tabt, fqt):
    rows = p.shape[0]
    width = pt.shape[0] // 3
    return call(
        attend_kernel, "attend", (PAIRS,), ids, (pt, pt, p, w_posk, w_posq, kf, tab, tabt, fqt),
        [
            pl.BlockSpec((128, rows), lambda i, ids: (i, 0)),
            pl.BlockSpec((128, rows), lambda i, ids: (2 * PAIRS + i, 0)),
            pl.BlockSpec((rows, 128), lambda i, ids: (0, PAIRS + i)),
            pl.BlockSpec((256, 128), lambda i, ids: (0, i)),
            pl.BlockSpec((256, 128), lambda i, ids: (0, i)),
            whole((rows, 256)), whole((4, rows, 128)), whole((4, 64, rows)), whole((256, rows)),
        ],
        [
            pl.BlockSpec((2, rows, rows), lambda i, ids: (i, 0, 0)),
            pl.BlockSpec((128, rows), lambda i, ids: (i, 0)),
            pl.BlockSpec((1, 2, rows), lambda i, ids: (i, 0, 0)),
        ],
        [SDS((HEADS, rows, rows), BF16), SDS((width, rows), BF16), SDS((PAIRS, 2, rows), F32)],
        [pltpu.VMEM((rows, 768), BF16), pltpu.VMEM((768, rows), BF16)],
        flops=2 * HEADS * rows * rows * 640, moved=2 * HEADS * rows * rows,
    )


def feed_kernel(ids, at_ref, own_ref, other_ref, wo_ref, bo_ref, g1_ref, s1_ref, wi_ref, bi_ref, wd_ref, bd_ref,
                g2_ref, s2_ref, cown_ref, cother_ref,
                flt_ref, norm_ref, rstd_ref, slope_ref, actt_ref, keep_ref, give_ref, dres_ref, dsec_ref, send_ref,
                rows_ref, first, low, second, cot):
    step = pl.program_id(0)
    half = own_ref.shape[1]

    @pl.when(step == 0)
    def _():
        first[:half, :] = own_ref[0].astype(F32)
        first[half:, :] = other_ref[0].astype(F32)
        cot[:half, :] = cown_ref[0]
        cot[half:, :] = cother_ref[...]
        v = first[...] + (mm(at_ref[...].T, wo_ref[...]) + bo_ref[...])
        c = v - jnp.mean(v, -1, keepdims=True)
        rstd = lax.rsqrt(jnp.mean(c * c, -1, keepdims=True) + 1e-6)
        normed = c * rstd
        norm_ref[...] = normed
        rstd_ref[...] = rstd
        f = normed * g1_ref[...] + s1_ref[...]
        first[...] = f + bd_ref[...]
        l = f.astype(BF16)
        low[...] = l
        flt_ref[...] = l.T

    h = mm(low[...], wi_ref[...]) + bi_ref[...]
    cdf = 0.5 * lax.erf(h * (0.5 ** 0.5)) + 0.5
    active = (h * cdf).astype(BF16)
    slope_ref[...] = (cdf + h * (jnp.exp(-0.5 * h * h) * ((2.0 * math.pi) ** -0.5))).astype(BF16)
    actt_ref[...] = active.T
    part = mm(active, wd_ref[...])

    @pl.when(step == 0)
    def _():
        second[...] = part

    @pl.when(step > 0)
    def _():
        second[...] += part

    @pl.when(step == pl.num_programs(0) - 1)
    def _():
        v = first[...] + second[...]
        c = v - jnp.mean(v, -1, keepdims=True)
        rstd = lax.rsqrt(jnp.mean(c * c, -1, keepdims=True) + 1e-6)
        normed = c * rstd
        out = (normed * g2_ref[...] + s2_ref[...]).astype(BF16)
        keep_ref[...] = out[:half, :]
        give_ref[...] = out[half:, :]
        g = cot[...].astype(F32)
        gg = g * g2_ref[...]
        d = rstd * (
            gg - jnp.mean(gg, -1, keepdims=True) - normed * jnp.mean(gg * normed, -1, keepdims=True)
        )
        dres_ref[...] = d
        l = d.astype(BF16)
        dsec_ref[...] = l
        side = send_ref.shape[1]
        send_ref[...] = dsec_ref[:, pl.ds(pl.multiple_of((1 - ids[1]) * side, 128), side)]
        rows_ref[0:1, :] = jnp.sum(g * normed, 0, keepdims=True)
        rows_ref[1:2, :] = jnp.sum(g, 0, keepdims=True)
        rows_ref[2:3, :] = jnp.sum(l.astype(F32), 0, keepdims=True)
        rows_ref[3:8, :] = jnp.zeros((5, rows_ref.shape[1]), F32)


def vec(at):
    return pl.BlockSpec((1, 768), lambda i, ids: (0, at))


def feed(ids, att, tokens, other, w_out, w_in, w_down, vectors, cot, cot_other):
    _, half, width = tokens.shape
    rows = 2 * half
    ff = w_in.shape[1]
    block = 512
    mat = whole((rows, width))
    return call(
        feed_kernel, "feed", (ff // block,), ids,
        (att, tokens, other, w_out, vectors, vectors, vectors, w_in, vectors, w_down, vectors, vectors, vectors,
         cot, cot_other),
        [
            whole((width, rows)), *page_specs(half, width), whole((width, width)), vec(7), vec(8), vec(9),
            pl.BlockSpec((width, block), lambda i, ids: (0, i)),
            pl.BlockSpec((1, block), lambda i, ids: (0, i)),
            pl.BlockSpec((block, width), lambda i, ids: (i, 0)),
            vec(10), vec(11), vec(12), page_specs(half, width)[0], whole((half, width)),
        ],
        [
            whole((width, rows)), mat, whole((rows, 1)),
            pl.BlockSpec((rows, block), lambda i, ids: (0, i)),
            pl.BlockSpec((block, rows), lambda i, ids: (i, 0)),
            whole((half, width)), whole((half, width)), mat, mat, whole((rows, width // 2)), whole((8, width)),
        ],
        [
            SDS((width, rows), BF16), SDS((rows, width), F32), SDS((rows, 1), F32),
            SDS((rows, ff), BF16), SDS((ff, rows), BF16),
            SDS((half, width), BF16), SDS((half, width), BF16), SDS((rows, width), F32), SDS((rows, width), BF16),
            SDS((rows, width // 2), BF16), SDS((8, width), F32),
        ],
        [pltpu.VMEM((rows, width), F32), pltpu.VMEM((rows, width), BF16), pltpu.VMEM((rows, width), F32),
         pltpu.VMEM((rows, width), BF16)],
        flops=2 * rows * width * (width + 2 * ff), moved=2 * (2 * width * ff + 2 * rows * ff),
    )


def hidden_kernel(ids, ds_ref, wd_ref, slope_ref, send_ref, own_ref, rows_ref):
    step = pl.program_id(0)
    d = mm_nt(ds_ref[...], wd_ref[...]).astype(BF16).astype(F32)
    dh = (d * slope_ref[...].astype(F32)).astype(BF16)
    rows_ref[...] = jnp.sum(dh.astype(F32), 0, keepdims=True)
    sends = pl.num_programs(0) // 2

    @pl.when(step < sends)
    def _():
        send_ref[...] = dh

    @pl.when(step >= sends)
    def _():
        own_ref[...] = dh


def hidden_back(ids, dsec, w_down, slope):
    rows, width = dsec.shape
    ff = w_down.shape[0]
    block = 768
    steps = ff // block
    s = steps // 2
    at = lambda i, ids: jnp.where(ids[1] == 0, (i + s) % steps, i)
    return call(
        hidden_kernel, "hidden_back", (steps,), ids, (dsec, w_down, slope),
        [
            whole((rows, width)),
            pl.BlockSpec((block, width), lambda i, ids: (at(i, ids), 0)),
            pl.BlockSpec((rows, block), lambda i, ids: (0, at(i, ids))),
        ],
        [
            pl.BlockSpec((rows, block), lambda i, ids: (0, jnp.minimum(i, s - 1))),
            pl.BlockSpec((rows, block), lambda i, ids: (0, jnp.maximum(i - s, 0))),
            pl.BlockSpec((1, block), lambda i, ids: (0, at(i, ids))),
        ],
        [SDS((rows, ff // 2), BF16), SDS((rows, ff // 2), BF16), SDS((1, ff), F32)],
        flops=2 * rows * width * ff, moved=2 * (width * ff + 2 * rows * ff),
    )


def first_kernel(ids, dsend_ref, down_ref, wsend_ref, wown_ref, dres_ref, norm_ref, rstd_ref, g1_ref, wo_ref,
                 res_ref, branch_ref, send_ref, datt_ref, rows_ref, acc):
    step = pl.program_id(0)
    part = mm_nt(dsend_ref[...], wsend_ref[...]) + mm_nt(down_ref[...], wown_ref[...])

    @pl.when(step == 0)
    def _():
        acc[...] = part

    @pl.when(step > 0)
    def _():
        acc[...] += part

    @pl.when(step == pl.num_programs(0) - 1)
    def _():
        g = dres_ref[...] + acc[...].astype(BF16).astype(F32)
        normed = norm_ref[...]
        gg = g * g1_ref[...]
        d = rstd_ref[...] * (
            gg - jnp.mean(gg, -1, keepdims=True) - normed * jnp.mean(gg * normed, -1, keepdims=True)
        )
        res_ref[...] = d
        l = d.astype(BF16)
        branch_ref[...] = l
        side = send_ref.shape[1]
        send_ref[...] = branch_ref[:, pl.ds(pl.multiple_of((1 - ids[1]) * side, 128), side)]
        datt_ref[...] = mm_nt(wo_ref[...], l).astype(BF16)
        rows_ref[0:1, :] = jnp.sum(g * normed, 0, keepdims=True)
        rows_ref[1:2, :] = jnp.sum(g, 0, keepdims=True)
        rows_ref[2:3, :] = jnp.sum(l.astype(F32), 0, keepdims=True)
        rows_ref[3:8, :] = jnp.zeros((5, rows_ref.shape[1]), F32)


def first_back(ids, dsend, down, w_in, dres, norm, rstd, vectors, w_out):
    rows, width = dres.shape
    ff = w_in.shape[1]
    block = 512
    s = ff // block // 2
    mat = whole((rows, width))
    return call(
        first_kernel, "first_back", (s,), ids, (dsend, down, w_in, w_in, dres, norm, rstd, vectors, w_out),
        [
            pl.BlockSpec((rows, block), lambda i, ids: (0, i)),
            pl.BlockSpec((rows, block), lambda i, ids: (0, i)),
            pl.BlockSpec((width, block), lambda i, ids: (0, (1 - ids[1]) * s + i)),
            pl.BlockSpec((width, block), lambda i, ids: (0, ids[1] * s + i)),
            mat, mat, whole((rows, 1)), vec(8), whole((width, width)),
        ],
        [mat, mat, whole((rows, width // 2)), whole((width, rows)), whole((8, width))],
        [
            SDS((rows, width), F32), SDS((rows, width), BF16), SDS((rows, width // 2), BF16), SDS((width, rows), BF16),
            SDS((8, width), F32),
        ],
        [pltpu.VMEM((rows, width), F32)],
        flops=2 * rows * width * (width + ff), moved=2 * (width * ff + rows * ff + 5 * rows * width),
    )


def attend_back_kernel(ids, e_ref, r_ref, da_ref, at_ref, qt_ref, kt_ref, v_ref, wkt_ref, wqt_ref, fkt_ref, fqt_ref,
                       tabt_ref, dp_ref, gk_ref, gq_ref, left_k, left_q):
    @pl.when(pl.program_id(0) == 0)
    def _():
        left_k[64:320, :] = fkt_ref[...]
        left_q[64:320, :] = fqt_ref[...]

    sx, cx, sy, cy = (tabt_ref[i] for i in range(4))
    lane = lax.broadcasted_iota(jnp.int32, (256, 128), 1)
    gk, gq = [], []
    for h in range(2):
        own = slice(h * 64, h * 64 + 64)
        da = da_ref[own, :].astype(F32) * r_ref[0, h : h + 1, :]
        delta = jnp.sum(da * at_ref[own, :].astype(F32), 0, keepdims=True)
        da = da.astype(BF16)
        zero = jnp.zeros_like(da)
        pad = jnp.concatenate([da, zero] if h == 0 else [zero, da], 0)
        e = e_ref[h]
        ds = (e.astype(F32) * (mm(v_ref[...], pad) - delta)).astype(BF16)
        left_k[0:64, :] = kt_ref[own, :]
        left_q[0:64, :] = qt_ref[own, :] * 0.125
        one = mm(left_k[...], ds) * 0.125
        two = mm_nt(left_q[...], ds)
        dv = mm_nt(da, e)
        ux1, ux2, uy1, uy2 = (one[64 + i * 64 : 128 + i * 64, :].astype(BF16).astype(F32) for i in range(4))
        d_a = jnp.concatenate(
            [ux1 * sx - ux2 * cx, ux1 * cx + ux2 * sx, uy1 * sy - uy2 * cy, uy1 * cy + uy2 * sy], 0
        ).astype(BF16)
        zx1, zx2, zy1, zy2 = (two[64 + i * 64 : 128 + i * 64, :] for i in range(4))
        d_b = jnp.concatenate(
            [zx1 * cx - zx2 * sx, zx1 * sx + zx2 * cx, zy1 * cy - zy2 * sy, zy1 * sy + zy2 * cy], 0
        ).astype(BF16)
        dp_ref[0, own, :] = (one[0:64, :] + mm(wkt_ref[own, :], d_a)).astype(BF16)
        dp_ref[1, own, :] = (two[0:64, :] + mm(wqt_ref[own, :], d_b)).astype(BF16)
        dp_ref[2, own, :] = dv.astype(BF16)
        gk.append(mm_nt(d_a, qt_ref[...]))
        gq.append(mm_nt(d_b, kt_ref[...]))
    gk_ref[...] = jnp.where(lane < 64, gk[0], gk[1]).astype(BF16)
    gq_ref[...] = jnp.where(lane < 64, gq[0], gq[1]).astype(BF16)


def attend_back(ids, own, e, r, datt, att, pt, p, wkt, wqt, fkt, fqt, tabt):
    rows = p.shape[0]
    pairs = PAIRS // 2
    lo = lambda ids: (ids[1] if own else 1 - ids[1]) * pairs
    pair = lambda base: pl.BlockSpec((128, rows), lambda i, ids: (base + lo(ids) + i, 0))
    wt = pl.BlockSpec((128, 256), lambda i, ids: (lo(ids) + i, 0))
    return call(
        attend_back_kernel, "attend_back", (pairs,), ids, (e, r, datt, att, pt, pt, p, wkt, wqt, fkt, fqt, tabt),
        [
            pl.BlockSpec((2, rows, rows), lambda i, ids: (lo(ids) + i, 0, 0)),
            pl.BlockSpec((1, 2, rows), lambda i, ids: (lo(ids) + i, 0, 0)),
            pair(0), pair(0), pair(0), pair(PAIRS),
            pl.BlockSpec((rows, 128), lambda i, ids: (0, 2 * PAIRS + lo(ids) + i)),
            wt, wt, whole((256, rows)), whole((256, rows)), whole((4, 64, rows)),
        ],
        [
            pl.BlockSpec((3, 128, rows), lambda i, ids: (0, i, 0)),
            pl.BlockSpec((256, 128), lambda i, ids: (0, i)),
            pl.BlockSpec((256, 128), lambda i, ids: (0, i)),
        ],
        [SDS((3, 128 * pairs, rows), BF16), SDS((256, 128 * pairs), BF16), SDS((256, 128 * pairs), BF16)],
        [pltpu.VMEM((320, rows), BF16), pltpu.VMEM((320, rows), BF16)],
        flops=2 * 2 * pairs * rows * rows * 900, moved=2 * 2 * pairs * rows * rows,
    )


def tokens_kernel(ids, w_ref, ds_ref, do_ref, dres_ref, keep_ref, give_ref, rows_ref):
    width = w_ref.shape[1] // 3
    side = width // 2
    half = keep_ref.shape[0]
    acc = None
    for h, ref in ((1 - ids[1], ds_ref), (ids[1], do_ref)):
        for s in range(3):
            at = pl.multiple_of(s * width + h * side, 128)
            part = mm(w_ref[:, pl.ds(at, side)], ref[s])
            acc = part if acc is None else acc + part
    out = (dres_ref[...] + acc.T).astype(BF16)
    keep_ref[...] = out[:half, :]
    give_ref[...] = out[half:, :]

    @pl.when(pl.program_id(0) == 0)
    def _():
        ones = jnp.ones((8, ds_ref.shape[2]), BF16)
        for s in range(3):
            for h, ref in ((1 - ids[1], ds_ref), (ids[1], do_ref)):
                at = pl.multiple_of(h * side, 128)
                rows_ref[s : s + 1, pl.ds(at, side)] = mm_nt(ones, ref[s])[0:1, :]
        rows_ref[3:8, :] = jnp.zeros((5, width), F32)


def tokens_back(ids, w_qkv, dsend, down, dres):
    rows, width = dres.shape
    cols = w_qkv.shape[1]
    block = 256
    half = rows // 2
    blk = pl.BlockSpec((half, block), lambda i, ids: (0, i))
    return call(
        tokens_kernel, "tokens_back", (width // block,), ids, (w_qkv, dsend, down, dres),
        [
            pl.BlockSpec((block, cols), lambda i, ids: (i, 0)), whole(dsend.shape), whole(down.shape),
            pl.BlockSpec((rows, block), lambda i, ids: (0, i)),
        ],
        [blk, blk, whole((8, width))],
        [SDS((half, width), BF16), SDS((half, width), BF16), SDS((8, width), F32)],
        flops=2 * rows * width * cols, moved=2 * (width * cols + rows * cols + 3 * rows * width),
    )


def chosen(core, pair):
    return jnp.where(core == 0, pair[0], pair[1])


def drop_bit(p, bit):
    return ((p >> (bit + 1)) << bit) | (p & ((1 << bit) - 1))


def put(ids, bits, p, lanes, value, send_ref, keep_ref):
    bit = chosen(ids[1], bits)
    here = ((p >> bit) & 1) == ((ids[0] >> bit) & 1)
    at = drop_bit(p, bit)

    @pl.when(here)
    def _():
        keep_ref[at, 0 : value.shape[0], lanes] = value

    @pl.when(jnp.logical_not(here))
    def _():
        send_ref[at, 0 : value.shape[0], lanes] = value


def down_kernel(n, bits, ids, a0_ref, a1_ref, b0_ref, b1_ref, send_ref, keep_ref):
    places = n // pl.num_programs(0)
    r, w = keep_ref.shape[1:]
    acc = mm(a0_ref[...], b0_ref[...]) + mm(a1_ref[...], b1_ref[...])
    for k in range(places):
        p = pl.program_id(0) * places + k
        put(ids, bits, p, slice(0, w), acc[k * r : k * r + r, :].astype(BF16), send_ref, keep_ref)


def down_grad(ids, n, bits, actt, actt_other, dsec, dsec_other):
    ff, rows = actt.shape
    side = dsec_other.shape[1]
    block = ff // 4
    part = (n // 2, ff // n, side)
    a = pl.BlockSpec((block, rows), lambda i, ids: (i, 0))
    return call(
        functools.partial(down_kernel, n, bits), "down_grad", (4,), ids, (actt, actt_other, dsec, dsec_other),
        [a, a, pl.BlockSpec((rows, side), lambda i, ids: (0, ids[1])), whole((rows, side))],
        [whole(part)] * 2, [SDS(part, BF16)] * 2,
        flops=4 * ff * rows * side, moved=2 * (2 * ff * rows + ff * side),
    )


def mid_kernel(n, bits, ids, f0_ref, f1_ref, h0_ref, h1_ref, a0_ref, a1_ref, c0_ref, c1_ref, send_ref, keep_ref):
    step = pl.program_id(0)
    last = pl.num_programs(0) - 1
    r = keep_ref.shape[1]
    w = h0_ref.shape[1]

    @pl.when(step < last)
    def _():
        acc = mm(f0_ref[...], h0_ref[...]) + mm(f1_ref[...], h1_ref[...])
        lanes = pl.ds(pl.multiple_of(step * w, 128), w)
        for p in range(n):
            put(ids, bits, p, lanes, acc[p * r : p * r + r, :].astype(BF16), send_ref, keep_ref)

    @pl.when(step == last)
    def _():
        acc = mm(a0_ref[...], c0_ref[...]) + mm(a1_ref[...], c1_ref[...])
        lanes = slice(keep_ref.shape[2] - acc.shape[1], keep_ref.shape[2])
        for p in range(n):
            put(ids, bits, p, lanes, acc[p * r : p * r + r, :].astype(BF16), send_ref, keep_ref)


def mid_grad(ids, n, bits, flt, flt_other, dh, dh_other, att, att_other, branch, branch_other):
    width, rows = flt.shape
    ffs = dh.shape[1]
    side = branch_other.shape[1]
    block = 768
    steps = ffs // block
    part = (n // 2, width // n, ffs + side)
    b = pl.BlockSpec((rows, block), lambda i, ids: (0, jnp.minimum(i, steps - 1)))
    a = whole((width, rows))
    return call(
        functools.partial(mid_kernel, n, bits), "mid_grad", (steps + 1,), ids,
        (flt, flt_other, dh, dh_other, att, att_other, branch, branch_other),
        [a, a, b, b, a, a, pl.BlockSpec((rows, side), lambda i, ids: (0, ids[1])), whole((rows, side))],
        [whole(part)] * 2, [SDS(part, BF16)] * 2,
        flops=4 * width * rows * (ffs + side), moved=2 * (2 * ffs * rows + 2 * width * (ffs + side)),
    )


def chunks(n, size):
    return max(((p + 1) * size - 1) // 128 - p * size // 128 + 1 for p in range(n))


def small_plan(n, sizes):
    plan, at = [], 0
    for size in sizes:
        plan.append((size, chunks(n, size), at))
        at += chunks(n, size)
    return plan, at


def qkv_kernel(n, bits, sizes, ids, x0_ref, x1_ref, d0_ref, d1_ref, k0_ref, k1_ref, q0_ref, q1_ref,
               two_ref, one_ref, in_ref, qkv_ref, send_ref, keep_ref):
    step = pl.program_id(0)
    last = pl.num_programs(0) - 1
    r = keep_ref.shape[1]
    side = d0_ref.shape[1]

    @pl.when(step < last)
    def _():
        acc = mm_nt(x0_ref[...], d0_ref[0]) + mm_nt(x1_ref[...], d1_ref[0])
        lanes = pl.ds(pl.multiple_of(step * side, 128), side)
        for p in range(n):
            put(ids, bits, p, lanes, acc[p * r : p * r + r, :].astype(BF16), send_ref, keep_ref)

    @pl.when(step == last)
    def _():
        base = 3 * side
        for own_ref, other_ref in ((k0_ref, k1_ref), (q0_ref, q1_ref)):
            acc = (own_ref[...].astype(F32) + other_ref[...].astype(F32)).astype(BF16)
            s = acc.shape[0] // n
            for p in range(n):
                rows = acc[p * s : p * s + s, :]
                stacked = jnp.concatenate([rows[:, 128 * i : 128 * i + 128] for i in range(side // 128)], 0)
                put(ids, bits, p, slice(base, base + 128), stacked, send_ref, keep_ref)
            base += 128
        vectors = (qkv_ref, one_ref, one_ref, one_ref, in_ref, two_ref, two_ref, two_ref)
        index = (None, 2, 0, 1, 0, 2, 0, 1)
        plan, _ = small_plan(n, sizes)
        for p in range(n):
            found = []
            for (size, count, _), ref, row in zip(plan, vectors, index):
                for c in range(count):
                    at = min(p * size // 128 + c, n * size // 128 - 1)
                    if row is None:
                        i, at = at * 128 // ref.shape[1], at * 128 % ref.shape[1]
                        found.append(ref[i : i + 1, at : at + 128])
                    else:
                        found.append(ref[row : row + 1, at * 128 : at * 128 + 128])
            found = jnp.concatenate(found + [jnp.zeros((r - len(found), 128), F32)], 0).astype(BF16)
            put(ids, bits, p, slice(base, base + 128), found, send_ref, keep_ref)


def qkv_grad(ids, n, bits, sizes, xt, xt_other, dp, dp_other, gk, gk_other, gq, gq_other, two, one, into, qkv):
    width, rows = xt.shape
    side = dp.shape[1]
    part = (n // 2, width // n, 3 * side + 3 * 128)
    d = pl.BlockSpec((1, side, rows), lambda i, ids: (jnp.minimum(i, 2), 0, 0))
    return call(
        functools.partial(qkv_kernel, n, bits, sizes), "qkv_grad", (4,), ids,
        (xt, xt_other, dp, dp_other, gk, gk_other, gq, gq_other, two, one, into, qkv),
        [whole(xt.shape)] * 2 + [d, d] + [whole(a.shape) for a in (gk, gk, gq, gq, two, one, into, qkv)],
        [whole(part)] * 2, [SDS(part, BF16)] * 2,
        flops=4 * width * rows * 3 * side, moved=2 * (2 * 3 * side * rows + 2 * width * 3 * side),
    )


def add_split_kernel(bits, lows, ids, keep_ref, got_ref, send_ref, next_ref):
    low = chosen(ids[1], lows)
    mine = (ids[0] >> chosen(ids[1], bits)) & 1

    @pl.loop(0, next_ref.shape[0])
    def _(q):
        base = ((q >> low) << (low + 1)) | (q & ((1 << low) - 1))
        for which, ref in ((1 - mine, send_ref), (mine, next_ref)):
            p = base + (which << low)
            ref[q] = (keep_ref[p].astype(F32) + got_ref[p].astype(F32)).astype(BF16)


def add_split(ids, keep, got, bits, lows):
    m, r, w = keep.shape
    part = (m // 2, r, w)
    return call(
        functools.partial(add_split_kernel, bits, lows), "add_split", (1,), ids, (keep, got),
        [whole(keep.shape)] * 2, [whole(part)] * 2, [SDS(part, BF16)] * 2, vmem=24, moved=6 * m * r * w,
    )


def add_last_kernel(ids, keep_ref, got_ref, out_ref):
    out_ref[...] = (keep_ref[0].astype(F32) + got_ref[0].astype(F32)).astype(BF16)


def add_last(ids, keep, got):
    _, r, w = keep.shape
    return call(
        add_last_kernel, "add_last", (1,), ids, (keep, got), [whole(keep.shape)] * 2, whole((r, w)), SDS((r, w), BF16),
        vmem=16, moved=6 * r * w,
    )


def swap(x):
    return lax.ppermute(x, "slab", [(0, 1), (1, 0)])


def across(x, n, bits):
    pairs = [(2 * p + c, 2 * (p ^ (1 << bits[c])) + c) for p in range(n) for c in range(2)]
    return lax.ppermute(x, ("pages", "slab"), pairs)


def orders(n):
    low = list(range(n.bit_length() - 1))
    if len(low) < 3:
        return low, low[::-1]
    a = low
    b = [low[1], low[0]] + low[:1:-1]
    return a, b


class Exchange:
    def __init__(self, ids, n, send, keep, order):
        self.ids, self.n, self.order = ids, n, order
        self.left = [sorted(o) for o in order]
        self.at = 0
        self.keep = keep
        self.got = across(send, n, self.bits(0))

    def bits(self, step):
        return tuple(o[step] for o in self.order)

    def step(self):
        for l, b in zip(self.left, self.bits(self.at)):
            l.remove(b)
        self.at += 1
        if self.at == len(self.order[0]):
            self.mine = add_last(self.ids, self.keep, self.got)
            self.other = swap(self.mine)
            return
        bits = self.bits(self.at)
        lows = tuple(l.index(b) for l, b in zip(self.left, bits))
        send, self.keep = add_split(self.ids, self.keep, self.got, bits, lows)
        self.got = across(send, self.n, bits)


def join_kernel(ids, mine_ref, other_ref, *outs):
    core = ids[1]
    at = 0
    for out in outs:
        side = out.shape[1] // 2
        for who, ref in ((core, mine_ref), (1 - core, other_ref)):
            out[:, pl.ds(pl.multiple_of(who * side, 128), side)] = ref[:, at : at + side].astype(F32)
        at += side


def join(ids, mine, other, widths):
    r = mine.shape[0]
    return call(
        join_kernel, "join", (1,), ids, (mine, other), [whole(mine.shape)] * 2,
        [whole((r, w)) for w in widths], [SDS((r, w), F32) for w in widths], vmem=16, moved=12 * r * sum(widths),
    )


def join_qkv_kernel(ids, mine_ref, other_ref, qkv_ref, posk_ref, posq_ref, small_ref):
    core = ids[1]
    r = mine_ref.shape[0]
    s = posk_ref.shape[0]
    count = r // s
    side = 128 * count
    width = qkv_ref.shape[1] // 3
    for who, ref in ((core, mine_ref), (1 - core, other_ref)):
        for i in range(3):
            at = pl.multiple_of(i * width + who * side, 128)
            qkv_ref[:, pl.ds(at, side)] = ref[:, i * side : i * side + side].astype(F32)
        for j, out in enumerate((posk_ref, posq_ref)):
            lanes = slice(3 * side + 128 * j, 3 * side + 128 * j + 128)
            for i in range(count):
                at = pl.multiple_of(who * side + 128 * i, 128)
                out[:, pl.ds(at, 128)] = ref[i * s : i * s + s, lanes].astype(F32)
    small_ref[...] = mine_ref[:, 3 * side + 256 :].astype(F32) + other_ref[:, 3 * side + 256 :].astype(F32)


def join_qkv(ids, mine, other, width, pos):
    r = mine.shape[0]
    shapes = [(r, 3 * width), (pos, width), (pos, width), (r, 128)]
    return call(
        join_qkv_kernel, "join_qkv", (1,), ids, (mine, other), [whole(mine.shape)] * 2,
        [whole(s) for s in shapes], [SDS(s, F32) for s in shapes], vmem=16, moved=12 * r * 4 * width,
    )


def plain_sum(g, n, place):
    left = list(range(n.bit_length() - 2, -1, -1))
    acc = g.astype(BF16).reshape((2,) * len(left) + (g.shape[0] // n, g.shape[1]))
    for bit in sorted(left):
        axis = left.index(bit)
        mine = (place >> bit) & 1
        send = lax.dynamic_index_in_dim(acc, 1 - mine, axis, keepdims=False)
        keep = lax.dynamic_index_in_dim(acc, mine, axis, keepdims=False)
        acc = (keep.astype(F32) + across(send, n, (bit, bit)).astype(F32)).astype(BF16)
        left.remove(bit)
    return acc


def plain_join(core, g):
    got = swap(g)
    sides = jnp.where(core == 0, jnp.stack([g, got], 1), jnp.stack([got, g], 1))
    return sides.reshape(g.shape[0], -1).astype(F32)


def pages(core, keep, got):
    return jnp.where(core == 0, jnp.stack([keep, got], 0), jnp.stack([got, keep], 0))


def after(value, *others):
    return lax.optimization_barrier((value, *others))[0]


def body(n, tokens, boxes, lengths, w_qkv, b_qkv, w_posk, w_posq, w_out, b_out, gain_one, shift_one,
         w_in, b_in, w_down, b_down, gain_two, shift_two, cotangent):
    place = lax.axis_index("pages").astype(jnp.int32)
    core = lax.axis_index("slab").astype(jnp.int32)
    ids = jnp.stack([place, core, lax.dynamic_index_in_dim(lengths, core, 0, keepdims=False)])
    _, half, width = tokens.shape
    other = swap(tokens)
    vectors = jnp.concatenate(
        [b_in, b_qkv, b_out, gain_one, shift_one, b_down, gain_two, shift_two]
    ).astype(F32)[None, :]
    cot_other = swap(lax.dynamic_index_in_dim(cotangent, 1 - core, 0, keepdims=False))

    pt, p, xt, kf, tab, tabt, fkt, fqt, wkt, wqt = project(
        ids, tokens, other, w_qkv, vectors, boxes, w_posk, w_posq
    )
    e, att, r = attend(ids, pt, p, w_posk, w_posq, kf, tab, tabt, fqt)
    (flt, norm, rstd, slope, actt, out_keep, out_give, dres_two, dsec, dsec_send, rows_two) = feed(
        ids, att, tokens, other, w_out, w_in, w_down, vectors, cotangent, cot_other
    )
    xt_other, att_other, flt_other, actt_other = swap(xt), swap(att), swap(flt), swap(actt)
    dsec_other = swap(dsec_send)
    out_got = swap(out_give)
    dh_send, dh, row_in = hidden_back(ids, dsec, w_down, slope)
    dh_other = swap(dh_send)
    if width // n % 16:
        dres_one, branch, branch_send, datt, rows_one = first_back(
            ids, dh_send, dh, w_in, dres_two, norm, rstd, vectors, w_out
        )
        args = dict(e=e, r=r, datt=datt, att=att, pt=pt, p=p, wkt=wkt, wqt=wqt, fkt=fkt, fqt=fqt, tabt=tabt)
        dp_send, gk_send, gq_send = attend_back(ids, own=False, **args)
        dp, gk, gq = attend_back(ids, own=True, **args)
        tok_keep, tok_give, rows_qkv = tokens_back(ids, w_qkv, dp_send, dp, dres_one)
        dp_other = swap(dp_send)

        def side_of(a):
            size = a.shape[1] // 2
            return lax.dynamic_slice_in_dim(a, core * size, size, 1)

        def total(g):
            return plain_join(core, plain_sum(g, n, place))

        both = lambda op, a, b, c, d: op(a, b) + op(c, d)
        g_down = total(both(mm, actt, side_of(dsec), actt_other, dsec_other))
        g_in = total(both(mm, flt, dh, flt_other, dh_other))
        g_out = total(both(mm, att, side_of(branch), att_other, swap(branch_send)))
        g_posk = total(gk.astype(F32) + swap(gk_send).astype(F32))
        g_posq = total(gq.astype(F32) + swap(gq_send).astype(F32))
        g_qkv = jnp.concatenate([total(both(mm_nt, xt, dp[i], xt_other, dp_other[i])) for i in range(3)], 1)
        small = (rows_qkv[0:3], rows_one[2], rows_one[0], rows_one[1], row_in, rows_two[2], rows_two[0], rows_two[1])
        packed = lax.psum(jnp.concatenate([v.reshape(n, -1) for v in small], 1), ("pages", "slab"))
        packed = lax.dynamic_index_in_dim(packed, place, 0, keepdims=False)
        totals, at = [], 0
        for v in small:
            totals.append(packed[at : at + v.size // n])
            at += v.size // n
        return (pages(core, out_keep, out_got), pages(core, tok_keep, swap(tok_give)), g_qkv, totals[0], g_posk,
                g_posq, g_out, totals[1], totals[2], totals[3], g_in, totals[4], g_down, totals[5], totals[6],
                totals[7])

    order = orders(n)
    bits = tuple(o[0] for o in order)
    down = Exchange(ids, n, *down_grad(ids, n, bits, actt, actt_other, dsec, dsec_other), order)
    dres_two = after(dres_two, down.keep)
    dres_one, branch, branch_send, datt, rows_one = first_back(
        ids, dh_send, dh, w_in, dres_two, norm, rstd, vectors, w_out
    )
    branch_other = swap(branch_send)
    mid = Exchange(
        ids, n, *mid_grad(ids, n, bits, flt, flt_other, dh, dh_other, att, att_other, branch, branch_other), order
    )
    down.step()
    datt = after(datt, mid.keep, down.keep)
    back = functools.partial(
        attend_back, ids, e=e, r=r, datt=datt, att=att, pt=pt, p=p, wkt=wkt, wqt=wqt, fkt=fkt, fqt=fqt, tabt=tabt
    )
    dp_send, gk_send, gq_send = back(own=False)
    dp_other, gk_other, gq_other = swap(dp_send), swap(gk_send), swap(gq_send)
    down.step()
    mid.step()
    ids_two = after(ids, dp_send, down.keep, mid.keep)
    dp, gk, gq = attend_back(
        ids_two, own=True, e=e, r=r, datt=datt, att=att, pt=pt, p=p, wkt=wkt, wqt=wqt, fkt=fkt, fqt=fqt, tabt=tabt
    )
    tok_keep, tok_give, rows_qkv = tokens_back(ids, w_qkv, dp_send, dp, dres_one)
    tok_got = swap(tok_give)
    small = (3 * width, width, width, width, w_in.shape[1], width, width, width)
    sizes = tuple(s // n for s in small)
    last = Exchange(
        ids, n, *qkv_grad(ids, n, bits, sizes, xt, xt_other, dp, dp_other, gk, gk_other, gq, gq_other,
                          rows_two, rows_one, row_in, rows_qkv), order
    )
    while mid.at < len(order[0]) or down.at < len(order[0]):
        for x in (down, mid):
            if x.at < len(order[0]):
                x.step()
    while last.at < len(order[0]):
        last.step()
    (g_down,) = join(ids, down.mine, down.other, (width,))
    g_in, g_out = join(ids, mid.mine, mid.other, (w_in.shape[1], width))
    g_qkv, g_posk, g_posq, summed = join_qkv(ids, last.mine, last.other, width, w_posk.shape[0] // n)
    plan, _ = small_plan(n, sizes)
    totals = [
        lax.dynamic_slice_in_dim(summed[at : at + count].reshape(-1), place * size % 128, size, 0)
        for size, count, at in plan
    ]

    return (pages(core, out_keep, out_got), pages(core, tok_keep, tok_got), g_qkv, totals[0], g_posk, g_posq, g_out,
            totals[1], totals[2], totals[3], g_in, totals[4], g_down, totals[5], totals[6], totals[7])


def solution(mesh):
    n = mesh.shape["pages"]
    rows, mat, flat = P("pages", "slab", None), P("pages", None), P("pages")
    return jax.shard_map(
        functools.partial(body, n),
        mesh=mesh,
        in_specs=(rows, P("pages", None, None), flat) + (P(),) * 14 + (rows,),
        out_specs=(rows, rows, mat, flat, mat, mat, mat, flat, flat, flat, mat, flat, mat, flat, flat, flat),
        check_vma=False,
    )
```

```python
import functools
import math

import jax
import jax.numpy as jnp
import numpy as np
from jax import lax
from jax.experimental import pallas as pl
from jax.experimental.pallas import tpu as pltpu
from jax.sharding import PartitionSpec as P

F32, BF16 = jnp.float32, jnp.bfloat16
HEADS = 12
PAIRS = HEADS // 2
BIG = 1e9
COST = 0.6e9
SDS = jax.ShapeDtypeStruct
HBM = pltpu.HBM


def mm(a, b):
    return lax.dot_general(a, b, (((1,), (0,)), ((), ())), preferred_element_type=F32)


def mm_nt(a, b):
    return lax.dot_general(a, b, (((1,), (1,)), ((), ())), preferred_element_type=F32)


def wide(ref):
    return ref[...].astype(F32).reshape(1, ref.shape[0])


def whole(shape):
    return pl.BlockSpec(shape, lambda *_: (0,) * len(shape))


def call(kernel, name, grid, ids, args, in_specs, out_specs, out_shape, scratch=(), vmem=17, us=1.0):
    return pl.pallas_call(
        kernel,
        grid_spec=pltpu.PrefetchScalarGridSpec(
            num_scalar_prefetch=1, grid=grid, in_specs=in_specs, out_specs=out_specs, scratch_shapes=list(scratch)
        ),
        out_shape=out_shape,
        compiler_params=pltpu.CompilerParams(vmem_limit_bytes=vmem << 20),
        cost_estimate=pl.CostEstimate(flops=int(us * COST), bytes_accessed=0, transcendentals=0),
        name=name,
    )(ids, *args)


def sin_cos(angle):
    turns = jnp.round(angle * (2.0 / math.pi))
    r = angle - turns * 1.5703125
    r = r - turns * 4.837512969970703125e-4
    r = r - turns * 7.54978995489188216e-8
    z = r * r
    s = ((-1.9515295891e-4 * z + 8.3321608736e-3) * z - 1.6666654611e-1) * z * r + r
    c = (
        (2.443315711809948e-5 * z - 1.388731625493765e-3) * z + 4.166664568298827e-2
    ) * z * z + (1.0 - 0.5 * z)
    q = turns.astype(jnp.int32)
    odd = (q & 1) == 1
    one, two = jnp.where(odd, c, s), jnp.where(odd, s, c)
    sine = jnp.where((q & 2) == 2, -one, one)
    cosine = jnp.where(((q + 1) & 2) == 2, -two, two)
    return sine, cosine


def tables_kernel(ids, box_ref, rrow_ref, rcol_ref, wk_ref, wq_ref,
                  kf_ref, tab_ref, tabt_ref, fkt_ref, fqt_ref, wkt_ref, wqt_ref):
    half = kf_ref.shape[0] // 2
    wkt_ref[...] = wk_ref[...].T
    wqt_ref[...] = wq_ref[...].T
    box = box_ref[0].astype(F32)
    centre = (box[0:2, :] + box[2:4, :]) * 0.5
    turned = jnp.concatenate([centre[:, half:], centre[:, :half]], 1)
    centre = jnp.where(ids[1] == 0, centre, turned)
    column = jnp.concatenate([centre, jnp.zeros((6, 2 * half), F32)], 0).T
    front = lax.broadcasted_iota(jnp.int32, (2 * half, 128), 1) < 64
    for axis in range(2):
        s, c = sin_cos(column[:, axis : axis + 1] * rrow_ref[...])
        kf_ref[:, axis * 128 : axis * 128 + 128] = jnp.where(front, c, s).astype(BF16)
        tab_ref[axis] = c
        tab_ref[2 + axis] = jnp.where(front, s, -s)
        st, ct = sin_cos(rcol_ref[...] * centre[axis : axis + 1, :])
        tabt_ref[2 * axis] = st
        tabt_ref[2 * axis + 1] = ct
        sl, cl = st.astype(BF16), ct.astype(BF16)
        at = 128 * axis
        fkt_ref[at : at + 64, :] = cl
        fkt_ref[at + 64 : at + 128, :] = sl
        fqt_ref[at : at + 64, :] = sl * 0.125
        fqt_ref[at + 64 : at + 128, :] = cl * 0.125


def tables(ids, boxes, wk, wq):
    rows = boxes.shape[2]
    width = wk.shape[1]
    rates = np.exp(np.arange(64) * (-math.log(10000.0) / 64)).astype(np.float32)
    shapes = [((rows, 256), BF16), ((4, rows, 128), F32), ((4, 64, rows), F32), ((256, rows), BF16), ((256, rows), BF16),
              ((width, 256), BF16), ((width, 256), BF16)]
    return call(
        tables_kernel, "tables", (1,), ids, (boxes, np.tile(rates, 2)[None, :], rates[:, None], wk, wq),
        [
            pl.BlockSpec((1, 4, rows), lambda i, ids: (ids[1], 0, 0)),
            whole((1, 128)), whole((64, 1)), whole((256, width)), whole((256, width)),
        ],
        [whole(s) for s, _ in shapes], [SDS(s, t) for s, t in shapes], us=3,
    )


def project_kernel(ids, own_ref, other_ref, w_ref, b_ref, pt_ref, p_ref, xt_ref, x, bias):
    step = pl.program_id(0)

    @pl.when(step == 0)
    def _():
        half = own_ref.shape[1]
        x[:half, :] = own_ref[0]
        x[half:, :] = other_ref[0]
        bias[...] = wide(b_ref)
        xt_ref[...] = x[...].T

    block = w_ref.shape[1]
    shift = bias[:, pl.ds(pl.multiple_of(step * block, 128), block)]
    p = (mm(x[...], w_ref[...]) + shift).astype(BF16)
    p_ref[...] = p
    pt_ref[...] = p.T


def page_specs(half, width):
    spec = pl.BlockSpec((1, half, width), lambda i, ids: (ids[1], 0, 0))
    return spec, spec


def project(ids, tokens, other, w, b):
    _, half, width = tokens.shape
    rows = 2 * half
    cols = w.shape[1]
    block = 768
    return call(
        project_kernel, "project", (cols // block,), ids, (tokens, other, w, b),
        [*page_specs(half, width), pl.BlockSpec((width, block), lambda i, ids: (0, i)), whole((cols,))],
        [
            pl.BlockSpec((block, rows), lambda i, ids: (i, 0)), pl.BlockSpec((rows, block), lambda i, ids: (0, i)),
            whole((width, rows)),
        ],
        [SDS((cols, rows), BF16), SDS((rows, cols), BF16), SDS((width, rows), BF16)],
        [pltpu.VMEM((rows, width), BF16), pltpu.VMEM((1, cols), F32)],
        us=5,
    )


def attend_kernel(ids, len_ref, qt_ref, vt_ref, k_ref, wk_ref, wq_ref, kf_ref, tab_ref, tabt_ref, fqt_ref,
                  e_ref, at_ref, r_ref, fk, fq):
    rows = k_ref.shape[0]

    @pl.when(pl.program_id(0) == 0)
    def _():
        lane = lax.broadcasted_iota(jnp.int32, (rows, 128), 1)
        at = lax.broadcasted_iota(jnp.int32, (rows, 128), 0)
        turned = jnp.where(at < rows // 2, at + rows // 2, at - rows // 2)
        at = jnp.where(ids[1] == 0, at, turned)
        fk[:, 0:256] = kf_ref[...]
        fk[:, 640:768] = jnp.where((lane == 0) & (at >= len_ref[ids[1]]), -BIG, 0.0).astype(BF16)
        fq[256:512, :] = fqt_ref[...]
        sub = lax.broadcasted_iota(jnp.int32, (128, rows), 0)
        fq[640:768, :] = jnp.where(sub == 0, 1.0, 0.0).astype(BF16)

    fk[:, 512:640] = k_ref[...]
    lane = lax.broadcasted_iota(jnp.int32, (256, 128), 1)
    for h in range(2):
        mine = (lane < 64) if h == 0 else (lane >= 64)
        qt = qt_ref[h * 64 : h * 64 + 64, :]
        zero = jnp.zeros_like(qt)
        pad = jnp.concatenate([qt, zero] if h == 0 else [zero, qt], 0)
        fq[512:640, :] = pad * 0.125
        a = mm(wk_ref[...], pad)
        sx, cx, sy, cy = (tabt_ref[i] * 0.125 for i in range(4))
        axs, axc, ays, ayc = (a[i * 64 : i * 64 + 64, :] for i in range(4))
        fq[0:64, :] = (axs * sx + axc * cx).astype(BF16)
        fq[64:128, :] = (axc * sx - axs * cx).astype(BF16)
        fq[128:192, :] = (ays * sy + ayc * cy).astype(BF16)
        fq[192:256, :] = (ayc * sy - ays * cy).astype(BF16)
        w = jnp.where(mine, wq_ref[...], 0).astype(BF16)
        b = mm_nt(k_ref[...], w)
        for axis in range(2):
            part = b[:, axis * 128 : axis * 128 + 128]
            turned = pltpu.roll(part, 64, 1)
            fk[:, 256 + axis * 128 : 384 + axis * 128] = (
                part * tab_ref[axis] + turned * tab_ref[2 + axis]
            ).astype(BF16)
        s = mm(fk[...], fq[...])
        e = jnp.exp(s - jnp.max(s, 0, keepdims=True))
        r = 1.0 / jnp.sum(e, 0, keepdims=True)
        low = e.astype(BF16)
        e_ref[h] = low
        at_ref[h * 64 : h * 64 + 64, :] = (mm(vt_ref[h * 64 : h * 64 + 64, :], low) * r).astype(BF16)
        r_ref[0, h : h + 1, :] = r


def attend(ids, lengths, pt, p, w_posk, w_posq, kf, tab, tabt, fqt):
    rows = p.shape[0]
    width = pt.shape[0] // 3
    return call(
        attend_kernel, "attend", (PAIRS,), ids, (lengths, pt, pt, p, w_posk, w_posq, kf, tab, tabt, fqt),
        [
            pl.BlockSpec(memory_space=pltpu.SMEM),
            pl.BlockSpec((128, rows), lambda i, ids: (i, 0)),
            pl.BlockSpec((128, rows), lambda i, ids: (2 * PAIRS + i, 0)),
            pl.BlockSpec((rows, 128), lambda i, ids: (0, PAIRS + i)),
            pl.BlockSpec((256, 128), lambda i, ids: (0, i)),
            pl.BlockSpec((256, 128), lambda i, ids: (0, i)),
            whole((rows, 256)), whole((4, rows, 128)), whole((4, 64, rows)), whole((256, rows)),
        ],
        [
            pl.BlockSpec((2, rows, rows), lambda i, ids: (i, 0, 0)),
            pl.BlockSpec((128, rows), lambda i, ids: (i, 0)),
            pl.BlockSpec((1, 2, rows), lambda i, ids: (i, 0, 0)),
        ],
        [HBM((HEADS, rows, rows), BF16), SDS((width, rows), BF16), SDS((PAIRS, 2, rows), F32)],
        [pltpu.VMEM((rows, 768), BF16), pltpu.VMEM((768, rows), BF16)],
        us=17,
    )


def feed_kernel(ids, at_ref, own_ref, other_ref, wo_ref, bo_ref, g1_ref, s1_ref, wi_ref, bi_ref, wd_ref, bd_ref,
                g2_ref, s2_ref, cown_ref, cother_ref,
                flt_ref, norm_ref, rstd_ref, slope_ref, actt_ref, keep_ref, give_ref, dres_ref, dsec_ref, send_ref,
                rows_ref, first, low, second, cot):
    step = pl.program_id(0)
    half = own_ref.shape[1]

    @pl.when(step == 0)
    def _():
        first[:half, :] = own_ref[0].astype(F32)
        first[half:, :] = other_ref[0].astype(F32)
        cot[:half, :] = cown_ref[0]
        cot[half:, :] = cother_ref[0]
        v = first[...] + (mm(at_ref[...].T, wo_ref[...]) + wide(bo_ref))
        c = v - jnp.mean(v, -1, keepdims=True)
        rstd = lax.rsqrt(jnp.mean(c * c, -1, keepdims=True) + 1e-6)
        normed = c * rstd
        norm_ref[...] = normed
        rstd_ref[...] = rstd
        f = normed * wide(g1_ref) + wide(s1_ref)
        first[...] = f + wide(bd_ref)
        l = f.astype(BF16)
        low[...] = l
        flt_ref[...] = l.T

    h = mm(low[...], wi_ref[...]) + wide(bi_ref)
    cdf = 0.5 * lax.erf(h * (0.5 ** 0.5)) + 0.5
    active = (h * cdf).astype(BF16)
    slope_ref[...] = (cdf + h * (jnp.exp(-0.5 * h * h) * ((2.0 * math.pi) ** -0.5))).astype(BF16)
    actt_ref[...] = active.T
    part = mm(active, wd_ref[...])

    @pl.when(step == 0)
    def _():
        second[...] = part

    @pl.when(step > 0)
    def _():
        second[...] += part

    @pl.when(step == pl.num_programs(0) - 1)
    def _():
        v = first[...] + second[...]
        c = v - jnp.mean(v, -1, keepdims=True)
        rstd = lax.rsqrt(jnp.mean(c * c, -1, keepdims=True) + 1e-6)
        normed = c * rstd
        out = (normed * wide(g2_ref) + wide(s2_ref)).astype(BF16)
        keep_ref[0] = out[:half, :]
        give_ref[...] = out[half:, :]
        g = cot[...].astype(F32)
        gg = g * wide(g2_ref)
        d = rstd * (
            gg - jnp.mean(gg, -1, keepdims=True) - normed * jnp.mean(gg * normed, -1, keepdims=True)
        )
        dres_ref[...] = d
        l = d.astype(BF16)
        dsec_ref[...] = l
        side = send_ref.shape[1]
        send_ref[...] = dsec_ref[:, pl.ds(pl.multiple_of((1 - ids[1]) * side, 128), side)]
        rows_ref[0:1, :] = jnp.sum(g * normed, 0, keepdims=True)
        rows_ref[1:2, :] = jnp.sum(g, 0, keepdims=True)
        rows_ref[2:3, :] = jnp.sum(l.astype(F32), 0, keepdims=True)
        rows_ref[3:8, :] = jnp.zeros((5, rows_ref.shape[1]), F32)


def vec(size):
    return pl.BlockSpec((size,), lambda i, ids: (0,))


def feed(ids, att, tokens, other, w_out, w_in, w_down, b_out, g1, s1, b_in, b_down, g2, s2, cot, cot_other):
    _, half, width = tokens.shape
    rows = 2 * half
    ff = w_in.shape[1]
    block = 512
    mat = whole((rows, width))
    return call(
        feed_kernel, "feed", (ff // block,), ids,
        (att, tokens, other, w_out, b_out, g1, s1, w_in, b_in, w_down, b_down, g2, s2, cot, cot_other),
        [
            whole((width, rows)), *page_specs(half, width), whole((width, width)), vec(width), vec(width), vec(width),
            pl.BlockSpec((width, block), lambda i, ids: (0, i)),
            pl.BlockSpec((block,), lambda i, ids: (i,)),
            pl.BlockSpec((block, width), lambda i, ids: (i, 0)),
            vec(width), vec(width), vec(width), *page_specs(half, width),
        ],
        [
            whole((width, rows)), mat, whole((rows, 1)),
            pl.BlockSpec((rows, block), lambda i, ids: (0, i)),
            pl.BlockSpec((block, rows), lambda i, ids: (i, 0)),
            page_specs(half, width)[0], whole((half, width)), mat, mat, whole((rows, width // 2)), whole((8, width)),
        ],
        [
            SDS((width, rows), BF16), SDS((rows, width), F32), SDS((rows, 1), F32),
            SDS((rows, ff), BF16), SDS((ff, rows), BF16),
            SDS((2, half, width), BF16), SDS((half, width), BF16), SDS((rows, width), F32), SDS((rows, width), BF16),
            SDS((rows, width // 2), BF16), SDS((8, width), F32),
        ],
        [pltpu.VMEM((rows, width), F32), pltpu.VMEM((rows, width), BF16), pltpu.VMEM((rows, width), F32),
         pltpu.VMEM((rows, width), BF16)],
        us=15,
    )


def hidden_kernel(ids, ds_ref, wd_ref, slope_ref, send_ref, own_ref, rows_ref):
    step = pl.program_id(0)
    d = mm_nt(ds_ref[...], wd_ref[...]).astype(BF16).astype(F32)
    dh = (d * slope_ref[...].astype(F32)).astype(BF16)
    rows_ref[...] = jnp.sum(dh.astype(F32), 0, keepdims=True)
    sends = pl.num_programs(0) // 2

    @pl.when(step < sends)
    def _():
        send_ref[...] = dh

    @pl.when(step >= sends)
    def _():
        own_ref[...] = dh


def hidden_back(ids, dsec, w_down, slope):
    rows, width = dsec.shape
    ff = w_down.shape[0]
    block = 768
    steps = ff // block
    s = steps // 2
    at = lambda i, ids: jnp.where(ids[1] == 0, (i + s) % steps, i)
    return call(
        hidden_kernel, "hidden_back", (steps,), ids, (dsec, w_down, slope),
        [
            whole((rows, width)),
            pl.BlockSpec((block, width), lambda i, ids: (at(i, ids), 0)),
            pl.BlockSpec((rows, block), lambda i, ids: (0, at(i, ids))),
        ],
        [
            pl.BlockSpec((rows, block), lambda i, ids: (0, jnp.minimum(i, s - 1))),
            pl.BlockSpec((rows, block), lambda i, ids: (0, jnp.maximum(i - s, 0))),
            pl.BlockSpec((1, block), lambda i, ids: (0, at(i, ids))),
        ],
        [SDS((rows, ff // 2), BF16), SDS((rows, ff // 2), BF16), SDS((1, ff), F32)],
        us=5,
    )


def first_kernel(ids, dsend_ref, down_ref, wsend_ref, wown_ref, dres_ref, norm_ref, rstd_ref, g1_ref, wo_ref,
                 res_ref, branch_ref, send_ref, datt_ref, rows_ref, acc):
    step = pl.program_id(0)
    part = mm_nt(dsend_ref[...], wsend_ref[...]) + mm_nt(down_ref[...], wown_ref[...])

    @pl.when(step == 0)
    def _():
        acc[...] = part

    @pl.when(step > 0)
    def _():
        acc[...] += part

    @pl.when(step == pl.num_programs(0) - 1)
    def _():
        g = dres_ref[...] + acc[...].astype(BF16).astype(F32)
        normed = norm_ref[...]
        gg = g * wide(g1_ref)
        d = rstd_ref[...] * (
            gg - jnp.mean(gg, -1, keepdims=True) - normed * jnp.mean(gg * normed, -1, keepdims=True)
        )
        res_ref[...] = d
        l = d.astype(BF16)
        branch_ref[...] = l
        side = send_ref.shape[1]
        send_ref[...] = branch_ref[:, pl.ds(pl.multiple_of((1 - ids[1]) * side, 128), side)]
        datt_ref[...] = mm_nt(wo_ref[...], l).astype(BF16)
        rows_ref[0:1, :] = jnp.sum(g * normed, 0, keepdims=True)
        rows_ref[1:2, :] = jnp.sum(g, 0, keepdims=True)
        rows_ref[2:3, :] = jnp.sum(l.astype(F32), 0, keepdims=True)
        rows_ref[3:8, :] = jnp.zeros((5, rows_ref.shape[1]), F32)


def first_back(ids, dsend, down, w_in, dres, norm, rstd, g1, w_out):
    rows, width = dres.shape
    ff = w_in.shape[1]
    block = 512
    s = ff // block // 2
    mat = whole((rows, width))
    return call(
        first_kernel, "first_back", (s,), ids, (dsend, down, w_in, w_in, dres, norm, rstd, g1, w_out),
        [
            pl.BlockSpec((rows, block), lambda i, ids: (0, i)),
            pl.BlockSpec((rows, block), lambda i, ids: (0, i)),
            pl.BlockSpec((width, block), lambda i, ids: (0, (1 - ids[1]) * s + i)),
            pl.BlockSpec((width, block), lambda i, ids: (0, ids[1] * s + i)),
            mat, mat, whole((rows, 1)), vec(width), whole((width, width)),
        ],
        [mat, mat, whole((rows, width // 2)), whole((width, rows)), whole((8, width))],
        [
            SDS((rows, width), F32), SDS((rows, width), BF16), SDS((rows, width // 2), BF16), SDS((width, rows), BF16),
            SDS((8, width), F32),
        ],
        [pltpu.VMEM((rows, width), F32)],
        us=8,
    )


def attend_back_kernel(ids, e_ref, r_ref, da_ref, at_ref, qt_ref, kt_ref, v_ref, wkt_ref, wqt_ref, fkt_ref, fqt_ref,
                       tabt_ref, dp_ref, gk_ref, gq_ref, rows_ref, left_k, left_q):
    @pl.when(pl.program_id(0) == 0)
    def _():
        left_k[64:320, :] = fkt_ref[...]
        left_q[64:320, :] = fqt_ref[...]

    sx, cx, sy, cy = (tabt_ref[i] for i in range(4))
    lane = lax.broadcasted_iota(jnp.int32, (256, 128), 1)
    gk, gq = [], []
    for h in range(2):
        own = slice(h * 64, h * 64 + 64)
        da = da_ref[own, :].astype(F32) * r_ref[0, h : h + 1, :]
        delta = jnp.sum(da * at_ref[own, :].astype(F32), 0, keepdims=True)
        da = da.astype(BF16)
        zero = jnp.zeros_like(da)
        pad = jnp.concatenate([da, zero] if h == 0 else [zero, da], 0)
        e = e_ref[h]
        ds = (e.astype(F32) * (mm(v_ref[...], pad) - delta)).astype(BF16)
        left_k[0:64, :] = kt_ref[own, :]
        left_q[0:64, :] = qt_ref[own, :] * 0.125
        one = mm(left_k[...], ds) * 0.125
        two = mm_nt(left_q[...], ds)
        dv = mm_nt(da, e)
        ux1, ux2, uy1, uy2 = (one[64 + i * 64 : 128 + i * 64, :].astype(BF16).astype(F32) for i in range(4))
        d_a = jnp.concatenate(
            [ux1 * sx - ux2 * cx, ux1 * cx + ux2 * sx, uy1 * sy - uy2 * cy, uy1 * cy + uy2 * sy], 0
        ).astype(BF16)
        zx1, zx2, zy1, zy2 = (two[64 + i * 64 : 128 + i * 64, :] for i in range(4))
        d_b = jnp.concatenate(
            [zx1 * cx - zx2 * sx, zx1 * sx + zx2 * cx, zy1 * cy - zy2 * sy, zy1 * sy + zy2 * cy], 0
        ).astype(BF16)
        dp_ref[0, own, :] = (one[0:64, :] + mm(wkt_ref[own, :], d_a)).astype(BF16)
        dp_ref[1, own, :] = (two[0:64, :] + mm(wqt_ref[own, :], d_b)).astype(BF16)
        dp_ref[2, own, :] = dv.astype(BF16)
        gk.append(mm_nt(d_a, qt_ref[...]))
        gq.append(mm_nt(d_b, kt_ref[...]))
    gk_ref[...] = jnp.where(lane < 64, gk[0], gk[1]).astype(BF16)
    gq_ref[...] = jnp.where(lane < 64, gq[0], gq[1]).astype(BF16)
    ones = jnp.ones((8, dp_ref.shape[2]), BF16)
    for i in range(3):
        rows_ref[8 * i : 8 * i + 8, :] = mm_nt(ones, dp_ref[i])


def attend_back(ids, own, e, r, datt, att, pt, p, wkt, wqt, fkt, fqt, tabt):
    rows = p.shape[0]
    pairs = PAIRS // 2
    lo = lambda ids: (ids[1] if own else 1 - ids[1]) * pairs
    pair = lambda base: pl.BlockSpec((128, rows), lambda i, ids: (base + lo(ids) + i, 0))
    wt = pl.BlockSpec((128, 256), lambda i, ids: (lo(ids) + i, 0))
    return call(
        attend_back_kernel, "attend_back", (pairs,), ids, (e, r, datt, att, pt, pt, p, wkt, wqt, fkt, fqt, tabt),
        [
            pl.BlockSpec((2, rows, rows), lambda i, ids: (lo(ids) + i, 0, 0)),
            pl.BlockSpec((1, 2, rows), lambda i, ids: (lo(ids) + i, 0, 0)),
            pair(0), pair(0), pair(0), pair(PAIRS),
            pl.BlockSpec((rows, 128), lambda i, ids: (0, 2 * PAIRS + lo(ids) + i)),
            wt, wt, whole((256, rows)), whole((256, rows)), whole((4, 64, rows)),
        ],
        [
            pl.BlockSpec((3, 128, rows), lambda i, ids: (0, i, 0)),
            pl.BlockSpec((256, 128), lambda i, ids: (0, i)),
            pl.BlockSpec((256, 128), lambda i, ids: (0, i)),
            pl.BlockSpec((24, 128), lambda i, ids: (0, i)),
        ],
        [
            SDS((3, 128 * pairs, rows), BF16), SDS((256, 128 * pairs), BF16), SDS((256, 128 * pairs), BF16),
            SDS((24, 128 * pairs), F32),
        ],
        [pltpu.VMEM((320, rows), BF16), pltpu.VMEM((320, rows), BF16)],
        us=9,
    )


def tokens_kernel(ids, w_ref, ds_ref, do_ref, dres_ref, keep_ref, give_ref):
    width = w_ref.shape[1] // 3
    side = width // 2
    half = keep_ref.shape[1]
    acc = None
    for h, ref in ((1 - ids[1], ds_ref), (ids[1], do_ref)):
        for s in range(3):
            at = pl.multiple_of(s * width + h * side, 128)
            part = mm(w_ref[:, pl.ds(at, side)], ref[s])
            acc = part if acc is None else acc + part
    out = (dres_ref[...] + acc.T).astype(BF16)
    keep_ref[0] = out[:half, :]
    give_ref[...] = out[half:, :]


def tokens_back(ids, w_qkv, dsend, down, dres):
    rows, width = dres.shape
    cols = w_qkv.shape[1]
    block = 256
    half = rows // 2
    blk = pl.BlockSpec((half, block), lambda i, ids: (0, i))
    return call(
        tokens_kernel, "tokens_back", (width // block,), ids, (w_qkv, dsend, down, dres),
        [
            pl.BlockSpec((block, cols), lambda i, ids: (i, 0)), whole(dsend.shape), whole(down.shape),
            pl.BlockSpec((rows, block), lambda i, ids: (0, i)),
        ],
        [pl.BlockSpec((1, half, block), lambda i, ids: (ids[1], 0, i)), blk],
        [SDS((2, half, width), BF16), SDS((half, width), BF16)],
        us=6,
    )


def chosen(core, pair):
    return jnp.where(core == 0, pair[0], pair[1])


def drop_bit(p, bit):
    return ((p >> (bit + 1)) << bit) | (p & ((1 << bit) - 1))


def put(ids, bits, p, lanes, value, send_ref, keep_ref):
    bit = chosen(ids[1], bits)
    here = ((p >> bit) & 1) == ((ids[0] >> bit) & 1)
    at = drop_bit(p, bit)

    @pl.when(here)
    def _():
        keep_ref[at, 0 : value.shape[0], lanes] = value

    @pl.when(jnp.logical_not(here))
    def _():
        send_ref[at, 0 : value.shape[0], lanes] = value


def down_kernel(n, bits, ids, a0_ref, a1_ref, b0_ref, b1_ref, send_ref, keep_ref):
    places = n // pl.num_programs(0)
    r, w = keep_ref.shape[1:]
    acc = mm(a0_ref[...], b0_ref[...]) + mm(a1_ref[...], b1_ref[...])
    for k in range(places):
        p = pl.program_id(0) * places + k
        put(ids, bits, p, slice(0, w), acc[k * r : k * r + r, :].astype(BF16), send_ref, keep_ref)


def down_grad(ids, n, bits, actt, actt_other, dsec, dsec_other):
    ff, rows = actt.shape
    side = dsec_other.shape[1]
    block = ff // 4
    part = (n // 2, ff // n, side)
    a = pl.BlockSpec((block, rows), lambda i, ids: (i, 0))
    return call(
        functools.partial(down_kernel, n, bits), "down_grad", (4,), ids, (actt, actt_other, dsec, dsec_other),
        [a, a, pl.BlockSpec((rows, side), lambda i, ids: (0, ids[1])), whole((rows, side))],
        [whole(part)] * 2, [SDS(part, BF16)] * 2,
        us=7,
    )


def mid_kernel(n, bits, ids, f0_ref, f1_ref, h0_ref, h1_ref, a0_ref, a1_ref, c0_ref, c1_ref, send_ref, keep_ref):
    step = pl.program_id(0)
    last = pl.num_programs(0) - 1
    r = keep_ref.shape[1]
    w = h0_ref.shape[1]

    @pl.when(step < last)
    def _():
        acc = mm(f0_ref[...], h0_ref[...]) + mm(f1_ref[...], h1_ref[...])
        lanes = pl.ds(pl.multiple_of(step * w, 128), w)
        for p in range(n):
            put(ids, bits, p, lanes, acc[p * r : p * r + r, :].astype(BF16), send_ref, keep_ref)

    @pl.when(step == last)
    def _():
        acc = mm(a0_ref[...], c0_ref[...]) + mm(a1_ref[...], c1_ref[...])
        lanes = slice(keep_ref.shape[2] - acc.shape[1], keep_ref.shape[2])
        for p in range(n):
            put(ids, bits, p, lanes, acc[p * r : p * r + r, :].astype(BF16), send_ref, keep_ref)


def mid_grad(ids, n, bits, flt, flt_other, dh, dh_other, att, att_other, branch, branch_other):
    width, rows = flt.shape
    ffs = dh.shape[1]
    side = branch_other.shape[1]
    block = 768
    steps = ffs // block
    part = (n // 2, width // n, ffs + side)
    b = pl.BlockSpec((rows, block), lambda i, ids: (0, jnp.minimum(i, steps - 1)))
    a = whole((width, rows))
    return call(
        functools.partial(mid_kernel, n, bits), "mid_grad", (steps + 1,), ids,
        (flt, flt_other, dh, dh_other, att, att_other, branch, branch_other),
        [a, a, b, b, a, a, pl.BlockSpec((rows, side), lambda i, ids: (0, ids[1])), whole((rows, side))],
        [whole(part)] * 2, [SDS(part, BF16)] * 2, us=6,
    )


def chunks(n, size):
    return max(((p + 1) * size - 1) // 128 - p * size // 128 + 1 for p in range(n))


def small_plan(n, sizes):
    plan, at = [], 0
    for size in sizes:
        plan.append((size, chunks(n, size), at))
        at += chunks(n, size)
    return plan, at


def qk_kernel(n, bits, sizes, ids, x0_ref, x1_ref, d0_ref, d1_ref, two_ref, one_ref, in_ref, rs_ref, ro_ref,
              send_ref, keep_ref, qkv_ref):
    r = keep_ref.shape[1]
    side = d0_ref.shape[1]
    for who, ref in ((1 - ids[1], rs_ref), (ids[1], ro_ref)):
        for i in range(3):
            at = pl.multiple_of(who * side, 128)
            qkv_ref[i : i + 1, pl.ds(at, side)] = ref[8 * i : 8 * i + 1, :]
    for i in range(2):
        acc = mm_nt(x0_ref[...], d0_ref[i]) + mm_nt(x1_ref[...], d1_ref[i])
        for p in range(n):
            put(ids, bits, p, slice(i * side, i * side + side), acc[p * r : p * r + r, :].astype(BF16), send_ref, keep_ref)
    vectors = (qkv_ref, one_ref, one_ref, one_ref, in_ref, two_ref, two_ref, two_ref)
    index = (None, 2, 0, 1, 0, 2, 0, 1)
    plan, _ = small_plan(n, sizes)
    for p in range(n):
        found = []
        for (size, count, _), ref, row in zip(plan, vectors, index):
            for c in range(count):
                at = min(p * size // 128 + c, n * size // 128 - 1)
                if row is None:
                    i, at = at * 128 // ref.shape[1], at * 128 % ref.shape[1]
                    found.append(ref[i : i + 1, at : at + 128])
                else:
                    found.append(ref[row : row + 1, at * 128 : at * 128 + 128])
        found = jnp.concatenate(found + [jnp.zeros((r - len(found), 128), F32)], 0).astype(BF16)
        put(ids, bits, p, slice(2 * side, 2 * side + 128), found, send_ref, keep_ref)


def qk_grad(ids, n, bits, sizes, xt, xt_other, dp, dp_other, two, one, into, rows_send, rows_own):
    width, rows = xt.shape
    side = dp.shape[1]
    part = (n // 2, width // n, 2 * side + 128)
    d = pl.BlockSpec((2, side, rows), lambda i, ids: (0, 0, 0))
    return call(
        functools.partial(qk_kernel, n, bits, sizes), "qk_grad", (1,), ids,
        (xt, xt_other, dp, dp_other, two, one, into, rows_send, rows_own),
        [whole(xt.shape)] * 2 + [d, d] + [whole(a.shape) for a in (two, one, into, rows_send, rows_own)],
        [whole(part)] * 2, [SDS(part, BF16)] * 2, [pltpu.VMEM((8, width), F32)],
        us=4,
    )


def vp_kernel(n, bits, ids, x0_ref, x1_ref, d0_ref, d1_ref, k0_ref, k1_ref, q0_ref, q1_ref, send_ref, keep_ref):
    r = keep_ref.shape[1]
    side = d0_ref.shape[1]
    acc = mm_nt(x0_ref[...], d0_ref[0]) + mm_nt(x1_ref[...], d1_ref[0])
    for p in range(n):
        put(ids, bits, p, slice(0, side), acc[p * r : p * r + r, :].astype(BF16), send_ref, keep_ref)
    base = side
    for own_ref, other_ref in ((k0_ref, k1_ref), (q0_ref, q1_ref)):
        acc = (own_ref[...].astype(F32) + other_ref[...].astype(F32)).astype(BF16)
        s = acc.shape[0] // n
        for p in range(n):
            rows = acc[p * s : p * s + s, :]
            stacked = jnp.concatenate([rows[:, 128 * i : 128 * i + 128] for i in range(side // 128)], 0)
            put(ids, bits, p, slice(base, base + 128), stacked, send_ref, keep_ref)
        base += 128


def vp_grad(ids, n, bits, xt, xt_other, dp, dp_other, gk, gk_other, gq, gq_other):
    width, rows = xt.shape
    side = dp.shape[1]
    part = (n // 2, width // n, side + 256)
    d = pl.BlockSpec((1, side, rows), lambda i, ids: (2, 0, 0))
    return call(
        functools.partial(vp_kernel, n, bits), "vp_grad", (1,), ids,
        (xt, xt_other, dp, dp_other, gk, gk_other, gq, gq_other),
        [whole(xt.shape)] * 2 + [d, d] + [whole(a.shape) for a in (gk, gk, gq, gq)],
        [whole(part)] * 2, [SDS(part, BF16)] * 2, us=3,
    )


def add_split_kernel(bits, lows, ids, keep_ref, got_ref, send_ref, next_ref):
    low = chosen(ids[1], lows)
    mine = (ids[0] >> chosen(ids[1], bits)) & 1

    @pl.loop(0, next_ref.shape[0])
    def _(q):
        base = ((q >> low) << (low + 1)) | (q & ((1 << low) - 1))
        for which, ref in ((1 - mine, send_ref), (mine, next_ref)):
            p = base + (which << low)
            ref[q] = (keep_ref[p].astype(F32) + got_ref[p].astype(F32)).astype(BF16)


def add_split(ids, keep, got, bits, lows):
    m, r, w = keep.shape
    part = (m // 2, r, w)
    return call(
        functools.partial(add_split_kernel, bits, lows), "add_split", (1,), ids, (keep, got),
        [whole(keep.shape)] * 2, [whole(part)] * 2, [SDS(part, BF16)] * 2, vmem=24, us=1,
    )


def add_last_kernel(ids, keep_ref, got_ref, out_ref):
    out_ref[...] = (keep_ref[0].astype(F32) + got_ref[0].astype(F32)).astype(BF16)


def add_last(ids, keep, got):
    _, r, w = keep.shape
    return call(
        add_last_kernel, "add_last", (1,), ids, (keep, got), [whole(keep.shape)] * 2, whole((r, w)), SDS((r, w), BF16),
        vmem=16, us=1,
    )


def swap(x):
    return lax.ppermute(x, "slab", [(0, 1), (1, 0)])


def across(x, n, bits):
    pairs = [(2 * p + c, 2 * (p ^ (1 << bits[c])) + c) for p in range(n) for c in range(2)]
    return lax.ppermute(x, ("pages", "slab"), pairs)


def orders(n):
    low = list(range(n.bit_length() - 1))
    if len(low) != 4:
        pair = (low, low[1::-1] + low[:1:-1])
        return pair, pair, pair, pair
    return ORDERS


ORDERS = (((0, 1, 2, 3), (1, 0, 3, 2)),) * 4


class Exchange:
    def __init__(self, ids, n, send, keep, order):
        self.ids, self.n, self.order = ids, n, order
        self.left = [sorted(o) for o in order]
        self.at = 0
        self.steps = len(order[0])
        self.keep = keep
        self.got = across(send, n, self.bits(0))

    @staticmethod
    def first(order):
        return tuple(o[0] for o in order)

    def bits(self, step):
        return tuple(o[step] for o in self.order)

    def step(self):
        for l, b in zip(self.left, self.bits(self.at)):
            l.remove(b)
        self.at += 1
        if self.at == self.steps:
            self.mine = add_last(self.ids, self.keep, self.got)
            self.other = swap(self.mine)
            return
        bits = self.bits(self.at)
        lows = tuple(l.index(b) for l, b in zip(self.left, bits))
        send, self.keep = add_split(self.ids, self.keep, self.got, bits, lows)
        self.got = across(send, self.n, bits)


def join_kernel(ids, mine_ref, other_ref, *outs):
    core = ids[1]
    at = 0
    for out in outs:
        side = out.shape[1] // 2
        for who, ref in ((core, mine_ref), (1 - core, other_ref)):
            out[:, pl.ds(pl.multiple_of(who * side, 128), side)] = ref[:, at : at + side].astype(F32)
        at += side


def join(ids, mine, other, widths):
    r = mine.shape[0]
    return call(
        join_kernel, "join", (1,), ids, (mine, other), [whole(mine.shape)] * 2,
        [whole((r, w)) for w in widths], [SDS((r, w), F32) for w in widths], vmem=16, us=2,
    )


def join_last_kernel(n, sizes, ids, qk_mine, qk_other, vo_mine, vo_other, qkv_ref, posk_ref, posq_ref, *vectors):
    core = ids[1]
    r, width = qkv_ref.shape[0], qkv_ref.shape[1] // 3
    side = width // 2
    s = posk_ref.shape[0]

    def lay(out, base, who, ref, at):
        out[:, pl.ds(pl.multiple_of(base + who * side, 128), side)] = ref[:, at : at + side].astype(F32)

    for who, qk, vo in ((core, qk_mine, vo_mine), (1 - core, qk_other, vo_other)):
        lay(qkv_ref, 0, who, qk, 0)
        lay(qkv_ref, width, who, qk, side)
        lay(qkv_ref, 2 * width, who, vo, 0)
        for j, out in enumerate((posk_ref, posq_ref)):
            lanes = slice(side + 128 * j, side + 128 * j + 128)
            for i in range(r // s):
                at = pl.multiple_of(who * side + 128 * i, 128)
                out[:, pl.ds(at, 128)] = vo[i * s : i * s + s, lanes].astype(F32)
    small = qk_mine[:, 2 * side :].astype(F32) + qk_other[:, 2 * side :].astype(F32)
    plan, _ = small_plan(n, sizes)
    for (size, count, at), out in zip(plan, vectors):
        line = jnp.concatenate([small[at + c : at + c + 1, :] for c in range(count)], 1)
        line = jnp.broadcast_to(line, (8, 128 * count))
        start = lax.rem(ids[0] * size, 128)
        out[...] = pltpu.roll(line, lax.rem(128 * count - start, 128 * count), 1)[0, :size]


def join_last(ids, n, sizes, qk, vo, width, pos):
    r = qk.mine.shape[0]
    shapes = [(r, 3 * width), (pos, width), (pos, width)] + [(s,) for s in sizes]
    return call(
        functools.partial(join_last_kernel, n, sizes), "join_last", (1,), ids, (qk.mine, qk.other, vo.mine, vo.other),
        [whole(qk.mine.shape)] * 2 + [whole(vo.mine.shape)] * 2,
        [whole(s) for s in shapes], [SDS(s, F32) for s in shapes], vmem=16, us=2,
    )


def plain_sum(g, n, place):
    left = list(range(n.bit_length() - 2, -1, -1))
    acc = g.astype(BF16).reshape((2,) * len(left) + (g.shape[0] // n, g.shape[1]))
    for bit in sorted(left):
        axis = left.index(bit)
        mine = (place >> bit) & 1
        send = lax.dynamic_index_in_dim(acc, 1 - mine, axis, keepdims=False)
        keep = lax.dynamic_index_in_dim(acc, mine, axis, keepdims=False)
        acc = (keep.astype(F32) + across(send, n, (bit, bit)).astype(F32)).astype(BF16)
        left.remove(bit)
    return acc


def plain_join(core, g):
    got = swap(g)
    sides = jnp.where(core == 0, jnp.stack([g, got], 1), jnp.stack([got, g], 1))
    return sides.reshape(g.shape[0], -1).astype(F32)


def pages(core, keep, got):
    return lax.dynamic_update_slice_in_dim(keep, got[None], 1 - core, 0)


def after(value, *others):
    return lax.optimization_barrier((value, *others))[0]


def body(n, tokens, boxes, lengths, w_qkv, b_qkv, w_posk, w_posq, w_out, b_out, gain_one, shift_one,
         w_in, b_in, w_down, b_down, gain_two, shift_two, cotangent):
    place = lax.axis_index("pages").astype(jnp.int32)
    core = lax.axis_index("slab").astype(jnp.int32)
    ids = jnp.stack([place, core])
    width = tokens.shape[2]
    other = swap(tokens)
    cot_other = swap(cotangent)

    kf, tab, tabt, fkt, fqt, wkt, wqt = tables(ids, boxes, w_posk, w_posq)
    pt, p, xt = project(after(ids, kf), tokens, other, w_qkv, b_qkv)
    e, att, r = attend(ids, lengths, pt, p, w_posk, w_posq, kf, tab, tabt, fqt)
    (flt, norm, rstd, slope, actt, out_keep, out_give, dres_two, dsec, dsec_send, rows_two) = feed(
        ids, att, tokens, other, w_out, w_in, w_down, b_out, gain_one, shift_one, b_in, b_down, gain_two, shift_two,
        cotangent, cot_other
    )
    xt_other, att_other, flt_other, actt_other = swap(xt), swap(att), swap(flt), swap(actt)
    dsec_other = swap(dsec_send)
    out_got = swap(out_give)
    dh_send, dh, row_in = hidden_back(ids, dsec, w_down, slope)
    dh_other = swap(dh_send)
    if width // n % 16:
        dres_one, branch, branch_send, datt, rows_one = first_back(
            ids, dh_send, dh, w_in, dres_two, norm, rstd, gain_one, w_out
        )
        args = dict(e=e, r=r, datt=datt, att=att, pt=pt, p=p, wkt=wkt, wqt=wqt, fkt=fkt, fqt=fqt, tabt=tabt)
        dp_send, gk_send, gq_send, bias_send = attend_back(ids, own=False, **args)
        dp, gk, gq, bias_own = attend_back(ids, own=True, **args)
        tok_keep, tok_give = tokens_back(ids, w_qkv, dp_send, dp, dres_one)
        first, second = jnp.where(core == 0, bias_own, bias_send), jnp.where(core == 0, bias_send, bias_own)
        rows_qkv = jnp.concatenate([first[::8], second[::8]], 1)
        dp_other = swap(dp_send)

        def side_of(a):
            size = a.shape[1] // 2
            return lax.dynamic_slice_in_dim(a, core * size, size, 1)

        def total(g):
            return plain_join(core, plain_sum(g, n, place))

        both = lambda op, a, b, c, d: op(a, b) + op(c, d)
        g_down = total(both(mm, actt, side_of(dsec), actt_other, dsec_other))
        g_in = total(both(mm, flt, dh, flt_other, dh_other))
        g_out = total(both(mm, att, side_of(branch), att_other, swap(branch_send)))
        g_posk = total(gk.astype(F32) + swap(gk_send).astype(F32))
        g_posq = total(gq.astype(F32) + swap(gq_send).astype(F32))
        g_qkv = jnp.concatenate([total(both(mm_nt, xt, dp[i], xt_other, dp_other[i])) for i in range(3)], 1)
        small = (rows_qkv, rows_one[2], rows_one[0], rows_one[1], row_in, rows_two[2], rows_two[0], rows_two[1])
        packed = lax.psum(jnp.concatenate([v.reshape(n, -1) for v in small], 1), ("pages", "slab"))
        packed = lax.dynamic_index_in_dim(packed, place, 0, keepdims=False)
        totals, at = [], 0
        for v in small:
            totals.append(packed[at : at + v.size // n])
            at += v.size // n
        return (pages(core, out_keep, out_got), pages(core, tok_keep, swap(tok_give)), g_qkv, totals[0], g_posk,
                g_posq, g_out, totals[1], totals[2], totals[3], g_in, totals[4], g_down, totals[5], totals[6],
                totals[7])

    order_down, order_mid, order_qk, order_vp = orders(n)
    first = Exchange.first
    down = Exchange(
        ids, n, *down_grad(ids, n, first(order_down), actt, actt_other, dsec, dsec_other), order_down
    )
    dres_one, branch, branch_send, datt, rows_one = first_back(
        after(ids, down.keep), dh_send, dh, w_in, dres_two, norm, rstd, gain_one, w_out
    )
    branch_other = swap(branch_send)
    mid = Exchange(
        ids, n, *mid_grad(ids, n, first(order_mid), flt, flt_other, dh, dh_other, att, att_other, branch, branch_other),
        order_mid,
    )
    down.step()
    back = functools.partial(
        attend_back, e=e, r=r, datt=datt, att=att, pt=pt, p=p, wkt=wkt, wqt=wqt, fkt=fkt, fqt=fqt, tabt=tabt
    )
    dp_send, gk_send, gq_send, bias_send = back(after(ids, mid.keep, down.keep), own=False)
    dp_other, gk_other, gq_other = swap(dp_send), swap(gk_send), swap(gq_send)
    down.step()
    dp, gk, gq, bias_own = back(after(ids, dp_send, down.keep), own=True)
    small = (3 * width, width, width, width, w_in.shape[1], width, width, width)
    sizes = tuple(s // n for s in small)
    mid.step()
    qk = Exchange(
        ids, n, *qk_grad(after(ids, mid.keep), n, first(order_qk), sizes, xt, xt_other, dp, dp_other,
                         rows_two, rows_one, row_in, bias_send, bias_own), order_qk
    )
    vp = Exchange(
        ids, n, *vp_grad(after(ids, qk.keep), n, first(order_vp), xt, xt_other, dp, dp_other,
                         gk, gk_other, gq, gq_other), order_vp
    )
    tok, tok_give = tokens_back(after(ids, vp.keep), w_qkv, dp_send, dp, dres_one)
    tok_got = swap(tok_give)
    while vp.at < vp.steps:
        for x in (down, mid, qk, vp):
            if x.at < x.steps:
                x.step()
    (g_down,) = join(ids, down.mine, down.other, (width,))
    g_in, g_out = join(ids, mid.mine, mid.other, (w_in.shape[1], width))
    g_qkv, g_posk, g_posq, *totals = join_last(ids, n, sizes, qk, vp, width, w_posk.shape[0] // n)
    return (pages(core, out_keep, out_got), pages(core, tok, tok_got), g_qkv, totals[0], g_posk, g_posq, g_out,
            totals[1], totals[2], totals[3], g_in, totals[4], g_down, totals[5], totals[6], totals[7])


def solution(mesh):
    n = mesh.shape["pages"]
    rows, mat, flat = P("pages", "slab", None), P("pages", None), P("pages")
    return jax.shard_map(
        functools.partial(body, n),
        mesh=mesh,
        in_specs=(rows, P("pages", None, None), flat) + (P(),) * 14 + (rows,),
        out_specs=(rows, rows, mat, flat, mat, mat, mat, flat, flat, flat, mat, flat, mat, flat, flat, flat),
        check_vma=False,
    )
```

```python
import functools
import math

import jax
import jax.numpy as jnp
from jax import lax
from jax.experimental import pallas as pl
from jax.experimental.pallas import tpu as pltpu
from jax.sharding import PartitionSpec as P

F32, BF16 = jnp.float32, jnp.bfloat16
HEADS = 12
PAIRS = HEADS // 2
BIG = 1e9
COST = 0.65e9
SDS = jax.ShapeDtypeStruct
HBM = pltpu.HBM


def mm(a, b):
    return lax.dot_general(a, b, (((1,), (0,)), ((), ())), preferred_element_type=F32)


def mm_nt(a, b):
    return lax.dot_general(a, b, (((1,), (1,)), ((), ())), preferred_element_type=F32)


def wide(ref):
    return ref[...].astype(F32).reshape(1, ref.shape[0])


def whole(shape):
    return pl.BlockSpec(shape, lambda *_: (0,) * len(shape))


def call(kernel, name, grid, ids, args, in_specs, out_specs, out_shape, scratch=(), vmem=17, us=1.0):
    return pl.pallas_call(
        kernel,
        grid_spec=pltpu.PrefetchScalarGridSpec(
            num_scalar_prefetch=1, grid=grid, in_specs=in_specs, out_specs=out_specs, scratch_shapes=list(scratch)
        ),
        out_shape=out_shape,
        compiler_params=pltpu.CompilerParams(vmem_limit_bytes=vmem << 20),
        cost_estimate=pl.CostEstimate(flops=int(us * COST), bytes_accessed=0, transcendentals=0),
        name=name,
    )(ids, *args)


def sin_cos(angle):
    turns = jnp.round(angle * (2.0 / math.pi))
    r = angle - turns * 1.5703125
    r = r - turns * 4.837512969970703125e-4
    r = r - turns * 7.54978995489188216e-8
    z = r * r
    s = ((-1.9515295891e-4 * z + 8.3321608736e-3) * z - 1.6666654611e-1) * z * r + r
    c = (
        (2.443315711809948e-5 * z - 1.388731625493765e-3) * z + 4.166664568298827e-2
    ) * z * z + (1.0 - 0.5 * z)
    q = turns.astype(jnp.int32)
    odd = (q & 1) == 1
    one, two = jnp.where(odd, c, s), jnp.where(odd, s, c)
    sine = jnp.where((q & 2) == 2, -one, one)
    cosine = jnp.where(((q + 1) & 2) == 2, -two, two)
    return sine, cosine


def rates(shape, dim):
    at = lax.broadcasted_iota(jnp.int32, shape, dim) & 63
    return jnp.exp(at.astype(F32) * (-math.log(10000.0) / 64))


def tables_kernel(ids, box_ref, kf_ref, tab_ref, tabt_ref, fkt_ref, fqt_ref):
    half = kf_ref.shape[0] // 2
    rate_row, rate_column = rates((8, 128), 1)[0:1, :], rates((64, 128), 0)[:, 0:1]
    box = box_ref[0].astype(F32)
    centre = (box[0:2, :] + box[2:4, :]) * 0.5
    turned = jnp.concatenate([centre[:, half:], centre[:, :half]], 1)
    centre = jnp.where(ids[1] == 0, centre, turned)
    column = jnp.concatenate([centre, jnp.zeros((6, 2 * half), F32)], 0).T
    front = lax.broadcasted_iota(jnp.int32, (2 * half, 128), 1) < 64
    for axis in range(2):
        s, c = sin_cos(column[:, axis : axis + 1] * rate_row)
        kf_ref[:, axis * 128 : axis * 128 + 128] = jnp.where(front, c, s).astype(BF16)
        tab_ref[axis] = c
        tab_ref[2 + axis] = jnp.where(front, s, -s)
        st, ct = sin_cos(rate_column * centre[axis : axis + 1, :])
        tabt_ref[2 * axis] = st
        tabt_ref[2 * axis + 1] = ct
        sl, cl = st.astype(BF16), ct.astype(BF16)
        at = 128 * axis
        fkt_ref[at : at + 64, :] = cl
        fkt_ref[at + 64 : at + 128, :] = sl
        fqt_ref[at : at + 64, :] = sl * 0.125
        fqt_ref[at + 64 : at + 128, :] = cl * 0.125


def tables(ids, boxes):
    rows = boxes.shape[2]
    shapes = [((rows, 256), BF16), ((4, rows, 128), F32), ((4, 64, rows), F32), ((256, rows), BF16), ((256, rows), BF16)]
    return call(
        tables_kernel, "tables", (1,), ids, (boxes,), [pl.BlockSpec((1, 4, rows), lambda i, ids: (ids[1], 0, 0))],
        [whole(s) for s, _ in shapes], [SDS(s, t) for s, t in shapes], us=3,
    )


def project_kernel(ids, own_ref, other_ref, w_ref, b_ref, pt_ref, p_ref, xt_ref, x, bias):
    step = pl.program_id(0)

    @pl.when(step == 0)
    def _():
        half = own_ref.shape[1]
        x[:half, :] = own_ref[0]
        x[half:, :] = other_ref[0]
        bias[...] = wide(b_ref)
        xt_ref[...] = x[...].T

    block = w_ref.shape[1]
    shift = bias[:, pl.ds(pl.multiple_of(step * block, 128), block)]
    p = (mm(x[...], w_ref[...]) + shift).astype(BF16)
    p_ref[...] = p
    pt_ref[...] = p.T


def page_specs(half, width):
    spec = pl.BlockSpec((1, half, width), lambda i, ids: (ids[1], 0, 0))
    return spec, spec


def project(ids, tokens, other, w, b):
    _, half, width = tokens.shape
    rows = 2 * half
    cols = w.shape[1]
    block = 768
    return call(
        project_kernel, "project", (cols // block,), ids, (tokens, other, w, b),
        [*page_specs(half, width), pl.BlockSpec((width, block), lambda i, ids: (0, i)), whole((cols,))],
        [
            pl.BlockSpec((block, rows), lambda i, ids: (i, 0)), pl.BlockSpec((rows, block), lambda i, ids: (0, i)),
            whole((width, rows)),
        ],
        [SDS((cols, rows), BF16), SDS((rows, cols), BF16), SDS((width, rows), BF16)],
        [pltpu.VMEM((rows, width), BF16), pltpu.VMEM((1, cols), F32)],
        us=5,
    )


def attend_kernel(ids, len_ref, qt_ref, vt_ref, k_ref, wk_ref, wq_ref, kf_ref, tab_ref, tabt_ref, fqt_ref,
                  e_ref, at_ref, r_ref, wkt_ref, wqt_ref, fk, fq):
    rows = k_ref.shape[0]
    wkt_ref[...] = wk_ref[...].T
    wqt_ref[...] = wq_ref[...].T
    heads = k_ref.shape[1] // 64

    @pl.when(pl.program_id(0) == 0)
    def _():
        lane = lax.broadcasted_iota(jnp.int32, (rows, 128), 1)
        at = lax.broadcasted_iota(jnp.int32, (rows, 128), 0)
        turned = jnp.where(at < rows // 2, at + rows // 2, at - rows // 2)
        at = jnp.where(ids[1] == 0, at, turned)
        mask = jnp.where((lane == 0) & (at >= len_ref[ids[1]]), -BIG, 0.0).astype(BF16)
        sub = lax.broadcasted_iota(jnp.int32, (128, rows), 0)
        for h in range(heads):
            fk[h, :, 0:256] = kf_ref[...]
            fk[h, :, 640:768] = mask
            fq[h, 256:512, :] = fqt_ref[...]
            fq[h, 640:768, :] = jnp.where(sub == 0, 1.0, 0.0).astype(BF16)

    lane = lax.broadcasted_iota(jnp.int32, (256, 128), 1)
    for h in range(heads):
        two = slice(h // 2 * 128, h // 2 * 128 + 128)
        fk[h, :, 512:640] = k_ref[:, two]
        mine = (lane < 64) if h % 2 == 0 else (lane >= 64)
        qt = qt_ref[h * 64 : h * 64 + 64, :]
        zero = jnp.zeros_like(qt)
        pad = jnp.concatenate([qt, zero] if h % 2 == 0 else [zero, qt], 0)
        fq[h, 512:640, :] = pad * 0.125
        a = mm(wk_ref[:, two], pad)
        sx, cx, sy, cy = (tabt_ref[i] * 0.125 for i in range(4))
        axs, axc, ays, ayc = (a[i * 64 : i * 64 + 64, :] for i in range(4))
        fq[h, 0:64, :] = (axs * sx + axc * cx).astype(BF16)
        fq[h, 64:128, :] = (axc * sx - axs * cx).astype(BF16)
        fq[h, 128:192, :] = (ays * sy + ayc * cy).astype(BF16)
        fq[h, 192:256, :] = (ayc * sy - ays * cy).astype(BF16)
        w = jnp.where(mine, wq_ref[:, two], 0).astype(BF16)
        b = mm_nt(k_ref[:, two], w)
        for axis in range(2):
            part = b[:, axis * 128 : axis * 128 + 128]
            turned = pltpu.roll(part, 64, 1)
            fk[h, :, 256 + axis * 128 : 384 + axis * 128] = (
                part * tab_ref[axis] + turned * tab_ref[2 + axis]
            ).astype(BF16)
    for h in range(heads):
        if h % 4 == 0:
            scores = [mm(fk[g], fq[g]) for g in range(h, h + 4)]
        s = scores[h % 4]
        e = jnp.exp(s - jnp.max(s, 0, keepdims=True))
        r = 1.0 / jnp.sum(e, 0, keepdims=True)
        low = e.astype(BF16)
        e_ref[h] = low
        at_ref[h * 64 : h * 64 + 64, :] = (mm(vt_ref[h * 64 : h * 64 + 64, :], low) * r).astype(BF16)
        r_ref[h // 2, h % 2 : h % 2 + 1, :] = r


def attend(ids, lengths, pt, p, w_posk, w_posq, kf, tab, tabt, fqt):
    rows = p.shape[0]
    width = pt.shape[0] // 3
    return call(
        attend_kernel, "attend", (PAIRS // 2,), ids, (lengths, pt, pt, p, w_posk, w_posq, kf, tab, tabt, fqt),
        [
            pl.BlockSpec(memory_space=pltpu.SMEM),
            pl.BlockSpec((256, rows), lambda i, ids: (i, 0)),
            pl.BlockSpec((256, rows), lambda i, ids: (2 * PAIRS // 2 + i, 0)),
            pl.BlockSpec((rows, 256), lambda i, ids: (0, PAIRS // 2 + i)),
            pl.BlockSpec((256, 256), lambda i, ids: (0, i)),
            pl.BlockSpec((256, 256), lambda i, ids: (0, i)),
            whole((rows, 256)), whole((4, rows, 128)), whole((4, 64, rows)), whole((256, rows)),
        ],
        [
            pl.BlockSpec((4, rows, rows), lambda i, ids: (i, 0, 0)),
            pl.BlockSpec((256, rows), lambda i, ids: (i, 0)),
            pl.BlockSpec((2, 2, rows), lambda i, ids: (i, 0, 0)),
            pl.BlockSpec((256, 256), lambda i, ids: (i, 0)),
            pl.BlockSpec((256, 256), lambda i, ids: (i, 0)),
        ],
        [
            HBM((HEADS, rows, rows), BF16), SDS((width, rows), BF16), SDS((PAIRS, 2, rows), F32),
            SDS((width, 256), BF16), SDS((width, 256), BF16),
        ],
        [pltpu.VMEM((4, rows, 768), BF16), pltpu.VMEM((4, 768, rows), BF16)],
        vmem=22, us=17,
    )


def feed_kernel(ids, at_ref, own_ref, other_ref, wo_ref, bo_ref, g1_ref, s1_ref, wi_ref, bi_ref, wd_ref, bd_ref,
                g2_ref, s2_ref, cown_ref, cother_ref,
                flt_ref, norm_ref, rstd_ref, slope_ref, actt_ref, keep_ref, give_ref, dres_ref, dsec_ref, send_ref,
                rows_ref, first, low, second, cot):
    step = pl.program_id(0)
    half = own_ref.shape[1]

    @pl.when(step == 0)
    def _():
        first[:half, :] = own_ref[0].astype(F32)
        first[half:, :] = other_ref[0].astype(F32)
        cot[:half, :] = cown_ref[0]
        cot[half:, :] = cother_ref[0]
        v = first[...] + (mm(at_ref[...].T, wo_ref[...]) + wide(bo_ref))
        c = v - jnp.mean(v, -1, keepdims=True)
        rstd = lax.rsqrt(jnp.mean(c * c, -1, keepdims=True) + 1e-6)
        normed = c * rstd
        norm_ref[...] = normed
        rstd_ref[...] = rstd
        f = normed * wide(g1_ref) + wide(s1_ref)
        first[...] = f + wide(bd_ref)
        l = f.astype(BF16)
        low[...] = l
        flt_ref[...] = l.T

    h = mm(low[...], wi_ref[...]) + wide(bi_ref)
    cdf = 0.5 * lax.erf(h * (0.5 ** 0.5)) + 0.5
    active = (h * cdf).astype(BF16)
    slope_ref[...] = (cdf + h * (jnp.exp(-0.5 * h * h) * ((2.0 * math.pi) ** -0.5))).astype(BF16)
    actt_ref[...] = active.T
    part = mm(active, wd_ref[...])

    @pl.when(step == 0)
    def _():
        second[...] = part

    @pl.when(step > 0)
    def _():
        second[...] += part

    @pl.when(step == pl.num_programs(0) - 1)
    def _():
        v = first[...] + second[...]
        c = v - jnp.mean(v, -1, keepdims=True)
        rstd = lax.rsqrt(jnp.mean(c * c, -1, keepdims=True) + 1e-6)
        normed = c * rstd
        out = (normed * wide(g2_ref) + wide(s2_ref)).astype(BF16)
        keep_ref[0] = out[:half, :]
        give_ref[...] = out[half:, :]
        g = cot[...].astype(F32)
        gg = g * wide(g2_ref)
        d = rstd * (
            gg - jnp.mean(gg, -1, keepdims=True) - normed * jnp.mean(gg * normed, -1, keepdims=True)
        )
        dres_ref[...] = d
        l = d.astype(BF16)
        dsec_ref[...] = l
        side = send_ref.shape[1]
        send_ref[...] = dsec_ref[:, pl.ds(pl.multiple_of((1 - ids[1]) * side, 128), side)]
        rows_ref[0:1, :] = jnp.sum(g * normed, 0, keepdims=True)
        rows_ref[1:2, :] = jnp.sum(g, 0, keepdims=True)
        rows_ref[2:3, :] = jnp.sum(l.astype(F32), 0, keepdims=True)
        rows_ref[3:8, :] = jnp.zeros((5, rows_ref.shape[1]), F32)


def vec(size):
    return pl.BlockSpec((size,), lambda i, ids: (0,))


def feed(ids, att, tokens, other, w_out, w_in, w_down, b_out, g1, s1, b_in, b_down, g2, s2, cot, cot_other):
    _, half, width = tokens.shape
    rows = 2 * half
    ff = w_in.shape[1]
    block = 1024
    mat = whole((rows, width))
    return call(
        feed_kernel, "feed", (ff // block,), ids,
        (att, tokens, other, w_out, b_out, g1, s1, w_in, b_in, w_down, b_down, g2, s2, cot, cot_other),
        [
            whole((width, rows)), *page_specs(half, width), whole((width, width)), vec(width), vec(width), vec(width),
            pl.BlockSpec((width, block), lambda i, ids: (0, i)),
            pl.BlockSpec((block,), lambda i, ids: (i,)),
            pl.BlockSpec((block, width), lambda i, ids: (i, 0)),
            vec(width), vec(width), vec(width), *page_specs(half, width),
        ],
        [
            whole((width, rows)), mat, whole((rows, 1)),
            pl.BlockSpec((rows, block), lambda i, ids: (0, i)),
            pl.BlockSpec((block, rows), lambda i, ids: (i, 0)),
            page_specs(half, width)[0], whole((half, width)), mat, mat, whole((rows, width // 2)), whole((8, width)),
        ],
        [
            SDS((width, rows), BF16), SDS((rows, width), F32), SDS((rows, 1), F32),
            SDS((rows, ff), BF16), SDS((ff, rows), BF16),
            SDS((2, half, width), BF16), SDS((half, width), BF16), SDS((rows, width), F32), SDS((rows, width), BF16),
            SDS((rows, width // 2), BF16), SDS((8, width), F32),
        ],
        [pltpu.VMEM((rows, width), F32), pltpu.VMEM((rows, width), BF16), pltpu.VMEM((rows, width), F32),
         pltpu.VMEM((rows, width), BF16)],
        vmem=24, us=15,
    )


def hidden_kernel(ids, ds_ref, wd_ref, slope_ref, send_ref, own_ref, rows_ref):
    step = pl.program_id(0)
    d = mm_nt(ds_ref[...], wd_ref[...]).astype(BF16).astype(F32)
    dh = (d * slope_ref[...].astype(F32)).astype(BF16)
    rows_ref[...] = jnp.sum(dh.astype(F32), 0, keepdims=True)
    sends = pl.num_programs(0) // 2

    @pl.when(step < sends)
    def _():
        send_ref[...] = dh

    @pl.when(step >= sends)
    def _():
        own_ref[...] = dh


def hidden_back(ids, dsec, w_down, slope):
    rows, width = dsec.shape
    ff = w_down.shape[0]
    block = 768
    steps = ff // block
    s = steps // 2
    at = lambda i, ids: jnp.where(ids[1] == 0, (i + s) % steps, i)
    return call(
        hidden_kernel, "hidden_back", (steps,), ids, (dsec, w_down, slope),
        [
            whole((rows, width)),
            pl.BlockSpec((block, width), lambda i, ids: (at(i, ids), 0)),
            pl.BlockSpec((rows, block), lambda i, ids: (0, at(i, ids))),
        ],
        [
            pl.BlockSpec((rows, block), lambda i, ids: (0, jnp.minimum(i, s - 1))),
            pl.BlockSpec((rows, block), lambda i, ids: (0, jnp.maximum(i - s, 0))),
            pl.BlockSpec((1, block), lambda i, ids: (0, at(i, ids))),
        ],
        [SDS((rows, ff // 2), BF16), SDS((rows, ff // 2), BF16), SDS((1, ff), F32)],
        us=5,
    )


def first_kernel(ids, dsend_ref, down_ref, wsend_ref, wown_ref, dres_ref, norm_ref, rstd_ref, g1_ref, wo_ref,
                 res_ref, branch_ref, send_ref, datt_ref, rows_ref, acc):
    step = pl.program_id(0)
    part = mm_nt(dsend_ref[...], wsend_ref[...]) + mm_nt(down_ref[...], wown_ref[...])

    @pl.when(step == 0)
    def _():
        acc[...] = part

    @pl.when(step > 0)
    def _():
        acc[...] += part

    @pl.when(step == pl.num_programs(0) - 1)
    def _():
        g = dres_ref[...] + acc[...].astype(BF16).astype(F32)
        normed = norm_ref[...]
        gg = g * wide(g1_ref)
        d = rstd_ref[...] * (
            gg - jnp.mean(gg, -1, keepdims=True) - normed * jnp.mean(gg * normed, -1, keepdims=True)
        )
        res_ref[...] = d
        l = d.astype(BF16)
        branch_ref[...] = l
        side = send_ref.shape[1]
        send_ref[...] = branch_ref[:, pl.ds(pl.multiple_of((1 - ids[1]) * side, 128), side)]
        datt_ref[...] = mm_nt(wo_ref[...], l).astype(BF16)
        rows_ref[0:1, :] = jnp.sum(g * normed, 0, keepdims=True)
        rows_ref[1:2, :] = jnp.sum(g, 0, keepdims=True)
        rows_ref[2:3, :] = jnp.sum(l.astype(F32), 0, keepdims=True)
        rows_ref[3:8, :] = jnp.zeros((5, rows_ref.shape[1]), F32)


def first_back(ids, dsend, down, w_in, dres, norm, rstd, g1, w_out):
    rows, width = dres.shape
    ff = w_in.shape[1]
    block = 512
    s = ff // block // 2
    mat = whole((rows, width))
    return call(
        first_kernel, "first_back", (s,), ids, (dsend, down, w_in, w_in, dres, norm, rstd, g1, w_out),
        [
            pl.BlockSpec((rows, block), lambda i, ids: (0, i)),
            pl.BlockSpec((rows, block), lambda i, ids: (0, i)),
            pl.BlockSpec((width, block), lambda i, ids: (0, (1 - ids[1]) * s + i)),
            pl.BlockSpec((width, block), lambda i, ids: (0, ids[1] * s + i)),
            mat, mat, whole((rows, 1)), vec(width), whole((width, width)),
        ],
        [mat, mat, whole((rows, width // 2)), whole((width, rows)), whole((8, width))],
        [
            SDS((rows, width), F32), SDS((rows, width), BF16), SDS((rows, width // 2), BF16), SDS((width, rows), BF16),
            SDS((8, width), F32),
        ],
        [pltpu.VMEM((rows, width), F32)],
        us=8,
    )


def attend_back_kernel(ids, e_ref, r_ref, da_ref, at_ref, qt_ref, kt_ref, v_ref, wkt_ref, wqt_ref, fkt_ref, fqt_ref,
                       tabt_ref, dp_ref, gk_ref, gq_ref, rows_ref, left_k, left_q):
    heads = 2

    @pl.when(pl.program_id(0) == 0)
    def _():
        for h in range(heads):
            left_k[h, 64:320, :] = fkt_ref[...]
            left_q[h, 64:320, :] = fqt_ref[...]

    sx, cx, sy, cy = (tabt_ref[i] for i in range(4))
    lane = lax.broadcasted_iota(jnp.int32, (256, 128), 1)
    own = [slice(h * 64, h * 64 + 64) for h in range(heads)]
    das, deltas, dps = [], [], []
    for h in range(heads):
        left_k[h, 0:64, :] = kt_ref[own[h], :]
        left_q[h, 0:64, :] = qt_ref[own[h], :] * 0.125
        da = da_ref[own[h], :].astype(F32) * r_ref[0, h : h + 1, :]
        deltas.append(jnp.sum(da * at_ref[own[h], :].astype(F32), 0, keepdims=True))
        da = da.astype(BF16)
        das.append(da)
        zero = jnp.zeros_like(da)
        pad = jnp.concatenate([da, zero] if h == 0 else [zero, da], 0)
        dps.append(mm(v_ref[...], pad))
    dss = [(e_ref[h].astype(F32) * (dps[h] - deltas[h])).astype(BF16) for h in range(heads)]
    ones = [mm(left_k[h], dss[h]) * 0.125 for h in range(heads)]
    twos = [mm_nt(left_q[h], dss[h]) for h in range(heads)]
    gk, gq = [], []
    for h in range(heads):
        dp_ref[2, own[h], :] = mm_nt(das[h], e_ref[h]).astype(BF16)
    for h in range(heads):
        one, two = ones[h], twos[h]
        ux1, ux2, uy1, uy2 = (one[64 + i * 64 : 128 + i * 64, :].astype(BF16).astype(F32) for i in range(4))
        d_a = jnp.concatenate(
            [ux1 * sx - ux2 * cx, ux1 * cx + ux2 * sx, uy1 * sy - uy2 * cy, uy1 * cy + uy2 * sy], 0
        ).astype(BF16)
        zx1, zx2, zy1, zy2 = (two[64 + i * 64 : 128 + i * 64, :] for i in range(4))
        d_b = jnp.concatenate(
            [zx1 * cx - zx2 * sx, zx1 * sx + zx2 * cx, zy1 * cy - zy2 * sy, zy1 * sy + zy2 * cy], 0
        ).astype(BF16)
        dp_ref[0, own[h], :] = (one[0:64, :] + mm(wkt_ref[own[h], :], d_a)).astype(BF16)
        dp_ref[1, own[h], :] = (two[0:64, :] + mm(wqt_ref[own[h], :], d_b)).astype(BF16)
        gk.append(mm_nt(d_a, qt_ref[...]))
        gq.append(mm_nt(d_b, kt_ref[...]))
    gk_ref[...] = jnp.where(lane < 64, gk[0], gk[1]).astype(BF16)
    gq_ref[...] = jnp.where(lane < 64, gq[0], gq[1]).astype(BF16)
    unit = jnp.ones((8, dp_ref.shape[2]), BF16)
    for i in range(3):
        rows_ref[8 * i : 8 * i + 8, :] = mm_nt(unit, dp_ref[i])


def attend_back(ids, own, e, r, datt, att, pt, p, wkt, wqt, fkt, fqt, tabt):
    rows = p.shape[0]
    pairs = PAIRS // 2
    lo = lambda ids: (ids[1] if own else 1 - ids[1]) * pairs
    pair = lambda base: pl.BlockSpec((128, rows), lambda i, ids: (base + lo(ids) + i, 0))
    wt = pl.BlockSpec((128, 256), lambda i, ids: (lo(ids) + i, 0))
    return call(
        attend_back_kernel, "attend_back", (pairs,), ids, (e, r, datt, att, pt, pt, p, wkt, wqt, fkt, fqt, tabt),
        [
            pl.BlockSpec((2, rows, rows), lambda i, ids: (lo(ids) + i, 0, 0)),
            pl.BlockSpec((1, 2, rows), lambda i, ids: (lo(ids) + i, 0, 0)),
            pair(0), pair(0), pair(0), pair(PAIRS),
            pl.BlockSpec((rows, 128), lambda i, ids: (0, 2 * PAIRS + lo(ids) + i)),
            wt, wt, whole((256, rows)), whole((256, rows)), whole((4, 64, rows)),
        ],
        [
            pl.BlockSpec((3, 128, rows), lambda i, ids: (0, i, 0)),
            pl.BlockSpec((256, 128), lambda i, ids: (0, i)),
            pl.BlockSpec((256, 128), lambda i, ids: (0, i)),
            pl.BlockSpec((24, 128), lambda i, ids: (0, i)),
        ],
        [
            SDS((3, 128 * pairs, rows), BF16), SDS((256, 128 * pairs), BF16), SDS((256, 128 * pairs), BF16),
            SDS((24, 128 * pairs), F32),
        ],
        [pltpu.VMEM((2, 320, rows), BF16), pltpu.VMEM((2, 320, rows), BF16)],
        us=9,
    )


def tokens_kernel(ids, w_ref, ds_ref, do_ref, dres_ref, keep_ref, give_ref):
    width = w_ref.shape[1] // 3
    side = width // 2
    half = keep_ref.shape[1]
    acc = None
    for h, ref in ((1 - ids[1], ds_ref), (ids[1], do_ref)):
        for s in range(3):
            at = pl.multiple_of(s * width + h * side, 128)
            part = mm(w_ref[:, pl.ds(at, side)], ref[s])
            acc = part if acc is None else acc + part
    out = (dres_ref[...] + acc.T).astype(BF16)
    keep_ref[0] = out[:half, :]
    give_ref[...] = out[half:, :]


def tokens_back(ids, w_qkv, dsend, down, dres):
    rows, width = dres.shape
    cols = w_qkv.shape[1]
    block = 256
    half = rows // 2
    blk = pl.BlockSpec((half, block), lambda i, ids: (0, i))
    return call(
        tokens_kernel, "tokens_back", (width // block,), ids, (w_qkv, dsend, down, dres),
        [
            pl.BlockSpec((block, cols), lambda i, ids: (i, 0)), whole(dsend.shape), whole(down.shape),
            pl.BlockSpec((rows, block), lambda i, ids: (0, i)),
        ],
        [pl.BlockSpec((1, half, block), lambda i, ids: (ids[1], 0, i)), blk],
        [SDS((2, half, width), BF16), SDS((half, width), BF16)],
        us=6,
    )


def chosen(core, pair):
    return jnp.where(core == 0, pair[0], pair[1])


def drop_bit(p, bit):
    return ((p >> (bit + 1)) << bit) | (p & ((1 << bit) - 1))


def put(ids, bits, p, lanes, value, send_ref, keep_ref):
    bit = chosen(ids[1], bits)
    here = ((p >> bit) & 1) == ((ids[0] >> bit) & 1)
    at = drop_bit(p, bit)

    @pl.when(here)
    def _():
        keep_ref[at, 0 : value.shape[0], lanes] = value

    @pl.when(jnp.logical_not(here))
    def _():
        send_ref[at, 0 : value.shape[0], lanes] = value


def down_kernel(n, bits, ids, a0_ref, a1_ref, b0_ref, b1_ref, send_ref, keep_ref):
    places = n // pl.num_programs(0)
    r, w = keep_ref.shape[1:]
    acc = mm(a0_ref[...], b0_ref[...]) + mm(a1_ref[...], b1_ref[...])
    for k in range(places):
        p = pl.program_id(0) * places + k
        put(ids, bits, p, slice(0, w), acc[k * r : k * r + r, :].astype(BF16), send_ref, keep_ref)


def down_grad(ids, n, bits, actt, actt_other, dsec, dsec_other):
    ff, rows = actt.shape
    side = dsec_other.shape[1]
    block = ff // 4
    part = (n // 2, ff // n, side)
    a = pl.BlockSpec((block, rows), lambda i, ids: (i, 0))
    return call(
        functools.partial(down_kernel, n, bits), "down_grad", (4,), ids, (actt, actt_other, dsec, dsec_other),
        [a, a, pl.BlockSpec((rows, side), lambda i, ids: (0, ids[1])), whole((rows, side))],
        [whole(part)] * 2, [SDS(part, BF16)] * 2,
        us=7,
    )


def mid_kernel(n, bits, ids, f0_ref, f1_ref, h0_ref, h1_ref, a0_ref, a1_ref, c0_ref, c1_ref, send_ref, keep_ref):
    step = pl.program_id(0)
    last = pl.num_programs(0) - 1
    r = keep_ref.shape[1]
    w = h0_ref.shape[1]

    @pl.when(step < last)
    def _():
        acc = mm(f0_ref[...], h0_ref[...]) + mm(f1_ref[...], h1_ref[...])
        lanes = pl.ds(pl.multiple_of(step * w, 128), w)
        for p in range(n):
            put(ids, bits, p, lanes, acc[p * r : p * r + r, :].astype(BF16), send_ref, keep_ref)

    @pl.when(step == last)
    def _():
        acc = mm(a0_ref[...], c0_ref[...]) + mm(a1_ref[...], c1_ref[...])
        lanes = slice(keep_ref.shape[2] - acc.shape[1], keep_ref.shape[2])
        for p in range(n):
            put(ids, bits, p, lanes, acc[p * r : p * r + r, :].astype(BF16), send_ref, keep_ref)


def mid_grad(ids, n, bits, flt, flt_other, dh, dh_other, att, att_other, branch, branch_other):
    width, rows = flt.shape
    ffs = dh.shape[1]
    side = branch_other.shape[1]
    block = 768
    steps = ffs // block
    part = (n // 2, width // n, ffs + side)
    b = pl.BlockSpec((rows, block), lambda i, ids: (0, jnp.minimum(i, steps - 1)))
    a = whole((width, rows))
    return call(
        functools.partial(mid_kernel, n, bits), "mid_grad", (steps + 1,), ids,
        (flt, flt_other, dh, dh_other, att, att_other, branch, branch_other),
        [a, a, b, b, a, a, pl.BlockSpec((rows, side), lambda i, ids: (0, ids[1])), whole((rows, side))],
        [whole(part)] * 2, [SDS(part, BF16)] * 2, us=6,
    )


def chunks(n, size):
    return max(((p + 1) * size - 1) // 128 - p * size // 128 + 1 for p in range(n))


def small_plan(n, sizes):
    plan, at = [], 0
    for size in sizes:
        plan.append((size, chunks(n, size), at))
        at += chunks(n, size)
    return plan, at


def qk_kernel(n, bits, sizes, ids, x0_ref, x1_ref, d0_ref, d1_ref, two_ref, one_ref, in_ref, rs_ref, ro_ref,
              send_ref, keep_ref, qkv_ref):
    r = keep_ref.shape[1]
    side = d0_ref.shape[1]
    for who, ref in ((1 - ids[1], rs_ref), (ids[1], ro_ref)):
        for i in range(3):
            at = pl.multiple_of(who * side, 128)
            qkv_ref[i : i + 1, pl.ds(at, side)] = ref[8 * i : 8 * i + 1, :]
    for i in range(2):
        acc = mm_nt(x0_ref[...], d0_ref[i]) + mm_nt(x1_ref[...], d1_ref[i])
        for p in range(n):
            put(ids, bits, p, slice(i * side, i * side + side), acc[p * r : p * r + r, :].astype(BF16), send_ref, keep_ref)
    vectors = (qkv_ref, one_ref, one_ref, one_ref, in_ref, two_ref, two_ref, two_ref)
    index = (None, 2, 0, 1, 0, 2, 0, 1)
    plan, _ = small_plan(n, sizes)
    for p in range(n):
        found = []
        for (size, count, _), ref, row in zip(plan, vectors, index):
            for c in range(count):
                at = min(p * size // 128 + c, n * size // 128 - 1)
                if row is None:
                    i, at = at * 128 // ref.shape[1], at * 128 % ref.shape[1]
                    found.append(ref[i : i + 1, at : at + 128])
                else:
                    found.append(ref[row : row + 1, at * 128 : at * 128 + 128])
        found = jnp.concatenate(found + [jnp.zeros((r - len(found), 128), F32)], 0).astype(BF16)
        put(ids, bits, p, slice(2 * side, 2 * side + 128), found, send_ref, keep_ref)


def qk_grad(ids, n, bits, sizes, xt, xt_other, dp, dp_other, two, one, into, rows_send, rows_own):
    width, rows = xt.shape
    side = dp.shape[1]
    part = (n // 2, width // n, 2 * side + 128)
    d = pl.BlockSpec((2, side, rows), lambda i, ids: (0, 0, 0))
    return call(
        functools.partial(qk_kernel, n, bits, sizes), "qk_grad", (1,), ids,
        (xt, xt_other, dp, dp_other, two, one, into, rows_send, rows_own),
        [whole(xt.shape)] * 2 + [d, d] + [whole(a.shape) for a in (two, one, into, rows_send, rows_own)],
        [whole(part)] * 2, [SDS(part, BF16)] * 2, [pltpu.VMEM((8, width), F32)],
        us=4,
    )


def vp_kernel(n, bits, ids, x0_ref, x1_ref, d0_ref, d1_ref, k0_ref, k1_ref, q0_ref, q1_ref, send_ref, keep_ref):
    r = keep_ref.shape[1]
    side = d0_ref.shape[1]
    acc = mm_nt(x0_ref[...], d0_ref[0]) + mm_nt(x1_ref[...], d1_ref[0])
    for p in range(n):
        put(ids, bits, p, slice(0, side), acc[p * r : p * r + r, :].astype(BF16), send_ref, keep_ref)
    base = side
    for own_ref, other_ref in ((k0_ref, k1_ref), (q0_ref, q1_ref)):
        acc = (own_ref[...].astype(F32) + other_ref[...].astype(F32)).astype(BF16)
        s = acc.shape[0] // n
        for p in range(n):
            rows = acc[p * s : p * s + s, :]
            stacked = jnp.concatenate([rows[:, 128 * i : 128 * i + 128] for i in range(side // 128)], 0)
            put(ids, bits, p, slice(base, base + 128), stacked, send_ref, keep_ref)
        base += 128


def vp_grad(ids, n, bits, xt, xt_other, dp, dp_other, gk, gk_other, gq, gq_other):
    width, rows = xt.shape
    side = dp.shape[1]
    part = (n // 2, width // n, side + 256)
    d = pl.BlockSpec((1, side, rows), lambda i, ids: (2, 0, 0))
    return call(
        functools.partial(vp_kernel, n, bits), "vp_grad", (1,), ids,
        (xt, xt_other, dp, dp_other, gk, gk_other, gq, gq_other),
        [whole(xt.shape)] * 2 + [d, d] + [whole(a.shape) for a in (gk, gk, gq, gq)],
        [whole(part)] * 2, [SDS(part, BF16)] * 2, us=3,
    )


def add_split_kernel(bits, lows, ids, keep_ref, got_ref, send_ref, next_ref):
    low = chosen(ids[1], lows)
    mine = (ids[0] >> chosen(ids[1], bits)) & 1

    @pl.loop(0, next_ref.shape[0])
    def _(q):
        base = ((q >> low) << (low + 1)) | (q & ((1 << low) - 1))
        for which, ref in ((1 - mine, send_ref), (mine, next_ref)):
            p = base + (which << low)
            ref[q] = (keep_ref[p].astype(F32) + got_ref[p].astype(F32)).astype(BF16)


def add_split(ids, keep, got, bits, lows):
    m, r, w = keep.shape
    part = (m // 2, r, w)
    return call(
        functools.partial(add_split_kernel, bits, lows), "add_split", (1,), ids, (keep, got),
        [whole(keep.shape)] * 2, [whole(part)] * 2, [SDS(part, BF16)] * 2, vmem=24, us=1,
    )


def add_last_kernel(ids, keep_ref, got_ref, out_ref):
    out_ref[...] = (keep_ref[0].astype(F32) + got_ref[0].astype(F32)).astype(BF16)


def add_last(ids, keep, got):
    _, r, w = keep.shape
    return call(
        add_last_kernel, "add_last", (1,), ids, (keep, got), [whole(keep.shape)] * 2, whole((r, w)), SDS((r, w), BF16),
        vmem=16, us=1,
    )


def swap(x):
    return lax.ppermute(x, "slab", [(0, 1), (1, 0)])


def across(x, n, bits):
    pairs = [(2 * p + c, 2 * (p ^ (1 << bits[c])) + c) for p in range(n) for c in range(2)]
    return lax.ppermute(x, ("pages", "slab"), pairs)


def orders(n):
    low = list(range(n.bit_length() - 1))
    if len(low) != 4:
        pair = (low, low[1::-1] + low[:1:-1])
        return pair, pair, pair, pair
    return ORDERS


ORDERS = (
    ((0, 2, 1, 3), (1, 2, 0, 3)),
    ((0, 1, 2, 3), (1, 0, 3, 2)),
    ((0, 1, 2, 3), (1, 0, 3, 2)),
    ((0, 1, 2, 3), (1, 0, 3, 2)),
)


class Chain:
    def __init__(self, ids):
        self.ids = ids

    def run(self, kernel, *args, **kwargs):
        out = kernel(self.ids, *args, **kwargs)
        self.ids = after(self.ids, out[0] if isinstance(out, (list, tuple)) else out)
        return out


class Exchange:
    def __init__(self, chain, n, send, keep, order):
        self.chain, self.n, self.order = chain, n, order
        self.left = [sorted(o) for o in order]
        self.at = 0
        self.steps = len(order[0])
        self.send, self.keep = send, keep

    @staticmethod
    def first(order):
        return tuple(o[0] for o in order)

    def bits(self, step):
        return tuple(o[step] for o in self.order)

    def start(self):
        self.got = across(self.send, self.n, self.bits(self.at))

    def step(self):
        for l, b in zip(self.left, self.bits(self.at)):
            l.remove(b)
        self.at += 1
        if self.at == self.steps:
            self.mine = self.chain.run(add_last, self.keep, self.got)
            self.other = swap(self.mine)
            return
        bits = self.bits(self.at)
        lows = tuple(l.index(b) for l, b in zip(self.left, bits))
        self.send, self.keep = self.chain.run(add_split, self.keep, self.got, bits, lows)
        self.start()


def join_kernel(ids, mine_ref, other_ref, *outs):
    core = ids[1]
    at = 0
    for out in outs:
        side = out.shape[1] // 2
        for who, ref in ((core, mine_ref), (1 - core, other_ref)):
            out[:, pl.ds(pl.multiple_of(who * side, 128), side)] = ref[:, at : at + side].astype(F32)
        at += side


def join(ids, mine, other, widths):
    r = mine.shape[0]
    return call(
        join_kernel, "join", (1,), ids, (mine, other), [whole(mine.shape)] * 2,
        [whole((r, w)) for w in widths], [SDS((r, w), F32) for w in widths], vmem=16, us=2,
    )


def join_last_kernel(n, sizes, ids, qk_mine, qk_other, vo_mine, vo_other, qkv_ref, posk_ref, posq_ref, *vectors):
    core = ids[1]
    r, width = qkv_ref.shape[0], qkv_ref.shape[1] // 3
    side = width // 2
    s = posk_ref.shape[0]

    def lay(out, base, who, ref, at):
        out[:, pl.ds(pl.multiple_of(base + who * side, 128), side)] = ref[:, at : at + side].astype(F32)

    for who, qk, vo in ((core, qk_mine, vo_mine), (1 - core, qk_other, vo_other)):
        lay(qkv_ref, 0, who, qk, 0)
        lay(qkv_ref, width, who, qk, side)
        lay(qkv_ref, 2 * width, who, vo, 0)
        for j, out in enumerate((posk_ref, posq_ref)):
            lanes = slice(side + 128 * j, side + 128 * j + 128)
            for i in range(r // s):
                at = pl.multiple_of(who * side + 128 * i, 128)
                out[:, pl.ds(at, 128)] = vo[i * s : i * s + s, lanes].astype(F32)
    small = qk_mine[:, 2 * side :].astype(F32) + qk_other[:, 2 * side :].astype(F32)
    plan, _ = small_plan(n, sizes)
    for (size, count, at), out in zip(plan, vectors):
        line = jnp.concatenate([small[at + c : at + c + 1, :] for c in range(count)], 1)
        line = jnp.broadcast_to(line, (8, 128 * count))
        start = lax.rem(ids[0] * size, 128)
        out[...] = pltpu.roll(line, lax.rem(128 * count - start, 128 * count), 1)[0, :size]


def join_last(ids, n, sizes, qk, vo, width, pos):
    r = qk.mine.shape[0]
    shapes = [(r, 3 * width), (pos, width), (pos, width)] + [(s,) for s in sizes]
    return call(
        functools.partial(join_last_kernel, n, sizes), "join_last", (1,), ids, (qk.mine, qk.other, vo.mine, vo.other),
        [whole(qk.mine.shape)] * 2 + [whole(vo.mine.shape)] * 2,
        [whole(s) for s in shapes], [SDS(s, F32) for s in shapes], vmem=16, us=2,
    )


def plain_sum(g, n, place):
    left = list(range(n.bit_length() - 2, -1, -1))
    acc = g.astype(BF16).reshape((2,) * len(left) + (g.shape[0] // n, g.shape[1]))
    for bit in sorted(left):
        axis = left.index(bit)
        mine = (place >> bit) & 1
        send = lax.dynamic_index_in_dim(acc, 1 - mine, axis, keepdims=False)
        keep = lax.dynamic_index_in_dim(acc, mine, axis, keepdims=False)
        acc = (keep.astype(F32) + across(send, n, (bit, bit)).astype(F32)).astype(BF16)
        left.remove(bit)
    return acc


def plain_join(core, g):
    got = swap(g)
    sides = jnp.where(core == 0, jnp.stack([g, got], 1), jnp.stack([got, g], 1))
    return sides.reshape(g.shape[0], -1).astype(F32)


def pages(core, keep, got):
    return lax.dynamic_update_slice_in_dim(keep, got[None], 1 - core, 0)


def after(value, *others):
    return lax.optimization_barrier((value, *others))[0]


def body(n, tokens, boxes, lengths, w_qkv, b_qkv, w_posk, w_posq, w_out, b_out, gain_one, shift_one,
         w_in, b_in, w_down, b_down, gain_two, shift_two, cotangent):
    place = lax.axis_index("pages").astype(jnp.int32)
    core = lax.axis_index("slab").astype(jnp.int32)
    ids = jnp.stack([place, core])
    width = tokens.shape[2]
    other = swap(tokens)
    cot_other = swap(cotangent)

    kf, tab, tabt, fkt, fqt = tables(ids, boxes)
    pt, p, xt = project(after(ids, kf), tokens, other, w_qkv, b_qkv)
    e, att, r, wkt, wqt = attend(ids, lengths, pt, p, w_posk, w_posq, kf, tab, tabt, fqt)
    (flt, norm, rstd, slope, actt, out_keep, out_give, dres_two, dsec, dsec_send, rows_two) = feed(
        ids, att, tokens, other, w_out, w_in, w_down, b_out, gain_one, shift_one, b_in, b_down, gain_two, shift_two,
        cotangent, cot_other
    )
    xt_other, att_other, flt_other, actt_other = swap(xt), swap(att), swap(flt), swap(actt)
    dsec_other = swap(dsec_send)
    out_got = swap(out_give)
    dh_send, dh, row_in = hidden_back(ids, dsec, w_down, slope)
    dh_other = swap(dh_send)
    if width // n % 16:
        dres_one, branch, branch_send, datt, rows_one = first_back(
            ids, dh_send, dh, w_in, dres_two, norm, rstd, gain_one, w_out
        )
        args = dict(e=e, r=r, datt=datt, att=att, pt=pt, p=p, wkt=wkt, wqt=wqt, fkt=fkt, fqt=fqt, tabt=tabt)
        dp_send, gk_send, gq_send, bias_send = attend_back(ids, own=False, **args)
        dp, gk, gq, bias_own = attend_back(ids, own=True, **args)
        tok_keep, tok_give = tokens_back(ids, w_qkv, dp_send, dp, dres_one)
        first, second = jnp.where(core == 0, bias_own, bias_send), jnp.where(core == 0, bias_send, bias_own)
        rows_qkv = jnp.concatenate([first[::8], second[::8]], 1)
        dp_other = swap(dp_send)

        def side_of(a):
            size = a.shape[1] // 2
            return lax.dynamic_slice_in_dim(a, core * size, size, 1)

        def total(g):
            return plain_join(core, plain_sum(g, n, place))

        both = lambda op, a, b, c, d: op(a, b) + op(c, d)
        g_down = total(both(mm, actt, side_of(dsec), actt_other, dsec_other))
        g_in = total(both(mm, flt, dh, flt_other, dh_other))
        g_out = total(both(mm, att, side_of(branch), att_other, swap(branch_send)))
        g_posk = total(gk.astype(F32) + swap(gk_send).astype(F32))
        g_posq = total(gq.astype(F32) + swap(gq_send).astype(F32))
        g_qkv = jnp.concatenate([total(both(mm_nt, xt, dp[i], xt_other, dp_other[i])) for i in range(3)], 1)
        small = (rows_qkv, rows_one[2], rows_one[0], rows_one[1], row_in, rows_two[2], rows_two[0], rows_two[1])
        packed = lax.psum(jnp.concatenate([v.reshape(n, -1) for v in small], 1), ("pages", "slab"))
        packed = lax.dynamic_index_in_dim(packed, place, 0, keepdims=False)
        totals, at = [], 0
        for v in small:
            totals.append(packed[at : at + v.size // n])
            at += v.size // n
        return (pages(core, out_keep, out_got), pages(core, tok_keep, swap(tok_give)), g_qkv, totals[0], g_posk,
                g_posq, g_out, totals[1], totals[2], totals[3], g_in, totals[4], g_down, totals[5], totals[6],
                totals[7])

    order_down, order_mid, order_qk, order_vp = orders(n)
    first = Exchange.first
    chain = Chain(after(ids, dh))
    down = Exchange(
        chain, n, *chain.run(down_grad, n, first(order_down), actt, actt_other, dsec, dsec_other), order_down
    )
    down.start()
    dres_one, branch, branch_send, datt, rows_one = chain.run(
        first_back, dh_send, dh, w_in, dres_two, norm, rstd, gain_one, w_out
    )
    branch_other = swap(branch_send)
    mid = Exchange(
        chain, n,
        *chain.run(mid_grad, n, first(order_mid), flt, flt_other, dh, dh_other, att, att_other, branch, branch_other),
        order_mid,
    )
    down.step()
    mid.send = after(mid.send, down.send)
    mid.start()
    back = functools.partial(
        chain.run, attend_back, e=e, r=r, datt=datt, att=att, pt=pt, p=p, wkt=wkt, wqt=wqt, fkt=fkt, fqt=fqt, tabt=tabt
    )
    dp_send, gk_send, gq_send, bias_send = back(own=False)
    dp_other, gk_other, gq_other = swap(dp_send), swap(gk_send), swap(gq_send)
    down.step()
    dp, gk, gq, bias_own = back(own=True)
    small = (3 * width, width, width, width, w_in.shape[1], width, width, width)
    sizes = tuple(s // n for s in small)
    down.step()
    mid.step()
    qk = Exchange(
        chain, n, *chain.run(qk_grad, n, first(order_qk), sizes, xt, xt_other, dp, dp_other,
                             rows_two, rows_one, row_in, bias_send, bias_own), order_qk
    )
    qk.start()
    vp = Exchange(
        chain, n, *chain.run(vp_grad, n, first(order_vp), xt, xt_other, dp, dp_other,
                             gk, gk_other, gq, gq_other), order_vp
    )
    vp.start()
    down.step()
    mid.step()
    tok, tok_give = chain.run(tokens_back, w_qkv, dp_send, dp, dres_one)
    tok_got = swap(tok_give)
    qk.step()
    vp.step()
    mid.step()
    (g_down,) = chain.run(join, down.mine, down.other, (width,))
    qk.step()
    vp.step()
    mid.step()
    qk.step()
    vp.step()
    g_in, g_out = chain.run(join, mid.mine, mid.other, (w_in.shape[1], width))
    qk.step()
    vp.step()
    g_qkv, g_posk, g_posq, *totals = join_last(ids, n, sizes, qk, vp, width, w_posk.shape[0] // n)
    return (pages(core, out_keep, out_got), pages(core, tok, tok_got), g_qkv, totals[0], g_posk, g_posq, g_out,
            totals[1], totals[2], totals[3], g_in, totals[4], g_down, totals[5], totals[6], totals[7])


def solution(mesh):
    n = mesh.shape["pages"]
    rows, mat, flat = P("pages", "slab", None), P("pages", None), P("pages")
    return jax.shard_map(
        functools.partial(body, n),
        mesh=mesh,
        in_specs=(rows, P("pages", None, None), flat) + (P(),) * 14 + (rows,),
        out_specs=(rows, rows, mat, flat, mat, mat, mat, flat, flat, flat, mat, flat, mat, flat, flat, flat),
        check_vma=False,
    )
```

```python
import functools
import math

import jax
import jax.numpy as jnp
from jax import lax
from jax.experimental import pallas as pl
from jax.experimental.pallas import tpu as pltpu
from jax.sharding import PartitionSpec as P

F32, BF16 = jnp.float32, jnp.bfloat16
HEADS = 12
PAIRS = HEADS // 2
BIG = 1e9
COST = 0.65e9
SDS = jax.ShapeDtypeStruct
HBM = pltpu.HBM


def mm(a, b):
    return lax.dot_general(a, b, (((1,), (0,)), ((), ())), preferred_element_type=F32)


def mm_nt(a, b):
    return lax.dot_general(a, b, (((1,), (1,)), ((), ())), preferred_element_type=F32)


def wide(ref):
    return ref[...].astype(F32).reshape(1, ref.shape[0])


def beside(*values):
    return jnp.concatenate(values, 1)


def below(*values):
    return jnp.concatenate(values, 0)


def whole(shape):
    return pl.BlockSpec(shape, lambda *_: (0,) * len(shape))


def call(kernel, name, grid, ids, args, in_specs, out_specs, out_shape, scratch=(), vmem=17, us=1.0):
    return pl.pallas_call(
        kernel,
        grid_spec=pltpu.PrefetchScalarGridSpec(
            num_scalar_prefetch=1, grid=grid, in_specs=in_specs, out_specs=out_specs, scratch_shapes=list(scratch)
        ),
        out_shape=out_shape,
        compiler_params=pltpu.CompilerParams(vmem_limit_bytes=vmem << 20),
        cost_estimate=pl.CostEstimate(flops=int(us * COST), bytes_accessed=0, transcendentals=0),
        name=name,
    )(ids, *args)


def sin_cos(angle):
    turns = jnp.round(angle * (2.0 / math.pi))
    r = angle - turns * 1.5703125
    r = r - turns * 4.837512969970703125e-4
    r = r - turns * 7.54978995489188216e-8
    z = r * r
    s = ((-1.9515295891e-4 * z + 8.3321608736e-3) * z - 1.6666654611e-1) * z * r + r
    c = (
        (2.443315711809948e-5 * z - 1.388731625493765e-3) * z + 4.166664568298827e-2
    ) * z * z + (1.0 - 0.5 * z)
    q = turns.astype(jnp.int32)
    odd = (q & 1) == 1
    one, two = jnp.where(odd, c, s), jnp.where(odd, s, c)
    sine = jnp.where((q & 2) == 2, -one, one)
    cosine = jnp.where(((q + 1) & 2) == 2, -two, two)
    return sine, cosine


def rates(shape, dim):
    at = lax.broadcasted_iota(jnp.int32, shape, dim) & 63
    return jnp.exp(at.astype(F32) * (-math.log(10000.0) / 64))


def tables_kernel(ids, box_ref, kf_ref, tab_ref, tabt_ref, fkt_ref, fqt_ref):
    half = kf_ref.shape[0] // 2
    rate_row, rate_column = rates((8, 128), 1)[0:1, :], rates((64, 128), 0)[:, 0:1]
    box = box_ref[0].astype(F32)
    centre = (box[0:2, :] + box[2:4, :]) * 0.5
    turned = jnp.concatenate([centre[:, half:], centre[:, :half]], 1)
    centre = jnp.where(ids[1] == 0, centre, turned)
    column = jnp.concatenate([centre, jnp.zeros((6, 2 * half), F32)], 0).T
    front = lax.broadcasted_iota(jnp.int32, (2 * half, 128), 1) < 64
    for axis in range(2):
        s, c = sin_cos(column[:, axis : axis + 1] * rate_row)
        kf_ref[:, axis * 128 : axis * 128 + 128] = jnp.where(front, c, s).astype(BF16)
        tab_ref[axis] = c
        tab_ref[2 + axis] = jnp.where(front, s, -s)
        st, ct = sin_cos(rate_column * centre[axis : axis + 1, :])
        tabt_ref[2 * axis] = st
        tabt_ref[2 * axis + 1] = ct
        sl, cl = st.astype(BF16), ct.astype(BF16)
        at = 128 * axis
        fkt_ref[at : at + 64, :] = cl
        fkt_ref[at + 64 : at + 128, :] = sl
        fqt_ref[at : at + 64, :] = sl * 0.125
        fqt_ref[at + 64 : at + 128, :] = cl * 0.125


def tables(ids, boxes):
    rows = boxes.shape[2]
    shapes = [((rows, 256), BF16), ((4, rows, 128), F32), ((4, 64, rows), F32), ((256, rows), BF16), ((256, rows), BF16)]
    return call(
        tables_kernel, "tables", (1,), ids, (boxes,), [pl.BlockSpec((1, 4, rows), lambda i, ids: (ids[1], 0, 0))],
        [whole(s) for s, _ in shapes], [SDS(s, t) for s, t in shapes], us=3,
    )


def project_kernel(ids, own_ref, other_ref, w_ref, b_ref, pt_ref, p_ref, xt_ref, x, bias):
    step = pl.program_id(0)

    @pl.when(step == 0)
    def _():
        half = own_ref.shape[1]
        x[:half, :] = own_ref[0]
        x[half:, :] = other_ref[0]
        bias[...] = wide(b_ref)
        xt_ref[...] = x[...].T

    block = w_ref.shape[1]
    shift = bias[:, pl.ds(pl.multiple_of(step * block, 128), block)]
    p = (mm(x[...], w_ref[...]) + shift).astype(BF16)
    p_ref[...] = p
    pt_ref[...] = p.T


def page_specs(half, width):
    spec = pl.BlockSpec((1, half, width), lambda i, ids: (ids[1], 0, 0))
    return spec, spec


def project(ids, tokens, other, w, b):
    _, half, width = tokens.shape
    rows = 2 * half
    cols = w.shape[1]
    block = 768
    return call(
        project_kernel, "project", (cols // block,), ids, (tokens, other, w, b),
        [*page_specs(half, width), pl.BlockSpec((width, block), lambda i, ids: (0, i)), whole((cols,))],
        [
            pl.BlockSpec((block, rows), lambda i, ids: (i, 0)), pl.BlockSpec((rows, block), lambda i, ids: (0, i)),
            whole((width, rows)),
        ],
        [SDS((cols, rows), BF16), SDS((rows, cols), BF16), SDS((width, rows), BF16)],
        [pltpu.VMEM((rows, width), BF16), pltpu.VMEM((1, cols), F32)],
        us=5,
    )


def attend_kernel(ids, len_ref, qt_ref, vt_ref, k_ref, wk_ref, wq_ref, kf_ref, tab_ref, tabt_ref, fqt_ref,
                  e_ref, at_ref, r_ref, wkt_ref, wqt_ref, fk, fq):
    rows = k_ref.shape[0]
    wkt_ref[...] = wk_ref[...].T
    wqt_ref[...] = wq_ref[...].T
    heads = k_ref.shape[1] // 64

    @pl.when(pl.program_id(0) == 0)
    def _():
        lane = lax.broadcasted_iota(jnp.int32, (rows, 128), 1)
        at = lax.broadcasted_iota(jnp.int32, (rows, 128), 0)
        turned = jnp.where(at < rows // 2, at + rows // 2, at - rows // 2)
        at = jnp.where(ids[1] == 0, at, turned)
        mask = jnp.where((lane == 0) & (at >= len_ref[ids[1]]), -BIG, 0.0).astype(BF16)
        sub = lax.broadcasted_iota(jnp.int32, (128, rows), 0)
        for h in range(heads):
            fk[h, :, 0:256] = kf_ref[...]
            fk[h, :, 640:768] = mask
            fq[h, 256:512, :] = fqt_ref[...]
            fq[h, 640:768, :] = jnp.where(sub == 0, 1.0, 0.0).astype(BF16)

    lane = lax.broadcasted_iota(jnp.int32, (256, 128), 1)
    for h in range(heads):
        two = slice(h // 2 * 128, h // 2 * 128 + 128)
        fk[h, :, 512:640] = k_ref[:, two]
        mine = (lane < 64) if h % 2 == 0 else (lane >= 64)
        qt = qt_ref[h * 64 : h * 64 + 64, :]
        zero = jnp.zeros_like(qt)
        pad = jnp.concatenate([qt, zero] if h % 2 == 0 else [zero, qt], 0)
        fq[h, 512:640, :] = pad * 0.125
        a = mm(wk_ref[:, two], pad)
        sx, cx, sy, cy = (tabt_ref[i] * 0.125 for i in range(4))
        axs, axc, ays, ayc = (a[i * 64 : i * 64 + 64, :] for i in range(4))
        fq[h, 0:64, :] = (axs * sx + axc * cx).astype(BF16)
        fq[h, 64:128, :] = (axc * sx - axs * cx).astype(BF16)
        fq[h, 128:192, :] = (ays * sy + ayc * cy).astype(BF16)
        fq[h, 192:256, :] = (ayc * sy - ays * cy).astype(BF16)
        w = jnp.where(mine, wq_ref[:, two], 0).astype(BF16)
        b = mm_nt(k_ref[:, two], w)
        for axis in range(2):
            part = b[:, axis * 128 : axis * 128 + 128]
            turned = pltpu.roll(part, 64, 1)
            fk[h, :, 256 + axis * 128 : 384 + axis * 128] = (
                part * tab_ref[axis] + turned * tab_ref[2 + axis]
            ).astype(BF16)
    for h in range(heads):
        if h % 4 == 0:
            scores = [mm(fk[g], fq[g]) for g in range(h, h + 4)]
        s = scores[h % 4]
        e = jnp.exp(s - jnp.max(s, 0, keepdims=True))
        r = 1.0 / jnp.sum(e, 0, keepdims=True)
        low = e.astype(BF16)
        e_ref[h] = low
        at_ref[h * 64 : h * 64 + 64, :] = (mm(vt_ref[h * 64 : h * 64 + 64, :], low) * r).astype(BF16)
        r_ref[h // 2, h % 2 : h % 2 + 1, :] = r


def attend(ids, lengths, pt, p, w_posk, w_posq, kf, tab, tabt, fqt):
    rows = p.shape[0]
    width = pt.shape[0] // 3
    return call(
        attend_kernel, "attend", (PAIRS // 2,), ids, (lengths, pt, pt, p, w_posk, w_posq, kf, tab, tabt, fqt),
        [
            pl.BlockSpec(memory_space=pltpu.SMEM),
            pl.BlockSpec((256, rows), lambda i, ids: (i, 0)),
            pl.BlockSpec((256, rows), lambda i, ids: (2 * PAIRS // 2 + i, 0)),
            pl.BlockSpec((rows, 256), lambda i, ids: (0, PAIRS // 2 + i)),
            pl.BlockSpec((256, 256), lambda i, ids: (0, i)),
            pl.BlockSpec((256, 256), lambda i, ids: (0, i)),
            whole((rows, 256)), whole((4, rows, 128)), whole((4, 64, rows)), whole((256, rows)),
        ],
        [
            pl.BlockSpec((4, rows, rows), lambda i, ids: (i, 0, 0)),
            pl.BlockSpec((256, rows), lambda i, ids: (i, 0)),
            pl.BlockSpec((2, 2, rows), lambda i, ids: (i, 0, 0)),
            pl.BlockSpec((256, 256), lambda i, ids: (i, 0)),
            pl.BlockSpec((256, 256), lambda i, ids: (i, 0)),
        ],
        [
            HBM((HEADS, rows, rows), BF16), SDS((width, rows), BF16), SDS((PAIRS, 2, rows), F32),
            SDS((width, 256), BF16), SDS((width, 256), BF16),
        ],
        [pltpu.VMEM((4, rows, 768), BF16), pltpu.VMEM((4, 768, rows), BF16)],
        vmem=22, us=17,
    )


def feed_kernel(ids, at_ref, own_ref, other_ref, wo_ref, bo_ref, g1_ref, s1_ref, wi_ref, bi_ref, wd_ref, bd_ref,
                g2_ref, s2_ref, cown_ref, cother_ref,
                flt_ref, norm_ref, rstd_ref, slope_ref, actt_ref, keep_ref, give_ref, dres_ref, dsec_ref, send_ref,
                rows_ref, first, low, second, cot):
    step = pl.program_id(0)
    half = own_ref.shape[1]

    @pl.when(step == 0)
    def _():
        first[:half, :] = own_ref[0].astype(F32)
        first[half:, :] = other_ref[0].astype(F32)
        cot[:half, :] = cown_ref[0]
        cot[half:, :] = cother_ref[0]
        v = first[...] + (mm(at_ref[...].T, wo_ref[...]) + wide(bo_ref))
        c = v - jnp.mean(v, -1, keepdims=True)
        rstd = lax.rsqrt(jnp.mean(c * c, -1, keepdims=True) + 1e-6)
        normed = c * rstd
        norm_ref[...] = normed
        rstd_ref[...] = rstd
        f = normed * wide(g1_ref) + wide(s1_ref)
        first[...] = f + wide(bd_ref)
        l = f.astype(BF16)
        low[...] = l
        flt_ref[...] = l.T

    h = mm(low[...], wi_ref[...]) + wide(bi_ref)
    cdf = 0.5 * lax.erf(h * (0.5 ** 0.5)) + 0.5
    active = (h * cdf).astype(BF16)
    slope_ref[...] = (cdf + h * (jnp.exp(-0.5 * h * h) * ((2.0 * math.pi) ** -0.5))).astype(BF16)
    actt_ref[...] = active.T
    part = mm(active, wd_ref[...])

    @pl.when(step == 0)
    def _():
        second[...] = part

    @pl.when(step > 0)
    def _():
        second[...] += part

    @pl.when(step == pl.num_programs(0) - 1)
    def _():
        v = first[...] + second[...]
        c = v - jnp.mean(v, -1, keepdims=True)
        rstd = lax.rsqrt(jnp.mean(c * c, -1, keepdims=True) + 1e-6)
        normed = c * rstd
        out = (normed * wide(g2_ref) + wide(s2_ref)).astype(BF16)
        keep_ref[0] = out[:half, :]
        give_ref[...] = out[half:, :]
        g = cot[...].astype(F32)
        gg = g * wide(g2_ref)
        d = rstd * (
            gg - jnp.mean(gg, -1, keepdims=True) - normed * jnp.mean(gg * normed, -1, keepdims=True)
        )
        dres_ref[...] = d
        l = d.astype(BF16)
        dsec_ref[...] = l
        side = send_ref.shape[1]
        send_ref[...] = dsec_ref[:, pl.ds(pl.multiple_of((1 - ids[1]) * side, 128), side)]
        rows_ref[0:1, :] = jnp.sum(g * normed, 0, keepdims=True)
        rows_ref[1:2, :] = jnp.sum(g, 0, keepdims=True)
        rows_ref[2:3, :] = jnp.sum(l.astype(F32), 0, keepdims=True)
        rows_ref[3:8, :] = jnp.zeros((5, rows_ref.shape[1]), F32)


def vec(size):
    return pl.BlockSpec((size,), lambda i, ids: (0,))


def feed(ids, att, tokens, other, w_out, w_in, w_down, b_out, g1, s1, b_in, b_down, g2, s2, cot, cot_other):
    _, half, width = tokens.shape
    rows = 2 * half
    ff = w_in.shape[1]
    block = 1024
    mat = whole((rows, width))
    return call(
        feed_kernel, "feed", (ff // block,), ids,
        (att, tokens, other, w_out, b_out, g1, s1, w_in, b_in, w_down, b_down, g2, s2, cot, cot_other),
        [
            whole((width, rows)), *page_specs(half, width), whole((width, width)), vec(width), vec(width), vec(width),
            pl.BlockSpec((width, block), lambda i, ids: (0, i)),
            pl.BlockSpec((block,), lambda i, ids: (i,)),
            pl.BlockSpec((block, width), lambda i, ids: (i, 0)),
            vec(width), vec(width), vec(width), *page_specs(half, width),
        ],
        [
            whole((width, rows)), mat, whole((rows, 1)),
            pl.BlockSpec((rows, block), lambda i, ids: (0, i)),
            pl.BlockSpec((block, rows), lambda i, ids: (i, 0)),
            page_specs(half, width)[0], whole((half, width)), mat, mat, whole((rows, width // 2)), whole((8, width)),
        ],
        [
            SDS((width, rows), BF16), SDS((rows, width), F32), SDS((rows, 1), F32),
            SDS((rows, ff), BF16), SDS((ff, rows), BF16),
            SDS((2, half, width), BF16), SDS((half, width), BF16), SDS((rows, width), F32), SDS((rows, width), BF16),
            SDS((rows, width // 2), BF16), SDS((8, width), F32),
        ],
        [pltpu.VMEM((rows, width), F32), pltpu.VMEM((rows, width), BF16), pltpu.VMEM((rows, width), F32),
         pltpu.VMEM((rows, width), BF16)],
        vmem=24, us=15,
    )


def hidden_kernel(ids, ds_ref, wd_ref, slope_ref, send_ref, own_ref, rows_ref):
    step = pl.program_id(0)
    d = mm_nt(ds_ref[...], wd_ref[...]).astype(BF16).astype(F32)
    dh = (d * slope_ref[...].astype(F32)).astype(BF16)
    rows_ref[...] = jnp.sum(dh.astype(F32), 0, keepdims=True)
    sends = pl.num_programs(0) // 2

    @pl.when(step < sends)
    def _():
        send_ref[...] = dh

    @pl.when(step >= sends)
    def _():
        own_ref[...] = dh


def hidden_back(ids, dsec, w_down, slope):
    rows, width = dsec.shape
    ff = w_down.shape[0]
    block = 1536
    steps = ff // block
    s = steps // 2
    at = lambda i, ids: jnp.where(ids[1] == 0, (i + s) % steps, i)
    return call(
        hidden_kernel, "hidden_back", (steps,), ids, (dsec, w_down, slope),
        [
            whole((rows, width)),
            pl.BlockSpec((block, width), lambda i, ids: (at(i, ids), 0)),
            pl.BlockSpec((rows, block), lambda i, ids: (0, at(i, ids))),
        ],
        [
            pl.BlockSpec((rows, block), lambda i, ids: (0, jnp.minimum(i, s - 1))),
            pl.BlockSpec((rows, block), lambda i, ids: (0, jnp.maximum(i - s, 0))),
            pl.BlockSpec((1, block), lambda i, ids: (0, at(i, ids))),
        ],
        [SDS((rows, ff // 2), BF16), SDS((rows, ff // 2), BF16), SDS((1, ff), F32)],
        us=5,
    )


def first_kernel(ids, dsend_ref, down_ref, wsend_ref, wown_ref, dres_ref, norm_ref, rstd_ref, g1_ref, wo_ref,
                 res_ref, branch_ref, send_ref, datt_ref, rows_ref, acc):
    step = pl.program_id(0)
    part = mm_nt(beside(dsend_ref[...], down_ref[...]), beside(wsend_ref[...], wown_ref[...]))

    @pl.when(step == 0)
    def _():
        acc[...] = part

    @pl.when(step > 0)
    def _():
        acc[...] += part

    @pl.when(step == pl.num_programs(0) - 1)
    def _():
        g = dres_ref[...] + acc[...].astype(BF16).astype(F32)
        normed = norm_ref[...]
        gg = g * wide(g1_ref)
        d = rstd_ref[...] * (
            gg - jnp.mean(gg, -1, keepdims=True) - normed * jnp.mean(gg * normed, -1, keepdims=True)
        )
        res_ref[...] = d
        l = d.astype(BF16)
        branch_ref[...] = l
        side = send_ref.shape[1]
        send_ref[...] = branch_ref[:, pl.ds(pl.multiple_of((1 - ids[1]) * side, 128), side)]
        datt_ref[...] = mm_nt(wo_ref[...], l).astype(BF16)
        rows_ref[0:1, :] = jnp.sum(g * normed, 0, keepdims=True)
        rows_ref[1:2, :] = jnp.sum(g, 0, keepdims=True)
        rows_ref[2:3, :] = jnp.sum(l.astype(F32), 0, keepdims=True)
        rows_ref[3:8, :] = jnp.zeros((5, rows_ref.shape[1]), F32)


def first_back(ids, dsend, down, w_in, dres, norm, rstd, g1, w_out):
    rows, width = dres.shape
    ff = w_in.shape[1]
    block = 768
    s = ff // block // 2
    mat = whole((rows, width))
    return call(
        first_kernel, "first_back", (s,), ids, (dsend, down, w_in, w_in, dres, norm, rstd, g1, w_out),
        [
            pl.BlockSpec((rows, block), lambda i, ids: (0, i)),
            pl.BlockSpec((rows, block), lambda i, ids: (0, i)),
            pl.BlockSpec((width, block), lambda i, ids: (0, (1 - ids[1]) * s + i)),
            pl.BlockSpec((width, block), lambda i, ids: (0, ids[1] * s + i)),
            mat, mat, whole((rows, 1)), vec(width), whole((width, width)),
        ],
        [mat, mat, whole((rows, width // 2)), whole((width, rows)), whole((8, width))],
        [
            SDS((rows, width), F32), SDS((rows, width), BF16), SDS((rows, width // 2), BF16), SDS((width, rows), BF16),
            SDS((8, width), F32),
        ],
        [pltpu.VMEM((rows, width), F32)],
        us=8,
    )


def attend_back_kernel(ids, e_ref, r_ref, da_ref, at_ref, qt_ref, kt_ref, v_ref, wkt_ref, wqt_ref, fkt_ref, fqt_ref,
                       tabt_ref, dp_ref, gk_ref, gq_ref, rows_ref, left_k, left_q):
    heads = 2

    @pl.when(pl.program_id(0) == 0)
    def _():
        for h in range(heads):
            left_k[h, 64:320, :] = fkt_ref[...]
            left_q[h, 64:320, :] = fqt_ref[...]

    sx, cx, sy, cy = (tabt_ref[i] for i in range(4))
    lane = lax.broadcasted_iota(jnp.int32, (256, 128), 1)
    own = [slice(h * 64, h * 64 + 64) for h in range(heads)]
    das, deltas, dps = [], [], []
    for h in range(heads):
        left_k[h, 0:64, :] = kt_ref[own[h], :]
        left_q[h, 0:64, :] = qt_ref[own[h], :] * 0.125
        da = da_ref[own[h], :].astype(F32) * r_ref[0, h : h + 1, :]
        deltas.append(jnp.sum(da * at_ref[own[h], :].astype(F32), 0, keepdims=True))
        da = da.astype(BF16)
        das.append(da)
        zero = jnp.zeros_like(da)
        pad = jnp.concatenate([da, zero] if h == 0 else [zero, da], 0)
        dps.append(mm(v_ref[...], pad))
    dss = [(e_ref[h].astype(F32) * (dps[h] - deltas[h])).astype(BF16) for h in range(heads)]
    ones = [mm(left_k[h], dss[h]) * 0.125 for h in range(heads)]
    twos = [mm_nt(left_q[h], dss[h]) for h in range(heads)]
    gk, gq = [], []
    for h in range(heads):
        dp_ref[2, own[h], :] = mm_nt(das[h], e_ref[h]).astype(BF16)
    for h in range(heads):
        one, two = ones[h], twos[h]
        ux1, ux2, uy1, uy2 = (one[64 + i * 64 : 128 + i * 64, :].astype(BF16).astype(F32) for i in range(4))
        d_a = jnp.concatenate(
            [ux1 * sx - ux2 * cx, ux1 * cx + ux2 * sx, uy1 * sy - uy2 * cy, uy1 * cy + uy2 * sy], 0
        ).astype(BF16)
        zx1, zx2, zy1, zy2 = (two[64 + i * 64 : 128 + i * 64, :] for i in range(4))
        d_b = jnp.concatenate(
            [zx1 * cx - zx2 * sx, zx1 * sx + zx2 * cx, zy1 * cy - zy2 * sy, zy1 * sy + zy2 * cy], 0
        ).astype(BF16)
        dp_ref[0, own[h], :] = (one[0:64, :] + mm(wkt_ref[own[h], :], d_a)).astype(BF16)
        dp_ref[1, own[h], :] = (two[0:64, :] + mm(wqt_ref[own[h], :], d_b)).astype(BF16)
        gk.append(mm_nt(d_a, qt_ref[...]))
        gq.append(mm_nt(d_b, kt_ref[...]))
    gk_ref[...] = jnp.where(lane < 64, gk[0], gk[1]).astype(BF16)
    gq_ref[...] = jnp.where(lane < 64, gq[0], gq[1]).astype(BF16)
    unit = jnp.ones((8, dp_ref.shape[2]), BF16)
    for i in range(3):
        rows_ref[8 * i : 8 * i + 8, :] = mm_nt(unit, dp_ref[i])


def attend_back(ids, own, e, r, datt, att, pt, p, wkt, wqt, fkt, fqt, tabt):
    rows = p.shape[0]
    pairs = PAIRS // 2
    lo = lambda ids: (ids[1] if own else 1 - ids[1]) * pairs
    pair = lambda base: pl.BlockSpec((128, rows), lambda i, ids: (base + lo(ids) + i, 0))
    wt = pl.BlockSpec((128, 256), lambda i, ids: (lo(ids) + i, 0))
    return call(
        attend_back_kernel, "attend_back", (pairs,), ids, (e, r, datt, att, pt, pt, p, wkt, wqt, fkt, fqt, tabt),
        [
            pl.BlockSpec((2, rows, rows), lambda i, ids: (lo(ids) + i, 0, 0)),
            pl.BlockSpec((1, 2, rows), lambda i, ids: (lo(ids) + i, 0, 0)),
            pair(0), pair(0), pair(0), pair(PAIRS),
            pl.BlockSpec((rows, 128), lambda i, ids: (0, 2 * PAIRS + lo(ids) + i)),
            wt, wt, whole((256, rows)), whole((256, rows)), whole((4, 64, rows)),
        ],
        [
            pl.BlockSpec((3, 128, rows), lambda i, ids: (0, i, 0)),
            pl.BlockSpec((256, 128), lambda i, ids: (0, i)),
            pl.BlockSpec((256, 128), lambda i, ids: (0, i)),
            pl.BlockSpec((24, 128), lambda i, ids: (0, i)),
        ],
        [
            SDS((3, 128 * pairs, rows), BF16), SDS((256, 128 * pairs), BF16), SDS((256, 128 * pairs), BF16),
            SDS((24, 128 * pairs), F32),
        ],
        [pltpu.VMEM((2, 320, rows), BF16), pltpu.VMEM((2, 320, rows), BF16)],
        us=9,
    )


def tokens_kernel(ids, w_ref, ds_ref, do_ref, dres_ref, keep_ref, give_ref):
    width = w_ref.shape[1] // 3
    side = width // 2
    half = keep_ref.shape[1]
    left, right = [], []
    for h, ref in ((1 - ids[1], ds_ref), (ids[1], do_ref)):
        for s in range(3):
            left.append(w_ref[:, pl.ds(pl.multiple_of(s * width + h * side, 128), side)])
            right.append(ref[s])
    acc = mm(beside(*left), below(*right))
    out = (dres_ref[...] + acc.T).astype(BF16)
    keep_ref[0] = out[:half, :]
    give_ref[...] = out[half:, :]


def tokens_back(ids, w_qkv, dsend, down, dres):
    rows, width = dres.shape
    cols = w_qkv.shape[1]
    block = 256
    half = rows // 2
    blk = pl.BlockSpec((half, block), lambda i, ids: (0, i))
    return call(
        tokens_kernel, "tokens_back", (width // block,), ids, (w_qkv, dsend, down, dres),
        [
            pl.BlockSpec((block, cols), lambda i, ids: (i, 0)), whole(dsend.shape), whole(down.shape),
            pl.BlockSpec((rows, block), lambda i, ids: (0, i)),
        ],
        [pl.BlockSpec((1, half, block), lambda i, ids: (ids[1], 0, i)), blk],
        [SDS((2, half, width), BF16), SDS((half, width), BF16)],
        us=6,
    )


def chosen(core, pair):
    return jnp.where(core == 0, pair[0], pair[1])


def drop_bit(p, bit):
    return ((p >> (bit + 1)) << bit) | (p & ((1 << bit) - 1))


def put(ids, bits, p, lanes, value, send_ref, keep_ref):
    bit = chosen(ids[1], bits)
    here = ((p >> bit) & 1) == ((ids[0] >> bit) & 1)
    at = drop_bit(p, bit)

    @pl.when(here)
    def _():
        keep_ref[at, 0 : value.shape[0], lanes] = value

    @pl.when(jnp.logical_not(here))
    def _():
        send_ref[at, 0 : value.shape[0], lanes] = value


def down_kernel(n, bits, ids, a0_ref, a1_ref, b0_ref, b1_ref, send_ref, keep_ref):
    places = n // pl.num_programs(0)
    r, w = keep_ref.shape[1:]
    acc = mm(beside(a0_ref[...], a1_ref[...]), below(b0_ref[...], b1_ref[...]))
    for k in range(places):
        p = pl.program_id(0) * places + k
        put(ids, bits, p, slice(0, w), acc[k * r : k * r + r, :].astype(BF16), send_ref, keep_ref)


def down_grad(ids, n, bits, actt, actt_other, dsec, dsec_other):
    ff, rows = actt.shape
    side = dsec_other.shape[1]
    block = ff // 4
    part = (n // 2, ff // n, side)
    a = pl.BlockSpec((block, rows), lambda i, ids: (i, 0))
    return call(
        functools.partial(down_kernel, n, bits), "down_grad", (4,), ids, (actt, actt_other, dsec, dsec_other),
        [a, a, pl.BlockSpec((rows, side), lambda i, ids: (0, ids[1])), whole((rows, side))],
        [whole(part)] * 2, [SDS(part, BF16)] * 2,
        us=7,
    )


def mid_kernel(n, bits, ids, f0_ref, f1_ref, h0_ref, h1_ref, a0_ref, a1_ref, c0_ref, c1_ref, send_ref, keep_ref):
    step = pl.program_id(0)
    last = pl.num_programs(0) - 1
    r = keep_ref.shape[1]
    w = h0_ref.shape[1]

    @pl.when(step < last)
    def _():
        acc = mm(beside(f0_ref[...], f1_ref[...]), below(h0_ref[...], h1_ref[...]))
        lanes = pl.ds(pl.multiple_of(step * w, 128), w)
        for p in range(n):
            put(ids, bits, p, lanes, acc[p * r : p * r + r, :].astype(BF16), send_ref, keep_ref)

    @pl.when(step == last)
    def _():
        acc = mm(beside(a0_ref[...], a1_ref[...]), below(c0_ref[...], c1_ref[...]))
        lanes = slice(keep_ref.shape[2] - acc.shape[1], keep_ref.shape[2])
        for p in range(n):
            put(ids, bits, p, lanes, acc[p * r : p * r + r, :].astype(BF16), send_ref, keep_ref)


def mid_grad(ids, n, bits, flt, flt_other, dh, dh_other, att, att_other, branch, branch_other):
    width, rows = flt.shape
    ffs = dh.shape[1]
    side = branch_other.shape[1]
    block = 768
    steps = ffs // block
    part = (n // 2, width // n, ffs + side)
    b = pl.BlockSpec((rows, block), lambda i, ids: (0, jnp.minimum(i, steps - 1)))
    a = whole((width, rows))
    return call(
        functools.partial(mid_kernel, n, bits), "mid_grad", (steps + 1,), ids,
        (flt, flt_other, dh, dh_other, att, att_other, branch, branch_other),
        [a, a, b, b, a, a, pl.BlockSpec((rows, side), lambda i, ids: (0, ids[1])), whole((rows, side))],
        [whole(part)] * 2, [SDS(part, BF16)] * 2, us=6,
    )


def chunks(n, size):
    return max(((p + 1) * size - 1) // 128 - p * size // 128 + 1 for p in range(n))


def small_plan(n, sizes):
    plan, at = [], 0
    for size in sizes:
        plan.append((size, chunks(n, size), at))
        at += chunks(n, size)
    return plan, at


def qk_kernel(n, bits, sizes, ids, x0_ref, x1_ref, d0_ref, d1_ref, two_ref, one_ref, in_ref, rs_ref, ro_ref,
              send_ref, keep_ref, qkv_ref):
    r = keep_ref.shape[1]
    side = d0_ref.shape[1]
    for who, ref in ((1 - ids[1], rs_ref), (ids[1], ro_ref)):
        for i in range(3):
            at = pl.multiple_of(who * side, 128)
            qkv_ref[i : i + 1, pl.ds(at, side)] = ref[8 * i : 8 * i + 1, :]
    acc = mm_nt(beside(x0_ref[...], x1_ref[...]), below(beside(d0_ref[0], d1_ref[0]), beside(d0_ref[1], d1_ref[1])))
    for p in range(n):
        put(ids, bits, p, slice(0, 2 * side), acc[p * r : p * r + r, :].astype(BF16), send_ref, keep_ref)
    vectors = (qkv_ref, one_ref, one_ref, one_ref, in_ref, two_ref, two_ref, two_ref)
    index = (None, 2, 0, 1, 0, 2, 0, 1)
    plan, _ = small_plan(n, sizes)
    for p in range(n):
        found = []
        for (size, count, _), ref, row in zip(plan, vectors, index):
            for c in range(count):
                at = min(p * size // 128 + c, n * size // 128 - 1)
                if row is None:
                    i, at = at * 128 // ref.shape[1], at * 128 % ref.shape[1]
                    found.append(ref[i : i + 1, at : at + 128])
                else:
                    found.append(ref[row : row + 1, at * 128 : at * 128 + 128])
        found = jnp.concatenate(found + [jnp.zeros((r - len(found), 128), F32)], 0).astype(BF16)
        put(ids, bits, p, slice(2 * side, 2 * side + 128), found, send_ref, keep_ref)


def qk_grad(ids, n, bits, sizes, xt, xt_other, dp, dp_other, two, one, into, rows_send, rows_own):
    width, rows = xt.shape
    side = dp.shape[1]
    part = (n // 2, width // n, 2 * side + 128)
    d = pl.BlockSpec((2, side, rows), lambda i, ids: (0, 0, 0))
    return call(
        functools.partial(qk_kernel, n, bits, sizes), "qk_grad", (1,), ids,
        (xt, xt_other, dp, dp_other, two, one, into, rows_send, rows_own),
        [whole(xt.shape)] * 2 + [d, d] + [whole(a.shape) for a in (two, one, into, rows_send, rows_own)],
        [whole(part)] * 2, [SDS(part, BF16)] * 2, [pltpu.VMEM((8, width), F32)],
        us=4,
    )


def vp_kernel(n, bits, ids, x0_ref, x1_ref, d0_ref, d1_ref, k0_ref, k1_ref, q0_ref, q1_ref, send_ref, keep_ref):
    r = keep_ref.shape[1]
    side = d0_ref.shape[1]
    acc = mm_nt(beside(x0_ref[...], x1_ref[...]), beside(d0_ref[0], d1_ref[0]))
    for p in range(n):
        put(ids, bits, p, slice(0, side), acc[p * r : p * r + r, :].astype(BF16), send_ref, keep_ref)
    base = side
    for own_ref, other_ref in ((k0_ref, k1_ref), (q0_ref, q1_ref)):
        acc = (own_ref[...].astype(F32) + other_ref[...].astype(F32)).astype(BF16)
        s = acc.shape[0] // n
        for p in range(n):
            rows = acc[p * s : p * s + s, :]
            stacked = jnp.concatenate([rows[:, 128 * i : 128 * i + 128] for i in range(side // 128)], 0)
            put(ids, bits, p, slice(base, base + 128), stacked, send_ref, keep_ref)
        base += 128


def vp_grad(ids, n, bits, xt, xt_other, dp, dp_other, gk, gk_other, gq, gq_other):
    width, rows = xt.shape
    side = dp.shape[1]
    part = (n // 2, width // n, side + 256)
    d = pl.BlockSpec((1, side, rows), lambda i, ids: (2, 0, 0))
    return call(
        functools.partial(vp_kernel, n, bits), "vp_grad", (1,), ids,
        (xt, xt_other, dp, dp_other, gk, gk_other, gq, gq_other),
        [whole(xt.shape)] * 2 + [d, d] + [whole(a.shape) for a in (gk, gk, gq, gq)],
        [whole(part)] * 2, [SDS(part, BF16)] * 2, us=3,
    )


def add_split_kernel(bits, lows, ids, keep_ref, got_ref, send_ref, next_ref):
    low = chosen(ids[1], lows)
    mine = (ids[0] >> chosen(ids[1], bits)) & 1

    @pl.loop(0, next_ref.shape[0])
    def _(q):
        base = ((q >> low) << (low + 1)) | (q & ((1 << low) - 1))
        for which, ref in ((1 - mine, send_ref), (mine, next_ref)):
            p = base + (which << low)
            ref[q] = (keep_ref[p].astype(F32) + got_ref[p].astype(F32)).astype(BF16)


def add_split(ids, keep, got, bits, lows):
    m, r, w = keep.shape
    part = (m // 2, r, w)
    return call(
        functools.partial(add_split_kernel, bits, lows), "add_split", (1,), ids, (keep, got),
        [whole(keep.shape)] * 2, [whole(part)] * 2, [SDS(part, BF16)] * 2, vmem=24, us=1,
    )


def add_last_kernel(ids, keep_ref, got_ref, out_ref):
    out_ref[...] = (keep_ref[0].astype(F32) + got_ref[0].astype(F32)).astype(BF16)


def add_last(ids, keep, got):
    _, r, w = keep.shape
    return call(
        add_last_kernel, "add_last", (1,), ids, (keep, got), [whole(keep.shape)] * 2, whole((r, w)), SDS((r, w), BF16),
        vmem=16, us=1,
    )


def swap(x):
    return lax.ppermute(x, "slab", [(0, 1), (1, 0)])


def across(x, n, bits):
    pairs = [(2 * p + c, 2 * (p ^ (1 << bits[c])) + c) for p in range(n) for c in range(2)]
    return lax.ppermute(x, ("pages", "slab"), pairs)


def orders(n):
    low = list(range(n.bit_length() - 1))
    if len(low) != 4:
        pair = (low, low[1::-1] + low[:1:-1])
        return pair, pair, pair, pair
    return ORDERS


ORDERS = (
    ((0, 2, 1, 3), (1, 2, 0, 3)),
    ((0, 1, 2, 3), (1, 0, 3, 2)),
    ((0, 1, 2, 3), (1, 0, 3, 2)),
    ((0, 1, 2, 3), (1, 0, 3, 2)),
)


class Chain:
    def __init__(self, ids):
        self.ids = ids

    def run(self, kernel, *args, **kwargs):
        out = kernel(self.ids, *args, **kwargs)
        self.ids = after(self.ids, out[0] if isinstance(out, (list, tuple)) else out)
        return out


class Exchange:
    def __init__(self, chain, n, send, keep, order):
        self.chain, self.n, self.order = chain, n, order
        self.left = [sorted(o) for o in order]
        self.at = 0
        self.steps = len(order[0])
        self.send, self.keep = send, keep

    @staticmethod
    def first(order):
        return tuple(o[0] for o in order)

    def bits(self, step):
        return tuple(o[step] for o in self.order)

    def start(self):
        self.got = across(self.send, self.n, self.bits(self.at))

    def step(self):
        for l, b in zip(self.left, self.bits(self.at)):
            l.remove(b)
        self.at += 1
        if self.at == self.steps:
            self.mine = self.chain.run(add_last, self.keep, self.got)
            self.other = swap(self.mine)
            return
        bits = self.bits(self.at)
        lows = tuple(l.index(b) for l, b in zip(self.left, bits))
        self.send, self.keep = self.chain.run(add_split, self.keep, self.got, bits, lows)
        self.start()


def join_kernel(ids, mine_ref, other_ref, *outs):
    core = ids[1]
    at = 0
    for out in outs:
        side = out.shape[1] // 2
        for who, ref in ((core, mine_ref), (1 - core, other_ref)):
            out[:, pl.ds(pl.multiple_of(who * side, 128), side)] = ref[:, at : at + side].astype(F32)
        at += side


def join(ids, mine, other, widths):
    r = mine.shape[0]
    return call(
        join_kernel, "join", (1,), ids, (mine, other), [whole(mine.shape)] * 2,
        [whole((r, w)) for w in widths], [SDS((r, w), F32) for w in widths], vmem=16, us=2,
    )


def join_last_kernel(n, sizes, ids, qk_mine, qk_other, vo_mine, vo_other, qkv_ref, posk_ref, posq_ref, *vectors):
    core = ids[1]
    r, width = qkv_ref.shape[0], qkv_ref.shape[1] // 3
    side = width // 2
    s = posk_ref.shape[0]

    def lay(out, base, who, ref, at):
        out[:, pl.ds(pl.multiple_of(base + who * side, 128), side)] = ref[:, at : at + side].astype(F32)

    for who, qk, vo in ((core, qk_mine, vo_mine), (1 - core, qk_other, vo_other)):
        lay(qkv_ref, 0, who, qk, 0)
        lay(qkv_ref, width, who, qk, side)
        lay(qkv_ref, 2 * width, who, vo, 0)
        for j, out in enumerate((posk_ref, posq_ref)):
            lanes = slice(side + 128 * j, side + 128 * j + 128)
            for i in range(r // s):
                at = pl.multiple_of(who * side + 128 * i, 128)
                out[:, pl.ds(at, 128)] = vo[i * s : i * s + s, lanes].astype(F32)
    small = qk_mine[:, 2 * side :].astype(F32) + qk_other[:, 2 * side :].astype(F32)
    plan, _ = small_plan(n, sizes)
    for (size, count, at), out in zip(plan, vectors):
        line = jnp.concatenate([small[at + c : at + c + 1, :] for c in range(count)], 1)
        line = jnp.broadcast_to(line, (8, 128 * count))
        start = lax.rem(ids[0] * size, 128)
        out[...] = pltpu.roll(line, lax.rem(128 * count - start, 128 * count), 1)[0, :size]


def join_last(ids, n, sizes, qk, vo, width, pos):
    r = qk.mine.shape[0]
    shapes = [(r, 3 * width), (pos, width), (pos, width)] + [(s,) for s in sizes]
    return call(
        functools.partial(join_last_kernel, n, sizes), "join_last", (1,), ids, (qk.mine, qk.other, vo.mine, vo.other),
        [whole(qk.mine.shape)] * 2 + [whole(vo.mine.shape)] * 2,
        [whole(s) for s in shapes], [SDS(s, F32) for s in shapes], vmem=16, us=2,
    )


def plain_sum(g, n, place):
    left = list(range(n.bit_length() - 2, -1, -1))
    acc = g.astype(BF16).reshape((2,) * len(left) + (g.shape[0] // n, g.shape[1]))
    for bit in sorted(left):
        axis = left.index(bit)
        mine = (place >> bit) & 1
        send = lax.dynamic_index_in_dim(acc, 1 - mine, axis, keepdims=False)
        keep = lax.dynamic_index_in_dim(acc, mine, axis, keepdims=False)
        acc = (keep.astype(F32) + across(send, n, (bit, bit)).astype(F32)).astype(BF16)
        left.remove(bit)
    return acc


def plain_join(core, g):
    got = swap(g)
    sides = jnp.where(core == 0, jnp.stack([g, got], 1), jnp.stack([got, g], 1))
    return sides.reshape(g.shape[0], -1).astype(F32)


def pages(core, keep, got):
    return lax.dynamic_update_slice_in_dim(keep, got[None], 1 - core, 0)


def after(value, *others):
    return lax.optimization_barrier((value, *others))[0]


def body(n, tokens, boxes, lengths, w_qkv, b_qkv, w_posk, w_posq, w_out, b_out, gain_one, shift_one,
         w_in, b_in, w_down, b_down, gain_two, shift_two, cotangent):
    place = lax.axis_index("pages").astype(jnp.int32)
    core = lax.axis_index("slab").astype(jnp.int32)
    ids = jnp.stack([place, core])
    width = tokens.shape[2]
    other = swap(tokens)
    cot_other = swap(cotangent)

    kf, tab, tabt, fkt, fqt = tables(ids, boxes)
    pt, p, xt = project(after(ids, kf), tokens, other, w_qkv, b_qkv)
    e, att, r, wkt, wqt = attend(ids, lengths, pt, p, w_posk, w_posq, kf, tab, tabt, fqt)
    (flt, norm, rstd, slope, actt, out_keep, out_give, dres_two, dsec, dsec_send, rows_two) = feed(
        ids, att, tokens, other, w_out, w_in, w_down, b_out, gain_one, shift_one, b_in, b_down, gain_two, shift_two,
        cotangent, cot_other
    )
    xt_other, att_other, flt_other, actt_other = swap(xt), swap(att), swap(flt), swap(actt)
    dsec_other = swap(dsec_send)
    out_got = swap(out_give)
    dh_send, dh, row_in = hidden_back(ids, dsec, w_down, slope)
    dh_other = swap(dh_send)
    if width // n % 16:
        dres_one, branch, branch_send, datt, rows_one = first_back(
            ids, dh_send, dh, w_in, dres_two, norm, rstd, gain_one, w_out
        )
        args = dict(e=e, r=r, datt=datt, att=att, pt=pt, p=p, wkt=wkt, wqt=wqt, fkt=fkt, fqt=fqt, tabt=tabt)
        dp_send, gk_send, gq_send, bias_send = attend_back(ids, own=False, **args)
        dp, gk, gq, bias_own = attend_back(ids, own=True, **args)
        tok_keep, tok_give = tokens_back(ids, w_qkv, dp_send, dp, dres_one)
        first, second = jnp.where(core == 0, bias_own, bias_send), jnp.where(core == 0, bias_send, bias_own)
        rows_qkv = jnp.concatenate([first[::8], second[::8]], 1)
        dp_other = swap(dp_send)

        def side_of(a):
            size = a.shape[1] // 2
            return lax.dynamic_slice_in_dim(a, core * size, size, 1)

        def total(g):
            return plain_join(core, plain_sum(g, n, place))

        both = lambda op, a, b, c, d: op(a, b) + op(c, d)
        g_down = total(both(mm, actt, side_of(dsec), actt_other, dsec_other))
        g_in = total(both(mm, flt, dh, flt_other, dh_other))
        g_out = total(both(mm, att, side_of(branch), att_other, swap(branch_send)))
        g_posk = total(gk.astype(F32) + swap(gk_send).astype(F32))
        g_posq = total(gq.astype(F32) + swap(gq_send).astype(F32))
        g_qkv = jnp.concatenate([total(both(mm_nt, xt, dp[i], xt_other, dp_other[i])) for i in range(3)], 1)
        small = (rows_qkv, rows_one[2], rows_one[0], rows_one[1], row_in, rows_two[2], rows_two[0], rows_two[1])
        packed = lax.psum(jnp.concatenate([v.reshape(n, -1) for v in small], 1), ("pages", "slab"))
        packed = lax.dynamic_index_in_dim(packed, place, 0, keepdims=False)
        totals, at = [], 0
        for v in small:
            totals.append(packed[at : at + v.size // n])
            at += v.size // n
        return (pages(core, out_keep, out_got), pages(core, tok_keep, swap(tok_give)), g_qkv, totals[0], g_posk,
                g_posq, g_out, totals[1], totals[2], totals[3], g_in, totals[4], g_down, totals[5], totals[6],
                totals[7])

    order_down, order_mid, order_qk, order_vp = orders(n)
    first = Exchange.first
    chain = Chain(after(ids, dh))
    down = Exchange(
        chain, n, *chain.run(down_grad, n, first(order_down), actt, actt_other, dsec, dsec_other), order_down
    )
    down.start()
    dres_one, branch, branch_send, datt, rows_one = chain.run(
        first_back, dh_send, dh, w_in, dres_two, norm, rstd, gain_one, w_out
    )
    branch_other = swap(branch_send)
    mid = Exchange(
        chain, n,
        *chain.run(mid_grad, n, first(order_mid), flt, flt_other, dh, dh_other, att, att_other, branch, branch_other),
        order_mid,
    )
    down.step()
    mid.send = after(mid.send, down.send)
    mid.start()
    back = functools.partial(
        chain.run, attend_back, e=e, r=r, datt=datt, att=att, pt=pt, p=p, wkt=wkt, wqt=wqt, fkt=fkt, fqt=fqt, tabt=tabt
    )
    dp_send, gk_send, gq_send, bias_send = back(own=False)
    dp_other, gk_other, gq_other = swap(dp_send), swap(gk_send), swap(gq_send)
    down.step()
    dp, gk, gq, bias_own = back(own=True)
    small = (3 * width, width, width, width, w_in.shape[1], width, width, width)
    sizes = tuple(s // n for s in small)
    mid.step()
    down.step()
    qk = Exchange(
        chain, n, *chain.run(qk_grad, n, first(order_qk), sizes, xt, xt_other, dp, dp_other,
                             rows_two, rows_one, row_in, bias_send, bias_own), order_qk
    )
    qk.start()
    vp = Exchange(
        chain, n, *chain.run(vp_grad, n, first(order_vp), xt, xt_other, dp, dp_other,
                             gk, gk_other, gq, gq_other), order_vp
    )
    vp.start()
    down.step()
    mid.step()
    tok, tok_give = chain.run(tokens_back, w_qkv, dp_send, dp, dres_one)
    tok_got = swap(tok_give)
    qk.step()
    vp.step()
    mid.step()
    (g_down,) = chain.run(join, down.mine, down.other, (width,))
    qk.step()
    vp.step()
    mid.step()
    qk.step()
    vp.step()
    g_in, g_out = chain.run(join, mid.mine, mid.other, (w_in.shape[1], width))
    qk.step()
    vp.step()
    g_qkv, g_posk, g_posq, *totals = join_last(ids, n, sizes, qk, vp, width, w_posk.shape[0] // n)
    return (pages(core, out_keep, out_got), pages(core, tok, tok_got), g_qkv, totals[0], g_posk, g_posq, g_out,
            totals[1], totals[2], totals[3], g_in, totals[4], g_down, totals[5], totals[6], totals[7])


def solution(mesh):
    n = mesh.shape["pages"]
    rows, mat, flat = P("pages", "slab", None), P("pages", None), P("pages")
    return jax.shard_map(
        functools.partial(body, n),
        mesh=mesh,
        in_specs=(rows, P("pages", None, None), flat) + (P(),) * 14 + (rows,),
        out_specs=(rows, rows, mat, flat, mat, mat, mat, flat, flat, flat, mat, flat, mat, flat, flat, flat),
        check_vma=False,
    )
```

```python
import functools
import math

import jax
import jax.numpy as jnp
from jax import lax
from jax.experimental import pallas as pl
from jax.experimental.pallas import tpu as pltpu
from jax.sharding import PartitionSpec as P

F32, BF16 = jnp.float32, jnp.bfloat16
HEADS = 12
PAIRS = HEADS // 2
BIG = 1e9
COST = 0.65e9
SDS = jax.ShapeDtypeStruct
HBM = pltpu.HBM


def mm(a, b):
    return lax.dot_general(a, b, (((1,), (0,)), ((), ())), preferred_element_type=F32)


def mm_nt(a, b):
    return lax.dot_general(a, b, (((1,), (1,)), ((), ())), preferred_element_type=F32)


def wide(ref):
    return ref[...].astype(F32).reshape(1, ref.shape[0])


def beside(*values):
    return jnp.concatenate(values, 1)


def below(*values):
    return jnp.concatenate(values, 0)


def whole(shape):
    return pl.BlockSpec(shape, lambda *_: (0,) * len(shape))


def call(kernel, name, grid, ids, args, in_specs, out_specs, out_shape, scratch=(), vmem=17, us=1.0):
    return pl.pallas_call(
        kernel,
        grid_spec=pltpu.PrefetchScalarGridSpec(
            num_scalar_prefetch=1, grid=grid, in_specs=in_specs, out_specs=out_specs, scratch_shapes=list(scratch)
        ),
        out_shape=out_shape,
        compiler_params=pltpu.CompilerParams(vmem_limit_bytes=vmem << 20),
        cost_estimate=pl.CostEstimate(flops=int(us * COST), bytes_accessed=0, transcendentals=0),
        name=name,
    )(ids, *args)


def sin_cos(angle):
    turns = jnp.round(angle * (2.0 / math.pi))
    r = angle - turns * 1.5703125
    r = r - turns * 4.837512969970703125e-4
    r = r - turns * 7.54978995489188216e-8
    z = r * r
    s = ((-1.9515295891e-4 * z + 8.3321608736e-3) * z - 1.6666654611e-1) * z * r + r
    c = (
        (2.443315711809948e-5 * z - 1.388731625493765e-3) * z + 4.166664568298827e-2
    ) * z * z + (1.0 - 0.5 * z)
    q = turns.astype(jnp.int32)
    odd = (q & 1) == 1
    one, two = jnp.where(odd, c, s), jnp.where(odd, s, c)
    sine = jnp.where((q & 2) == 2, -one, one)
    cosine = jnp.where(((q + 1) & 2) == 2, -two, two)
    return sine, cosine


def rates(shape, dim):
    at = lax.broadcasted_iota(jnp.int32, shape, dim) & 63
    return jnp.exp(at.astype(F32) * (-math.log(10000.0) / 64))


def tables_kernel(ids, box_ref, kf_ref, tab_ref, tabt_ref, fkt_ref, fqt_ref):
    half = kf_ref.shape[0] // 2
    rate_row, rate_column = rates((8, 128), 1)[0:1, :], rates((64, 128), 0)[:, 0:1]
    box = box_ref[0].astype(F32)
    centre = (box[0:2, :] + box[2:4, :]) * 0.5
    turned = jnp.concatenate([centre[:, half:], centre[:, :half]], 1)
    centre = jnp.where(ids[1] == 0, centre, turned)
    column = jnp.concatenate([centre, jnp.zeros((6, 2 * half), F32)], 0).T
    front = lax.broadcasted_iota(jnp.int32, (2 * half, 128), 1) < 64
    for axis in range(2):
        s, c = sin_cos(column[:, axis : axis + 1] * rate_row)
        kf_ref[:, axis * 128 : axis * 128 + 128] = jnp.where(front, c, s).astype(BF16)
        tab_ref[axis] = c
        tab_ref[2 + axis] = jnp.where(front, s, -s)
        st, ct = sin_cos(rate_column * centre[axis : axis + 1, :])
        tabt_ref[2 * axis] = st
        tabt_ref[2 * axis + 1] = ct
        sl, cl = st.astype(BF16), ct.astype(BF16)
        at = 128 * axis
        fkt_ref[at : at + 64, :] = cl
        fkt_ref[at + 64 : at + 128, :] = sl
        fqt_ref[at : at + 64, :] = sl * 0.125
        fqt_ref[at + 64 : at + 128, :] = cl * 0.125


def tables(ids, boxes):
    rows = boxes.shape[2]
    shapes = [((rows, 256), BF16), ((4, rows, 128), F32), ((4, 64, rows), F32), ((256, rows), BF16), ((256, rows), BF16)]
    return call(
        tables_kernel, "tables", (1,), ids, (boxes,), [pl.BlockSpec((1, 4, rows), lambda i, ids: (ids[1], 0, 0))],
        [whole(s) for s, _ in shapes], [SDS(s, t) for s, t in shapes], us=3,
    )


def project_kernel(ids, own_ref, other_ref, w_ref, b_ref, pt_ref, p_ref, xt_ref, x, bias):
    step = pl.program_id(0)

    @pl.when(step == 0)
    def _():
        half = own_ref.shape[1]
        x[:half, :] = own_ref[0]
        x[half:, :] = other_ref[0]
        bias[...] = wide(b_ref)
        xt_ref[...] = x[...].T

    block = w_ref.shape[1]
    shift = bias[:, pl.ds(pl.multiple_of(step * block, 128), block)]
    p = (mm(x[...], w_ref[...]) + shift).astype(BF16)
    p_ref[...] = p
    pt_ref[...] = p.T


def page_specs(half, width):
    spec = pl.BlockSpec((1, half, width), lambda i, ids: (ids[1], 0, 0))
    return spec, spec


def project(ids, tokens, other, w, b):
    _, half, width = tokens.shape
    rows = 2 * half
    cols = w.shape[1]
    block = 768
    return call(
        project_kernel, "project", (cols // block,), ids, (tokens, other, w, b),
        [*page_specs(half, width), pl.BlockSpec((width, block), lambda i, ids: (0, i)), whole((cols,))],
        [
            pl.BlockSpec((block, rows), lambda i, ids: (i, 0)), pl.BlockSpec((rows, block), lambda i, ids: (0, i)),
            whole((width, rows)),
        ],
        [SDS((cols, rows), BF16), SDS((rows, cols), BF16), SDS((width, rows), BF16)],
        [pltpu.VMEM((rows, width), BF16), pltpu.VMEM((1, cols), F32)],
        us=5,
    )


def attend_kernel(ids, len_ref, qt_ref, vt_ref, k_ref, wk_ref, wq_ref, kf_ref, tab_ref, tabt_ref, fqt_ref,
                  e_ref, at_ref, r_ref, wkt_ref, wqt_ref, fk, fq):
    rows = k_ref.shape[0]
    wkt_ref[...] = wk_ref[...].T
    wqt_ref[...] = wq_ref[...].T
    heads = k_ref.shape[1] // 64

    @pl.when(pl.program_id(0) == 0)
    def _():
        lane = lax.broadcasted_iota(jnp.int32, (rows, 128), 1)
        at = lax.broadcasted_iota(jnp.int32, (rows, 128), 0)
        turned = jnp.where(at < rows // 2, at + rows // 2, at - rows // 2)
        at = jnp.where(ids[1] == 0, at, turned)
        mask = jnp.where((lane == 0) & (at >= len_ref[ids[1]]), -BIG, 0.0).astype(BF16)
        sub = lax.broadcasted_iota(jnp.int32, (128, rows), 0)
        for h in range(heads):
            fk[h, :, 0:256] = kf_ref[...]
            fk[h, :, 640:768] = mask
            fq[h, 256:512, :] = fqt_ref[...]
            fq[h, 640:768, :] = jnp.where(sub == 0, 1.0, 0.0).astype(BF16)

    lane = lax.broadcasted_iota(jnp.int32, (256, 128), 1)
    for h in range(heads):
        two = slice(h // 2 * 128, h // 2 * 128 + 128)
        fk[h, :, 512:640] = k_ref[:, two]
        mine = (lane < 64) if h % 2 == 0 else (lane >= 64)
        qt = qt_ref[h * 64 : h * 64 + 64, :]
        zero = jnp.zeros_like(qt)
        pad = jnp.concatenate([qt, zero] if h % 2 == 0 else [zero, qt], 0)
        fq[h, 512:640, :] = pad * 0.125
        a = mm(wk_ref[:, two], pad)
        sx, cx, sy, cy = (tabt_ref[i] * 0.125 for i in range(4))
        axs, axc, ays, ayc = (a[i * 64 : i * 64 + 64, :] for i in range(4))
        fq[h, 0:64, :] = (axs * sx + axc * cx).astype(BF16)
        fq[h, 64:128, :] = (axc * sx - axs * cx).astype(BF16)
        fq[h, 128:192, :] = (ays * sy + ayc * cy).astype(BF16)
        fq[h, 192:256, :] = (ayc * sy - ays * cy).astype(BF16)
        w = jnp.where(mine, wq_ref[:, two], 0).astype(BF16)
        b = mm_nt(k_ref[:, two], w)
        for axis in range(2):
            part = b[:, axis * 128 : axis * 128 + 128]
            turned = pltpu.roll(part, 64, 1)
            fk[h, :, 256 + axis * 128 : 384 + axis * 128] = (
                part * tab_ref[axis] + turned * tab_ref[2 + axis]
            ).astype(BF16)
    for h in range(heads):
        if h % 4 == 0:
            scores = [mm(fk[g], fq[g]) for g in range(h, h + 4)]
        s = scores[h % 4]
        e = jnp.exp(s - jnp.max(s, 0, keepdims=True))
        r = 1.0 / jnp.sum(e, 0, keepdims=True)
        low = e.astype(BF16)
        e_ref[h] = low
        at_ref[h * 64 : h * 64 + 64, :] = (mm(vt_ref[h * 64 : h * 64 + 64, :], low) * r).astype(BF16)
        r_ref[h // 2, h % 2 : h % 2 + 1, :] = r


def attend(ids, lengths, pt, p, w_posk, w_posq, kf, tab, tabt, fqt):
    rows = p.shape[0]
    width = pt.shape[0] // 3
    return call(
        attend_kernel, "attend", (PAIRS // 2,), ids, (lengths, pt, pt, p, w_posk, w_posq, kf, tab, tabt, fqt),
        [
            pl.BlockSpec(memory_space=pltpu.SMEM),
            pl.BlockSpec((256, rows), lambda i, ids: (i, 0)),
            pl.BlockSpec((256, rows), lambda i, ids: (2 * PAIRS // 2 + i, 0)),
            pl.BlockSpec((rows, 256), lambda i, ids: (0, PAIRS // 2 + i)),
            pl.BlockSpec((256, 256), lambda i, ids: (0, i)),
            pl.BlockSpec((256, 256), lambda i, ids: (0, i)),
            whole((rows, 256)), whole((4, rows, 128)), whole((4, 64, rows)), whole((256, rows)),
        ],
        [
            pl.BlockSpec((4, rows, rows), lambda i, ids: (i, 0, 0)),
            pl.BlockSpec((256, rows), lambda i, ids: (i, 0)),
            pl.BlockSpec((2, 2, rows), lambda i, ids: (i, 0, 0)),
            pl.BlockSpec((256, 256), lambda i, ids: (i, 0)),
            pl.BlockSpec((256, 256), lambda i, ids: (i, 0)),
        ],
        [
            HBM((HEADS, rows, rows), BF16), SDS((width, rows), BF16), SDS((PAIRS, 2, rows), F32),
            SDS((width, 256), BF16), SDS((width, 256), BF16),
        ],
        [pltpu.VMEM((4, rows, 768), BF16), pltpu.VMEM((4, 768, rows), BF16)],
        vmem=22, us=17,
    )


def feed_kernel(ids, at_ref, own_ref, other_ref, wo_ref, bo_ref, g1_ref, s1_ref, wi_ref, bi_ref, wd_ref, bd_ref,
                g2_ref, s2_ref, cown_ref, cother_ref,
                flt_ref, norm_ref, rstd_ref, slope_ref, actt_ref, keep_ref, give_ref, dres_ref, dsec_ref, send_ref,
                rows_ref, first, low, second, cot):
    step = pl.program_id(0)
    half = own_ref.shape[1]

    @pl.when(step == 0)
    def _():
        first[:half, :] = own_ref[0].astype(F32)
        first[half:, :] = other_ref[0].astype(F32)
        cot[:half, :] = cown_ref[0]
        cot[half:, :] = cother_ref[0]
        v = first[...] + (mm(at_ref[...].T, wo_ref[...]) + wide(bo_ref))
        c = v - jnp.mean(v, -1, keepdims=True)
        rstd = lax.rsqrt(jnp.mean(c * c, -1, keepdims=True) + 1e-6)
        normed = c * rstd
        norm_ref[...] = normed
        rstd_ref[...] = rstd
        f = normed * wide(g1_ref) + wide(s1_ref)
        first[...] = f + wide(bd_ref)
        l = f.astype(BF16)
        low[...] = l
        flt_ref[...] = l.T

    h = mm(low[...], wi_ref[...]) + wide(bi_ref)
    cdf = 0.5 * lax.erf(h * (0.5 ** 0.5)) + 0.5
    active = (h * cdf).astype(BF16)
    slope_ref[...] = (cdf + h * (jnp.exp(-0.5 * h * h) * ((2.0 * math.pi) ** -0.5))).astype(BF16)
    actt_ref[...] = active.T
    part = mm(active, wd_ref[...])

    @pl.when(step == 0)
    def _():
        second[...] = part

    @pl.when(step > 0)
    def _():
        second[...] += part

    @pl.when(step == pl.num_programs(0) - 1)
    def _():
        v = first[...] + second[...]
        c = v - jnp.mean(v, -1, keepdims=True)
        rstd = lax.rsqrt(jnp.mean(c * c, -1, keepdims=True) + 1e-6)
        normed = c * rstd
        out = (normed * wide(g2_ref) + wide(s2_ref)).astype(BF16)
        keep_ref[0] = out[:half, :]
        give_ref[...] = out[half:, :]
        g = cot[...].astype(F32)
        gg = g * wide(g2_ref)
        d = rstd * (
            gg - jnp.mean(gg, -1, keepdims=True) - normed * jnp.mean(gg * normed, -1, keepdims=True)
        )
        dres_ref[...] = d
        l = d.astype(BF16)
        dsec_ref[...] = l
        side = send_ref.shape[1]
        send_ref[...] = dsec_ref[:, pl.ds(pl.multiple_of((1 - ids[1]) * side, 128), side)]
        rows_ref[0:1, :] = jnp.sum(g * normed, 0, keepdims=True)
        rows_ref[1:2, :] = jnp.sum(g, 0, keepdims=True)
        rows_ref[2:3, :] = jnp.sum(l.astype(F32), 0, keepdims=True)
        rows_ref[3:8, :] = jnp.zeros((5, rows_ref.shape[1]), F32)


def vec(size):
    return pl.BlockSpec((size,), lambda i, ids: (0,))


def feed(ids, att, tokens, other, w_out, w_in, w_down, b_out, g1, s1, b_in, b_down, g2, s2, cot, cot_other):
    _, half, width = tokens.shape
    rows = 2 * half
    ff = w_in.shape[1]
    block = 1024
    mat = whole((rows, width))
    return call(
        feed_kernel, "feed", (ff // block,), ids,
        (att, tokens, other, w_out, b_out, g1, s1, w_in, b_in, w_down, b_down, g2, s2, cot, cot_other),
        [
            whole((width, rows)), *page_specs(half, width), whole((width, width)), vec(width), vec(width), vec(width),
            pl.BlockSpec((width, block), lambda i, ids: (0, i)),
            pl.BlockSpec((block,), lambda i, ids: (i,)),
            pl.BlockSpec((block, width), lambda i, ids: (i, 0)),
            vec(width), vec(width), vec(width), *page_specs(half, width),
        ],
        [
            whole((width, rows)), mat, whole((rows, 1)),
            pl.BlockSpec((rows, block), lambda i, ids: (0, i)),
            pl.BlockSpec((block, rows), lambda i, ids: (i, 0)),
            page_specs(half, width)[0], whole((half, width)), mat, mat, whole((rows, width // 2)), whole((8, width)),
        ],
        [
            SDS((width, rows), BF16), SDS((rows, width), F32), SDS((rows, 1), F32),
            SDS((rows, ff), BF16), SDS((ff, rows), BF16),
            SDS((2, half, width), BF16), SDS((half, width), BF16), SDS((rows, width), F32), SDS((rows, width), BF16),
            SDS((rows, width // 2), BF16), SDS((8, width), F32),
        ],
        [pltpu.VMEM((rows, width), F32), pltpu.VMEM((rows, width), BF16), pltpu.VMEM((rows, width), F32),
         pltpu.VMEM((rows, width), BF16)],
        vmem=24, us=15,
    )


def hidden_kernel(ids, ds_ref, wd_ref, slope_ref, send_ref, own_ref, rows_ref):
    step = pl.program_id(0)
    d = mm_nt(ds_ref[...], wd_ref[...]).astype(BF16).astype(F32)
    dh = (d * slope_ref[...].astype(F32)).astype(BF16)
    rows_ref[...] = jnp.sum(dh.astype(F32), 0, keepdims=True)
    sends = pl.num_programs(0) // 2

    @pl.when(step < sends)
    def _():
        send_ref[...] = dh

    @pl.when(step >= sends)
    def _():
        own_ref[...] = dh


def hidden_back(ids, dsec, w_down, slope):
    rows, width = dsec.shape
    ff = w_down.shape[0]
    block = 1536
    steps = ff // block
    s = steps // 2
    at = lambda i, ids: jnp.where(ids[1] == 0, (i + s) % steps, i)
    return call(
        hidden_kernel, "hidden_back", (steps,), ids, (dsec, w_down, slope),
        [
            whole((rows, width)),
            pl.BlockSpec((block, width), lambda i, ids: (at(i, ids), 0)),
            pl.BlockSpec((rows, block), lambda i, ids: (0, at(i, ids))),
        ],
        [
            pl.BlockSpec((rows, block), lambda i, ids: (0, jnp.minimum(i, s - 1))),
            pl.BlockSpec((rows, block), lambda i, ids: (0, jnp.maximum(i - s, 0))),
            pl.BlockSpec((1, block), lambda i, ids: (0, at(i, ids))),
        ],
        [SDS((rows, ff // 2), BF16), SDS((rows, ff // 2), BF16), SDS((1, ff), F32)],
        us=5,
    )


def first_kernel(ids, dsend_ref, down_ref, wsend_ref, wown_ref, dres_ref, norm_ref, rstd_ref, g1_ref, wo_ref,
                 res_ref, branch_ref, send_ref, datt_ref, rows_ref, acc):
    step = pl.program_id(0)
    part = mm_nt(beside(dsend_ref[...], down_ref[...]), beside(wsend_ref[...], wown_ref[...]))

    @pl.when(step == 0)
    def _():
        acc[...] = part

    @pl.when(step > 0)
    def _():
        acc[...] += part

    @pl.when(step == pl.num_programs(0) - 1)
    def _():
        g = dres_ref[...] + acc[...].astype(BF16).astype(F32)
        normed = norm_ref[...]
        gg = g * wide(g1_ref)
        d = rstd_ref[...] * (
            gg - jnp.mean(gg, -1, keepdims=True) - normed * jnp.mean(gg * normed, -1, keepdims=True)
        )
        res_ref[...] = d
        l = d.astype(BF16)
        branch_ref[...] = l
        side = send_ref.shape[1]
        send_ref[...] = branch_ref[:, pl.ds(pl.multiple_of((1 - ids[1]) * side, 128), side)]
        datt_ref[...] = mm_nt(wo_ref[...], l).astype(BF16)
        rows_ref[0:1, :] = jnp.sum(g * normed, 0, keepdims=True)
        rows_ref[1:2, :] = jnp.sum(g, 0, keepdims=True)
        rows_ref[2:3, :] = jnp.sum(l.astype(F32), 0, keepdims=True)
        rows_ref[3:8, :] = jnp.zeros((5, rows_ref.shape[1]), F32)


def first_back(ids, dsend, down, w_in, dres, norm, rstd, g1, w_out):
    rows, width = dres.shape
    ff = w_in.shape[1]
    block = 768
    s = ff // block // 2
    mat = whole((rows, width))
    return call(
        first_kernel, "first_back", (s,), ids, (dsend, down, w_in, w_in, dres, norm, rstd, g1, w_out),
        [
            pl.BlockSpec((rows, block), lambda i, ids: (0, i)),
            pl.BlockSpec((rows, block), lambda i, ids: (0, i)),
            pl.BlockSpec((width, block), lambda i, ids: (0, (1 - ids[1]) * s + i)),
            pl.BlockSpec((width, block), lambda i, ids: (0, ids[1] * s + i)),
            mat, mat, whole((rows, 1)), vec(width), whole((width, width)),
        ],
        [mat, mat, whole((rows, width // 2)), whole((width, rows)), whole((8, width))],
        [
            SDS((rows, width), F32), SDS((rows, width), BF16), SDS((rows, width // 2), BF16), SDS((width, rows), BF16),
            SDS((8, width), F32),
        ],
        [pltpu.VMEM((rows, width), F32)],
        us=8,
    )


def attend_back_kernel(ids, e_ref, r_ref, da_ref, at_ref, qt_ref, kt_ref, v_ref, wkt_ref, wqt_ref, fkt_ref, fqt_ref,
                       tabt_ref, dp_ref, gk_ref, gq_ref, rows_ref, left_k, left_q):
    heads = 2

    @pl.when(pl.program_id(0) == 0)
    def _():
        for h in range(heads):
            left_k[h, 64:320, :] = fkt_ref[...]
            left_q[h, 64:320, :] = fqt_ref[...]

    sx, cx, sy, cy = (tabt_ref[i] for i in range(4))
    lane = lax.broadcasted_iota(jnp.int32, (256, 128), 1)
    own = [slice(h * 64, h * 64 + 64) for h in range(heads)]
    das, deltas, dps = [], [], []
    for h in range(heads):
        left_k[h, 0:64, :] = kt_ref[own[h], :]
        left_q[h, 0:64, :] = qt_ref[own[h], :] * 0.125
        da = da_ref[own[h], :].astype(F32) * r_ref[0, h : h + 1, :]
        deltas.append(jnp.sum(da * at_ref[own[h], :].astype(F32), 0, keepdims=True))
        da = da.astype(BF16)
        das.append(da)
        zero = jnp.zeros_like(da)
        pad = jnp.concatenate([da, zero] if h == 0 else [zero, da], 0)
        dps.append(mm(v_ref[...], pad))
    dss = [(e_ref[h].astype(F32) * (dps[h] - deltas[h])).astype(BF16) for h in range(heads)]
    ones = [mm(left_k[h], dss[h]) * 0.125 for h in range(heads)]
    twos = [mm_nt(left_q[h], dss[h]) for h in range(heads)]
    gk, gq = [], []
    for h in range(heads):
        dp_ref[2, own[h], :] = mm_nt(das[h], e_ref[h]).astype(BF16)
    for h in range(heads):
        one, two = ones[h], twos[h]
        ux1, ux2, uy1, uy2 = (one[64 + i * 64 : 128 + i * 64, :].astype(BF16).astype(F32) for i in range(4))
        d_a = jnp.concatenate(
            [ux1 * sx - ux2 * cx, ux1 * cx + ux2 * sx, uy1 * sy - uy2 * cy, uy1 * cy + uy2 * sy], 0
        ).astype(BF16)
        zx1, zx2, zy1, zy2 = (two[64 + i * 64 : 128 + i * 64, :] for i in range(4))
        d_b = jnp.concatenate(
            [zx1 * cx - zx2 * sx, zx1 * sx + zx2 * cx, zy1 * cy - zy2 * sy, zy1 * sy + zy2 * cy], 0
        ).astype(BF16)
        dp_ref[0, own[h], :] = (one[0:64, :] + mm(wkt_ref[own[h], :], d_a)).astype(BF16)
        dp_ref[1, own[h], :] = (two[0:64, :] + mm(wqt_ref[own[h], :], d_b)).astype(BF16)
        gk.append(mm_nt(d_a, qt_ref[...]))
        gq.append(mm_nt(d_b, kt_ref[...]))
    gk_ref[...] = jnp.where(lane < 64, gk[0], gk[1]).astype(BF16)
    gq_ref[...] = jnp.where(lane < 64, gq[0], gq[1]).astype(BF16)
    unit = jnp.ones((8, dp_ref.shape[2]), BF16)
    for i in range(3):
        rows_ref[8 * i : 8 * i + 8, :] = mm_nt(unit, dp_ref[i])


def attend_back(ids, own, e, r, datt, att, pt, p, wkt, wqt, fkt, fqt, tabt):
    rows = p.shape[0]
    pairs = PAIRS // 2
    lo = lambda ids: (ids[1] if own else 1 - ids[1]) * pairs
    pair = lambda base: pl.BlockSpec((128, rows), lambda i, ids: (base + lo(ids) + i, 0))
    wt = pl.BlockSpec((128, 256), lambda i, ids: (lo(ids) + i, 0))
    return call(
        attend_back_kernel, "attend_back", (pairs,), ids, (e, r, datt, att, pt, pt, p, wkt, wqt, fkt, fqt, tabt),
        [
            pl.BlockSpec((2, rows, rows), lambda i, ids: (lo(ids) + i, 0, 0)),
            pl.BlockSpec((1, 2, rows), lambda i, ids: (lo(ids) + i, 0, 0)),
            pair(0), pair(0), pair(0), pair(PAIRS),
            pl.BlockSpec((rows, 128), lambda i, ids: (0, 2 * PAIRS + lo(ids) + i)),
            wt, wt, whole((256, rows)), whole((256, rows)), whole((4, 64, rows)),
        ],
        [
            pl.BlockSpec((3, 128, rows), lambda i, ids: (0, i, 0)),
            pl.BlockSpec((256, 128), lambda i, ids: (0, i)),
            pl.BlockSpec((256, 128), lambda i, ids: (0, i)),
            pl.BlockSpec((24, 128), lambda i, ids: (0, i)),
        ],
        [
            SDS((3, 128 * pairs, rows), BF16), SDS((256, 128 * pairs), BF16), SDS((256, 128 * pairs), BF16),
            SDS((24, 128 * pairs), F32),
        ],
        [pltpu.VMEM((2, 320, rows), BF16), pltpu.VMEM((2, 320, rows), BF16)],
        us=9,
    )


def tokens_kernel(ids, w_ref, ds_ref, do_ref, dres_ref, keep_ref, give_ref):
    width = w_ref.shape[1] // 3
    side = width // 2
    half = keep_ref.shape[1]
    left, right = [], []
    for h, ref in ((1 - ids[1], ds_ref), (ids[1], do_ref)):
        for s in range(3):
            left.append(w_ref[:, pl.ds(pl.multiple_of(s * width + h * side, 128), side)])
            right.append(ref[s])
    acc = mm(beside(*left), below(*right))
    out = (dres_ref[...] + acc.T).astype(BF16)
    keep_ref[0] = out[:half, :]
    give_ref[...] = out[half:, :]


def tokens_back(ids, w_qkv, dsend, down, dres):
    rows, width = dres.shape
    cols = w_qkv.shape[1]
    block = 256
    half = rows // 2
    blk = pl.BlockSpec((half, block), lambda i, ids: (0, i))
    return call(
        tokens_kernel, "tokens_back", (width // block,), ids, (w_qkv, dsend, down, dres),
        [
            pl.BlockSpec((block, cols), lambda i, ids: (i, 0)), whole(dsend.shape), whole(down.shape),
            pl.BlockSpec((rows, block), lambda i, ids: (0, i)),
        ],
        [pl.BlockSpec((1, half, block), lambda i, ids: (ids[1], 0, i)), blk],
        [SDS((2, half, width), BF16), SDS((half, width), BF16)],
        us=6,
    )


def chosen(core, pair):
    return jnp.where(core == 0, pair[0], pair[1])


def drop_bit(p, bit):
    return ((p >> (bit + 1)) << bit) | (p & ((1 << bit) - 1))


def put(ids, bits, p, lanes, value, send_ref, keep_ref):
    bit = chosen(ids[1], bits)
    here = ((p >> bit) & 1) == ((ids[0] >> bit) & 1)
    at = drop_bit(p, bit)

    @pl.when(here)
    def _():
        keep_ref[at, 0 : value.shape[0], lanes] = value

    @pl.when(jnp.logical_not(here))
    def _():
        send_ref[at, 0 : value.shape[0], lanes] = value


def down_kernel(n, bits, ids, a0_ref, a1_ref, b0_ref, b1_ref, send_ref, keep_ref):
    places = n // pl.num_programs(0)
    r, w = keep_ref.shape[1:]
    acc = mm(beside(a0_ref[...], a1_ref[...]), below(b0_ref[...], b1_ref[...]))
    for k in range(places):
        p = pl.program_id(0) * places + k
        put(ids, bits, p, slice(0, w), acc[k * r : k * r + r, :].astype(BF16), send_ref, keep_ref)


def down_grad(ids, n, bits, actt, actt_other, dsec, dsec_other):
    ff, rows = actt.shape
    side = dsec_other.shape[1]
    block = ff // 2
    part = (n // 2, ff // n, side)
    a = pl.BlockSpec((block, rows), lambda i, ids: (i, 0))
    return call(
        functools.partial(down_kernel, n, bits), "down_grad", (2,), ids, (actt, actt_other, dsec, dsec_other),
        [a, a, pl.BlockSpec((rows, side), lambda i, ids: (0, ids[1])), whole((rows, side))],
        [whole(part)] * 2, [SDS(part, BF16)] * 2,
        us=7,
    )


def mid_kernel(n, bits, ids, f0_ref, f1_ref, h0_ref, h1_ref, a0_ref, a1_ref, c0_ref, c1_ref, send_ref, keep_ref):
    step = pl.program_id(0)
    last = pl.num_programs(0) - 1
    r = keep_ref.shape[1]
    w = h0_ref.shape[1]

    @pl.when(step < last)
    def _():
        acc = mm(beside(f0_ref[...], f1_ref[...]), below(h0_ref[...], h1_ref[...]))
        lanes = pl.ds(pl.multiple_of(step * w, 128), w)
        for p in range(n):
            put(ids, bits, p, lanes, acc[p * r : p * r + r, :].astype(BF16), send_ref, keep_ref)

    @pl.when(step == last)
    def _():
        acc = mm(beside(a0_ref[...], a1_ref[...]), below(c0_ref[...], c1_ref[...]))
        lanes = slice(keep_ref.shape[2] - acc.shape[1], keep_ref.shape[2])
        for p in range(n):
            put(ids, bits, p, lanes, acc[p * r : p * r + r, :].astype(BF16), send_ref, keep_ref)


def mid_grad(ids, n, bits, flt, flt_other, dh, dh_other, att, att_other, branch, branch_other):
    width, rows = flt.shape
    ffs = dh.shape[1]
    side = branch_other.shape[1]
    block = 768
    steps = ffs // block
    part = (n // 2, width // n, ffs + side)
    b = pl.BlockSpec((rows, block), lambda i, ids: (0, jnp.minimum(i, steps - 1)))
    a = whole((width, rows))
    return call(
        functools.partial(mid_kernel, n, bits), "mid_grad", (steps + 1,), ids,
        (flt, flt_other, dh, dh_other, att, att_other, branch, branch_other),
        [a, a, b, b, a, a, pl.BlockSpec((rows, side), lambda i, ids: (0, ids[1])), whole((rows, side))],
        [whole(part)] * 2, [SDS(part, BF16)] * 2, us=6,
    )


def chunks(n, size):
    return max(((p + 1) * size - 1) // 128 - p * size // 128 + 1 for p in range(n))


def small_plan(n, sizes):
    plan, at = [], 0
    for size in sizes:
        plan.append((size, chunks(n, size), at))
        at += chunks(n, size)
    return plan, at


def qk_kernel(n, bits, sizes, ids, x0_ref, x1_ref, d0_ref, d1_ref, two_ref, one_ref, in_ref, rs_ref, ro_ref,
              send_ref, keep_ref, qkv_ref):
    r = keep_ref.shape[1]
    side = d0_ref.shape[1]
    for who, ref in ((1 - ids[1], rs_ref), (ids[1], ro_ref)):
        for i in range(3):
            at = pl.multiple_of(who * side, 128)
            qkv_ref[i : i + 1, pl.ds(at, side)] = ref[8 * i : 8 * i + 1, :]
    acc = mm_nt(beside(x0_ref[...], x1_ref[...]), below(beside(d0_ref[0], d1_ref[0]), beside(d0_ref[1], d1_ref[1])))
    for p in range(n):
        put(ids, bits, p, slice(0, 2 * side), acc[p * r : p * r + r, :].astype(BF16), send_ref, keep_ref)
    vectors = (qkv_ref, one_ref, one_ref, one_ref, in_ref, two_ref, two_ref, two_ref)
    index = (None, 2, 0, 1, 0, 2, 0, 1)
    plan, _ = small_plan(n, sizes)
    for p in range(n):
        found = []
        for (size, count, _), ref, row in zip(plan, vectors, index):
            for c in range(count):
                at = min(p * size // 128 + c, n * size // 128 - 1)
                if row is None:
                    i, at = at * 128 // ref.shape[1], at * 128 % ref.shape[1]
                    found.append(ref[i : i + 1, at : at + 128])
                else:
                    found.append(ref[row : row + 1, at * 128 : at * 128 + 128])
        found = jnp.concatenate(found + [jnp.zeros((r - len(found), 128), F32)], 0).astype(BF16)
        put(ids, bits, p, slice(2 * side, 2 * side + 128), found, send_ref, keep_ref)


def qk_grad(ids, n, bits, sizes, xt, xt_other, dp, dp_other, two, one, into, rows_send, rows_own):
    width, rows = xt.shape
    side = dp.shape[1]
    part = (n // 2, width // n, 2 * side + 128)
    d = pl.BlockSpec((2, side, rows), lambda i, ids: (0, 0, 0))
    return call(
        functools.partial(qk_kernel, n, bits, sizes), "qk_grad", (1,), ids,
        (xt, xt_other, dp, dp_other, two, one, into, rows_send, rows_own),
        [whole(xt.shape)] * 2 + [d, d] + [whole(a.shape) for a in (two, one, into, rows_send, rows_own)],
        [whole(part)] * 2, [SDS(part, BF16)] * 2, [pltpu.VMEM((8, width), F32)],
        us=4,
    )


def vp_kernel(n, bits, ids, x0_ref, x1_ref, d0_ref, d1_ref, k0_ref, k1_ref, q0_ref, q1_ref, send_ref, keep_ref):
    r = keep_ref.shape[1]
    side = d0_ref.shape[1]
    acc = mm_nt(beside(x0_ref[...], x1_ref[...]), beside(d0_ref[0], d1_ref[0]))
    for p in range(n):
        put(ids, bits, p, slice(0, side), acc[p * r : p * r + r, :].astype(BF16), send_ref, keep_ref)
    base = side
    for own_ref, other_ref in ((k0_ref, k1_ref), (q0_ref, q1_ref)):
        acc = (own_ref[...].astype(F32) + other_ref[...].astype(F32)).astype(BF16)
        s = acc.shape[0] // n
        for p in range(n):
            rows = acc[p * s : p * s + s, :]
            stacked = jnp.concatenate([rows[:, 128 * i : 128 * i + 128] for i in range(side // 128)], 0)
            put(ids, bits, p, slice(base, base + 128), stacked, send_ref, keep_ref)
        base += 128


def vp_grad(ids, n, bits, xt, xt_other, dp, dp_other, gk, gk_other, gq, gq_other):
    width, rows = xt.shape
    side = dp.shape[1]
    part = (n // 2, width // n, side + 256)
    d = pl.BlockSpec((1, side, rows), lambda i, ids: (2, 0, 0))
    return call(
        functools.partial(vp_kernel, n, bits), "vp_grad", (1,), ids,
        (xt, xt_other, dp, dp_other, gk, gk_other, gq, gq_other),
        [whole(xt.shape)] * 2 + [d, d] + [whole(a.shape) for a in (gk, gk, gq, gq)],
        [whole(part)] * 2, [SDS(part, BF16)] * 2, us=3,
    )


def add_split_kernel(bits, lows, ids, keep_ref, got_ref, send_ref, next_ref):
    low = chosen(ids[1], lows)
    mine = (ids[0] >> chosen(ids[1], bits)) & 1

    @pl.loop(0, next_ref.shape[0])
    def _(q):
        base = ((q >> low) << (low + 1)) | (q & ((1 << low) - 1))
        for which, ref in ((1 - mine, send_ref), (mine, next_ref)):
            p = base + (which << low)
            ref[q] = (keep_ref[p].astype(F32) + got_ref[p].astype(F32)).astype(BF16)


def add_split(ids, keep, got, bits, lows):
    m, r, w = keep.shape
    part = (m // 2, r, w)
    return call(
        functools.partial(add_split_kernel, bits, lows), "add_split", (1,), ids, (keep, got),
        [whole(keep.shape)] * 2, [whole(part)] * 2, [SDS(part, BF16)] * 2, vmem=24, us=1,
    )


def add_last_kernel(ids, keep_ref, got_ref, out_ref):
    out_ref[...] = (keep_ref[0].astype(F32) + got_ref[0].astype(F32)).astype(BF16)


def add_last(ids, keep, got):
    _, r, w = keep.shape
    return call(
        add_last_kernel, "add_last", (1,), ids, (keep, got), [whole(keep.shape)] * 2, whole((r, w)), SDS((r, w), BF16),
        vmem=16, us=1,
    )


def swap(x):
    return lax.ppermute(x, "slab", [(0, 1), (1, 0)])


def across(x, n, bits):
    pairs = [(2 * p + c, 2 * (p ^ (1 << bits[c])) + c) for p in range(n) for c in range(2)]
    return lax.ppermute(x, ("pages", "slab"), pairs)


def orders(n):
    low = list(range(n.bit_length() - 1))
    if len(low) != 4:
        pair = (low, low[1::-1] + low[:1:-1])
        return pair, pair, pair, pair
    return ORDERS


ORDERS = (
    ((0, 2, 1, 3), (1, 2, 0, 3)),
    ((0, 1, 2, 3), (1, 0, 3, 2)),
    ((0, 1, 2, 3), (1, 0, 3, 2)),
    ((0, 1, 2, 3), (1, 0, 3, 2)),
)


class Chain:
    def __init__(self, ids):
        self.ids = ids

    def run(self, kernel, *args, **kwargs):
        out = kernel(self.ids, *args, **kwargs)
        self.ids = after(self.ids, out[0] if isinstance(out, (list, tuple)) else out)
        return out


class Exchange:
    def __init__(self, chain, n, send, keep, order):
        self.chain, self.n, self.order = chain, n, order
        self.left = [sorted(o) for o in order]
        self.at = 0
        self.steps = len(order[0])
        self.send, self.keep = send, keep

    @staticmethod
    def first(order):
        return tuple(o[0] for o in order)

    def bits(self, step):
        return tuple(o[step] for o in self.order)

    def start(self):
        self.got = across(self.send, self.n, self.bits(self.at))

    def step(self):
        for l, b in zip(self.left, self.bits(self.at)):
            l.remove(b)
        self.at += 1
        if self.at == self.steps:
            self.mine = self.chain.run(add_last, self.keep, self.got)
            self.other = swap(self.mine)
            return
        bits = self.bits(self.at)
        lows = tuple(l.index(b) for l, b in zip(self.left, bits))
        self.send, self.keep = self.chain.run(add_split, self.keep, self.got, bits, lows)
        self.start()


def join_kernel(ids, mine_ref, other_ref, *outs):
    core = ids[1]
    at = 0
    for out in outs:
        side = out.shape[1] // 2
        for who, ref in ((core, mine_ref), (1 - core, other_ref)):
            out[:, pl.ds(pl.multiple_of(who * side, 128), side)] = ref[:, at : at + side].astype(F32)
        at += side


def join(ids, mine, other, widths):
    r = mine.shape[0]
    return call(
        join_kernel, "join", (1,), ids, (mine, other), [whole(mine.shape)] * 2,
        [whole((r, w)) for w in widths], [SDS((r, w), F32) for w in widths], vmem=16, us=2,
    )


def join_last_kernel(n, sizes, ids, qk_mine, qk_other, vo_mine, vo_other, qkv_ref, posk_ref, posq_ref, *vectors):
    core = ids[1]
    r, width = qkv_ref.shape[0], qkv_ref.shape[1] // 3
    side = width // 2
    s = posk_ref.shape[0]

    def lay(out, base, who, ref, at):
        out[:, pl.ds(pl.multiple_of(base + who * side, 128), side)] = ref[:, at : at + side].astype(F32)

    for who, qk, vo in ((core, qk_mine, vo_mine), (1 - core, qk_other, vo_other)):
        lay(qkv_ref, 0, who, qk, 0)
        lay(qkv_ref, width, who, qk, side)
        lay(qkv_ref, 2 * width, who, vo, 0)
        for j, out in enumerate((posk_ref, posq_ref)):
            lanes = slice(side + 128 * j, side + 128 * j + 128)
            for i in range(r // s):
                at = pl.multiple_of(who * side + 128 * i, 128)
                out[:, pl.ds(at, 128)] = vo[i * s : i * s + s, lanes].astype(F32)
    small = qk_mine[:, 2 * side :].astype(F32) + qk_other[:, 2 * side :].astype(F32)
    plan, _ = small_plan(n, sizes)
    for (size, count, at), out in zip(plan, vectors):
        line = jnp.concatenate([small[at + c : at + c + 1, :] for c in range(count)], 1)
        line = jnp.broadcast_to(line, (8, 128 * count))
        start = lax.rem(ids[0] * size, 128)
        out[...] = pltpu.roll(line, lax.rem(128 * count - start, 128 * count), 1)[0, :size]


def join_last(ids, n, sizes, qk, vo, width, pos):
    r = qk.mine.shape[0]
    shapes = [(r, 3 * width), (pos, width), (pos, width)] + [(s,) for s in sizes]
    return call(
        functools.partial(join_last_kernel, n, sizes), "join_last", (1,), ids, (qk.mine, qk.other, vo.mine, vo.other),
        [whole(qk.mine.shape)] * 2 + [whole(vo.mine.shape)] * 2,
        [whole(s) for s in shapes], [SDS(s, F32) for s in shapes], vmem=16, us=2,
    )


def plain_sum(g, n, place):
    left = list(range(n.bit_length() - 2, -1, -1))
    acc = g.astype(BF16).reshape((2,) * len(left) + (g.shape[0] // n, g.shape[1]))
    for bit in sorted(left):
        axis = left.index(bit)
        mine = (place >> bit) & 1
        send = lax.dynamic_index_in_dim(acc, 1 - mine, axis, keepdims=False)
        keep = lax.dynamic_index_in_dim(acc, mine, axis, keepdims=False)
        acc = (keep.astype(F32) + across(send, n, (bit, bit)).astype(F32)).astype(BF16)
        left.remove(bit)
    return acc


def plain_join(core, g):
    got = swap(g)
    sides = jnp.where(core == 0, jnp.stack([g, got], 1), jnp.stack([got, g], 1))
    return sides.reshape(g.shape[0], -1).astype(F32)


def pages(core, keep, got):
    return lax.dynamic_update_slice_in_dim(keep, got[None], 1 - core, 0)


def after(value, *others):
    return lax.optimization_barrier((value, *others))[0]


def body(n, tokens, boxes, lengths, w_qkv, b_qkv, w_posk, w_posq, w_out, b_out, gain_one, shift_one,
         w_in, b_in, w_down, b_down, gain_two, shift_two, cotangent):
    place = lax.axis_index("pages").astype(jnp.int32)
    core = lax.axis_index("slab").astype(jnp.int32)
    ids = jnp.stack([place, core])
    width = tokens.shape[2]
    other = swap(tokens)
    cot_other = swap(cotangent)

    kf, tab, tabt, fkt, fqt = tables(ids, boxes)
    pt, p, xt = project(after(ids, kf), tokens, other, w_qkv, b_qkv)
    e, att, r, wkt, wqt = attend(ids, lengths, pt, p, w_posk, w_posq, kf, tab, tabt, fqt)
    (flt, norm, rstd, slope, actt, out_keep, out_give, dres_two, dsec, dsec_send, rows_two) = feed(
        ids, att, tokens, other, w_out, w_in, w_down, b_out, gain_one, shift_one, b_in, b_down, gain_two, shift_two,
        cotangent, cot_other
    )
    xt_other, att_other, flt_other, actt_other = swap(xt), swap(att), swap(flt), swap(actt)
    dsec_other = swap(dsec_send)
    out_got = swap(out_give)
    dh_send, dh, row_in = hidden_back(ids, dsec, w_down, slope)
    dh_other = swap(dh_send)
    if width // n % 16:
        dres_one, branch, branch_send, datt, rows_one = first_back(
            ids, dh_send, dh, w_in, dres_two, norm, rstd, gain_one, w_out
        )
        args = dict(e=e, r=r, datt=datt, att=att, pt=pt, p=p, wkt=wkt, wqt=wqt, fkt=fkt, fqt=fqt, tabt=tabt)
        dp_send, gk_send, gq_send, bias_send = attend_back(ids, own=False, **args)
        dp, gk, gq, bias_own = attend_back(ids, own=True, **args)
        tok_keep, tok_give = tokens_back(ids, w_qkv, dp_send, dp, dres_one)
        first, second = jnp.where(core == 0, bias_own, bias_send), jnp.where(core == 0, bias_send, bias_own)
        rows_qkv = jnp.concatenate([first[::8], second[::8]], 1)
        dp_other = swap(dp_send)

        def side_of(a):
            size = a.shape[1] // 2
            return lax.dynamic_slice_in_dim(a, core * size, size, 1)

        def total(g):
            return plain_join(core, plain_sum(g, n, place))

        both = lambda op, a, b, c, d: op(a, b) + op(c, d)
        g_down = total(both(mm, actt, side_of(dsec), actt_other, dsec_other))
        g_in = total(both(mm, flt, dh, flt_other, dh_other))
        g_out = total(both(mm, att, side_of(branch), att_other, swap(branch_send)))
        g_posk = total(gk.astype(F32) + swap(gk_send).astype(F32))
        g_posq = total(gq.astype(F32) + swap(gq_send).astype(F32))
        g_qkv = jnp.concatenate([total(both(mm_nt, xt, dp[i], xt_other, dp_other[i])) for i in range(3)], 1)
        small = (rows_qkv, rows_one[2], rows_one[0], rows_one[1], row_in, rows_two[2], rows_two[0], rows_two[1])
        packed = lax.psum(jnp.concatenate([v.reshape(n, -1) for v in small], 1), ("pages", "slab"))
        packed = lax.dynamic_index_in_dim(packed, place, 0, keepdims=False)
        totals, at = [], 0
        for v in small:
            totals.append(packed[at : at + v.size // n])
            at += v.size // n
        return (pages(core, out_keep, out_got), pages(core, tok_keep, swap(tok_give)), g_qkv, totals[0], g_posk,
                g_posq, g_out, totals[1], totals[2], totals[3], g_in, totals[4], g_down, totals[5], totals[6],
                totals[7])

    order_down, order_mid, order_qk, order_vp = orders(n)
    first = Exchange.first
    chain = Chain(after(ids, dh))
    down = Exchange(
        chain, n, *chain.run(down_grad, n, first(order_down), actt, actt_other, dsec, dsec_other), order_down
    )
    down.start()
    dres_one, branch, branch_send, datt, rows_one = chain.run(
        first_back, dh_send, dh, w_in, dres_two, norm, rstd, gain_one, w_out
    )
    branch_other = swap(branch_send)
    mid = Exchange(
        chain, n,
        *chain.run(mid_grad, n, first(order_mid), flt, flt_other, dh, dh_other, att, att_other, branch, branch_other),
        order_mid,
    )
    down.step()
    mid.send = after(mid.send, down.send)
    mid.start()
    back = functools.partial(
        chain.run, attend_back, e=e, r=r, datt=datt, att=att, pt=pt, p=p, wkt=wkt, wqt=wqt, fkt=fkt, fqt=fqt, tabt=tabt
    )
    dp_send, gk_send, gq_send, bias_send = back(own=False)
    dp_other, gk_other, gq_other = swap(dp_send), swap(gk_send), swap(gq_send)
    down.step()
    dp, gk, gq, bias_own = back(own=True)
    small = (3 * width, width, width, width, w_in.shape[1], width, width, width)
    sizes = tuple(s // n for s in small)
    mid.step()
    down.step()
    qk = Exchange(
        chain, n, *chain.run(qk_grad, n, first(order_qk), sizes, xt, xt_other, dp, dp_other,
                             rows_two, rows_one, row_in, bias_send, bias_own), order_qk
    )
    qk.start()
    vp = Exchange(
        chain, n, *chain.run(vp_grad, n, first(order_vp), xt, xt_other, dp, dp_other,
                             gk, gk_other, gq, gq_other), order_vp
    )
    vp.start()
    down.step()
    mid.step()
    tok, tok_give = chain.run(tokens_back, w_qkv, dp_send, dp, dres_one)
    tok_got = swap(tok_give)
    qk.step()
    vp.step()
    mid.step()
    (g_down,) = chain.run(join, down.mine, down.other, (width,))
    qk.step()
    vp.step()
    mid.step()
    qk.step()
    vp.step()
    g_in, g_out = chain.run(join, mid.mine, mid.other, (w_in.shape[1], width))
    qk.step()
    vp.step()
    g_qkv, g_posk, g_posq, *totals = join_last(ids, n, sizes, qk, vp, width, w_posk.shape[0] // n)
    return (pages(core, out_keep, out_got), pages(core, tok, tok_got), g_qkv, totals[0], g_posk, g_posq, g_out,
            totals[1], totals[2], totals[3], g_in, totals[4], g_down, totals[5], totals[6], totals[7])


def solution(mesh):
    n = mesh.shape["pages"]
    rows, mat, flat = P("pages", "slab", None), P("pages", None), P("pages")
    return jax.shard_map(
        functools.partial(body, n),
        mesh=mesh,
        in_specs=(rows, P("pages", None, None), flat) + (P(),) * 14 + (rows,),
        out_specs=(rows, rows, mat, flat, mat, mat, mat, flat, flat, flat, mat, flat, mat, flat, flat, flat),
        check_vma=False,
    )
```
